128 devices in a mesh: group: 2 (over core), member: 64 (over x, y, z).
Axes of the slice: x: 4, y: 4, z: 4, core: 2. Of those that a mesh axis runs over, the one named last changes fastest.
Arguments:
- events: bfloat16 [65536, 512], P(('group', 'member')), may hold values from -6 to 6
- route: int32 [4096], P(('group', 'member')), may hold values from 0 to 2047, as said below
- block_offset: int32 [512], P(('group', 'member')), may hold values from 0 to 1, as said below
- hist_length: int32 [512], P(('group', 'member')), may hold values from 64 to 256, as said below
- cotangent: bfloat16 [65536, 512], P(('group', 'member')), may hold values from -6 to 6
- w_in: bfloat16 [512, 2048], replicated, may hold values from -0.25 to 0.25
- w_out: bfloat16 [512, 512], replicated, may hold values from -0.25 to 0.25
- rab: float32 [4, 12], replicated, may hold values from -4 to 4
Outputs:
- outputs: bfloat16 [65536, 512], P(('group', 'member'))
- events_grad: bfloat16 [65536, 512], P(('group', 'member'))
- w_in_grad: float32 [512, 2048], replicated
- w_out_grad: float32 [512, 512], replicated
The draws below stay inside these ranges and needn't reach their ends.
Inputs may be any that keep to these rules, and one draw needn't show every extreme that they name: Within each group, route is a permutation of the group's piece places; place t lies on member t // 32 at piece t % 32. A device sends either no piece or exactly 1 pieces to each device of its group. Every device of the balanced layout holds whole histories in consecutive blocks, block_offset counting 0, 1, 2, ... within each: one history of 2 blocks and two of one block, in any order. `hist_length`: all blocks of a history carry its length; a history of n blocks has 128 * (n - 1) + 1 to 128 * n events, one of one block 64 or more.
All inputs are finite; a program needn't handle non-finite values.
Results may differ from the reference program's by a relative error of at most 0.01.
Values may be sent and summed in bfloat16 or wider, within the bound.
No kernel may reach another device: no remote copies, remote signals or barrier semaphores. Data moves between devices by JAX's collectives and lax.ppermute only.
A program may use at most 128 MiB of HBM per device.

```python
import math
import jax
import jax.numpy as jnp
from jax import lax

D = 512
HEADS = 4
BUCKETS = 12
BLOCK = 128
PIECE = 16
BLK_DEV = 4
PIECES_DEV = 32
CAP = 1
MAX_LEN = 256
ROWS = 65536
N_GROUP = 2
N_MEMBER = 64


def template_blocks():
    extents = []
    extent = BLK_DEV // 2
    while extent >= 1:
        extents.append(extent)
        extent = extent // 2
    extents.append(1)
    return jnp.array(extents, dtype=jnp.int32)


def history_layout(key):
    extents = template_blocks()
    history_count = extents.shape[0]
    devices = N_GROUP * N_MEMBER
    slot_ids = jnp.arange(BLK_DEV, dtype=jnp.int32)

    def one_device(device_key):
        order_key, length_key = jax.random.split(device_key)
        chosen = extents[jax.random.permutation(order_key, history_count)]
        starts = (jnp.cumsum(chosen) - chosen).astype(jnp.int32)
        lowest = jnp.maximum(BLOCK // 2, BLOCK * (chosen - 1) + 1)
        lengths = jax.random.randint(length_key, (history_count,), lowest, BLOCK * chosen + 1)
        owners = jnp.sum((starts[None, :] <= slot_ids[:, None]).astype(jnp.int32), axis=1) - 1
        offsets = slot_ids - starts[owners]
        return (offsets.astype(jnp.int32), lengths[owners].astype(jnp.int32), chosen[owners])
    offsets, lengths, blocks_of = jax.vmap(one_device)(jax.random.split(key, devices))
    leading = (jnp.arange(devices, dtype=jnp.int32) % N_MEMBER == 0)[:, None]
    lengths = jnp.where(leading & (blocks_of == BLK_DEV // 2), MAX_LEN, lengths)
    return (offsets.reshape(-1).astype(jnp.int32), lengths.reshape(-1).astype(jnp.int32))


def draw_block_offset(key, part):
    offsets, lengths = history_layout(key)
    return offsets


def draw_hist_length(key, part):
    offsets, lengths = history_layout(key)
    return lengths


def draw_route(key, part):
    key = jax.random.fold_in(key, 7)
    total = N_MEMBER * PIECES_DEV
    spread = PIECES_DEV // CAP
    senders = jnp.arange(N_MEMBER, dtype=jnp.int32)[:, None]
    piece_ids = jnp.arange(PIECES_DEV, dtype=jnp.int32)[None, :]
    shift_ids = jnp.arange(N_MEMBER, dtype=jnp.int32)
    special = (shift_ids == N_MEMBER // 2) | (shift_ids == 1) | (shift_ids == N_MEMBER - 1)

    def one_order(order_sub):
        return jax.random.permutation(order_sub, PIECES_DEV).astype(jnp.int32)

    def one_group(group_key):
        pick_key, shuffle_key, order_key = jax.random.split(group_key, 3)
        ranks = jax.random.permutation(pick_key, N_MEMBER).astype(jnp.int32)
        priority = jnp.where(special, shift_ids - N_MEMBER, ranks).astype(jnp.int32)
        chosen = jnp.argsort(priority, stable=True)[:spread].astype(jnp.int32)
        shifts = jax.random.permutation(shuffle_key, jnp.repeat(chosen, CAP)).astype(jnp.int32)
        orders = jax.vmap(one_order)(jax.random.split(order_key, N_MEMBER))
        targets = (senders - shifts[None, :]) % N_MEMBER * PIECES_DEV + piece_ids
        sources = senders * PIECES_DEV + orders
        return jnp.zeros((total,), jnp.int32).at[sources.reshape(-1)].set(targets.reshape(-1).astype(jnp.int32))
    return jax.vmap(one_group)(jax.random.split(key, N_GROUP)).reshape(-1)


def level_of(own_key, shape, cuts, smallest, high):
    level, own = 1.0, jax.random.fold_in(own_key, 6)
    for axis_at, blocks in cuts:
        draws = jnp.exp(jax.random.uniform(jax.random.fold_in(own, axis_at), (blocks,), jnp.float32, smallest / len(cuts), high / len(cuts)))
        level = level * jnp.repeat(draws, shape[axis_at] // blocks).reshape([-1 if axis == axis_at else 1 for axis in range(len(shape))])
    return level


def scatter_about(rng, dims, scale, most, cuts=(), kind=jnp.bfloat16):
    values = scale * jax.random.normal(rng, dims, jnp.float32)
    if cuts:
        values = values * level_of(rng, dims, cuts, -0.22, 0.18)
    return jnp.clip(values, -most, most).astype(kind)


def setup_inputs(seed: int = 0) -> dict:
    arg_keys = jax.random.split(jax.random.key(seed), 9)
    events = scatter_about(arg_keys[0], (ROWS, D), 1.0, 6.0, ((0, 128),))
    route = draw_route(jax.random.fold_in(arg_keys[8], 71), 0)
    block_offset = draw_block_offset(jax.random.fold_in(arg_keys[8], 71), 0)
    hist_length = draw_hist_length(jax.random.fold_in(arg_keys[8], 71), 0)
    cotangent = scatter_about(arg_keys[4], (ROWS, D), 1.0, 6.0, ((0, 128),))
    w_in = scatter_about(arg_keys[5], (D, 4 * D), D ** -0.5, 0.25)
    w_out = scatter_about(arg_keys[6], (D, D), D ** -0.5, 0.25)
    rab = scatter_about(arg_keys[7], (HEADS, BUCKETS), 1.0, 4.0, (), jnp.float32)
    return {"events": events, "route": route, "block_offset": block_offset, "hist_length": hist_length, "cotangent": cotangent, "w_in": w_in, "w_out": w_out, "rab": rab}


EPS = 1e-05

def normalize(vector):
    average = lax.optimization_barrier(jnp.mean(vector, axis=-1, keepdims=True))
    centered = vector - average
    variance = lax.optimization_barrier(jnp.mean(centered * centered, axis=-1, keepdims=True))
    return centered * lax.rsqrt(variance + EPS)

def silu_slope(inputs):
    sigmoid = jax.nn.sigmoid(inputs)
    return sigmoid * (1.0 + inputs * (1.0 - sigmoid))

def lookup(entries, indices):
    matches = indices[:, None] == jnp.arange(entries.shape[0], dtype=jnp.int32)[None, :]
    return lax.optimization_barrier(jnp.sum(jnp.where(matches, entries[None, :], 0), axis=1)).astype(jnp.int32)

def template_extents(block_count):
    extents = []
    extent = block_count // 2
    while extent >= 1:
        extents.append(extent)
        extent = extent // 2
    extents.append(1)
    return extents

def listed_pairs(offsets):
    block_count = offsets.shape[0]
    tile_count = sum((extent * (extent + 1) // 2 for extent in template_extents(block_count)))
    padded = -(-tile_count // 16) * 16
    spans = offsets + 1
    starts = (jnp.cumsum(spans) - spans).astype(jnp.int32)
    places = jnp.arange(padded, dtype=jnp.int32)
    owners = lax.optimization_barrier(jnp.sum((starts[None, :] <= places[:, None]).astype(jnp.int32), axis=1)).astype(jnp.int32) - 1
    steps_back = places - lookup(starts, owners)
    in_use = places < tile_count
    query_at = jnp.where(in_use, owners, 0).astype(jnp.int32)
    key_at = jnp.where(in_use, owners - steps_back, 0).astype(jnp.int32)
    return (query_at, key_at, in_use)

def tile_terms(offsets, lengths, rab, query_at, key_at, in_use, block_rows):
    row_ids = jnp.arange(block_rows, dtype=jnp.int32)
    query_pos = lookup(offsets, query_at)[:, None] * block_rows + row_ids[None, :]
    key_pos = lookup(offsets, key_at)[:, None] * block_rows + row_ids[None, :]
    limits = lookup(lengths, query_at)
    distance = query_pos[:, :, None] - key_pos[:, None, :]
    allowed = (distance >= 0) & (query_pos[:, :, None] < limits[:, None, None]) & in_use[:, None, None]
    rel_bias = jnp.zeros((query_at.shape[0], rab.shape[0], block_rows, block_rows), jnp.float32) + rab[:, 0][None, :, None, None]
    for bucket in range(1, rab.shape[1]):
        stride = rab[:, bucket] - rab[:, bucket - 1]
        reached = (distance >= 2 ** (bucket - 1)).astype(jnp.float32)
        rel_bias = rel_bias + stride[None, :, None, None] * reached[:, None, :, :]
    return (allowed[:, None, :, :], rel_bias)

def attend(queries, keys, values, offsets, lengths, rab, pairs):
    block_count, block_rows, features = queries.shape
    head_count = rab.shape[0]
    head_depth = features // head_count
    scaling = 1.0 / math.sqrt(head_depth)
    batched = tuple((member.reshape(-1, 16) for member in pairs))

    def advance(totals, element):
        query_at, key_at, in_use = element
        query_tile = queries[query_at].reshape(16, block_rows, head_count, head_depth).astype(jnp.float32)
        key_tile = keys[key_at].reshape(16, block_rows, head_count, head_depth).astype(jnp.float32)
        value_tile = values[key_at].reshape(16, block_rows, head_count, head_depth).astype(jnp.float32)
        allowed, rel_bias = tile_terms(offsets, lengths, rab, query_at, key_at, in_use, block_rows)
        scores = jnp.einsum('tiha,tjha->thij', query_tile, key_tile) * scaling + rel_bias
        weights = jnp.where(allowed, jax.nn.silu(scores), 0.0).astype(jnp.bfloat16)
        context = jnp.einsum('thij,tjha->tiha', weights.astype(jnp.float32), value_tile)
        return (totals.at[query_at].add(context.reshape(16, block_rows, features)), None)
    totals, _ = lax.scan(advance, jnp.zeros((block_count, block_rows, features), jnp.float32), batched)
    return totals

def attend_back(queries, keys, values, grad_context, offsets, lengths, rab, pairs):
    block_count, block_rows, features = queries.shape
    head_count = rab.shape[0]
    head_depth = features // head_count
    scaling = 1.0 / math.sqrt(head_depth)
    batched = tuple((member.reshape(-1, 16) for member in pairs))

    def advance(totals, element):
        query_at, key_at, in_use = element
        shape = (16, block_rows, head_count, head_depth)
        query_tile = queries[query_at].reshape(shape).astype(jnp.float32)
        key_tile = keys[key_at].reshape(shape).astype(jnp.float32)
        value_tile = values[key_at].reshape(shape).astype(jnp.float32)
        grad_tile = grad_context[query_at].reshape(shape).astype(jnp.float32)
        allowed, rel_bias = tile_terms(offsets, lengths, rab, query_at, key_at, in_use, block_rows)
        scores = jnp.einsum('tiha,tjha->thij', query_tile, key_tile) * scaling + rel_bias
        weights = jnp.where(allowed, jax.nn.silu(scores), 0.0).astype(jnp.bfloat16).astype(jnp.float32)
        grad_weights = jnp.einsum('tiha,tjha->thij', grad_tile, value_tile)
        grad_scores = jnp.where(allowed, grad_weights * silu_slope(scores), 0.0).astype(jnp.bfloat16).astype(jnp.float32)
        grad_v = jnp.einsum('thij,tiha->tjha', weights, grad_tile)
        grad_q = jnp.einsum('thij,tjha->tiha', grad_scores, key_tile) * scaling
        grad_k = jnp.einsum('thij,tiha->tjha', grad_scores, query_tile) * scaling
        sum_q, sum_k, sum_v = totals
        sum_q = sum_q.at[query_at].add(grad_q.reshape(16, block_rows, features))
        sum_k = sum_k.at[key_at].add(grad_k.reshape(16, block_rows, features))
        sum_v = sum_v.at[key_at].add(grad_v.reshape(16, block_rows, features))
        return ((sum_q, sum_k, sum_v), None)
    empty = jnp.zeros((block_count, block_rows, features), jnp.float32)
    totals, _ = lax.scan(advance, (empty, empty, empty), batched)
    return totals

def layer(inputs, upstream_raw, offsets, lengths, w_in, w_out, rab, pairs):
    block_count, block_rows, features = inputs.shape
    row_count = block_count * block_rows
    flat = inputs.reshape(row_count, features).astype(jnp.float32)
    normed_f, norm_back = jax.vjp(normalize, flat)
    normed = normed_f.astype(jnp.bfloat16)
    preact = jnp.dot(normed, w_in, preferred_element_type=jnp.float32)
    hidden = jax.nn.silu(preact).astype(jnp.bfloat16)
    gate_u = hidden[:, :features]
    values = hidden[:, features:2 * features].reshape(block_count, block_rows, features)
    queries = hidden[:, 2 * features:3 * features].reshape(block_count, block_rows, features)
    keys = hidden[:, 3 * features:].reshape(block_count, block_rows, features)
    context = attend(queries, keys, values, offsets, lengths, rab, pairs).reshape(row_count, features)

    def combine(context_in, gate_in):
        return normalize(context_in) * gate_in
    mixed_f, mix_back = jax.vjp(combine, context, gate_u.astype(jnp.float32))
    mixed = mixed_f.astype(jnp.bfloat16)
    row_ids = jnp.arange(block_rows, dtype=jnp.int32)
    valid_rows = (offsets[:, None] * block_rows + row_ids[None, :] < lengths[:, None]).reshape(row_count, 1)
    outputs = jnp.where(valid_rows, flat + jnp.dot(mixed, w_out, preferred_element_type=jnp.float32), 0.0).astype(jnp.bfloat16)
    upstream = jnp.where(valid_rows, upstream_raw.reshape(row_count, features), jnp.zeros((), jnp.bfloat16))
    grad_mixed = jnp.dot(upstream, w_out.T, preferred_element_type=jnp.float32)
    grad_context, grad_gate = mix_back(grad_mixed)
    grad_context_b = grad_context.astype(jnp.bfloat16).reshape(block_count, block_rows, features)
    grad_q, grad_k, grad_v = attend_back(queries, keys, values, grad_context_b, offsets, lengths, rab, pairs)
    joined = jnp.concatenate([grad_gate, grad_v.reshape(row_count, features), grad_q.reshape(row_count, features), grad_k.reshape(row_count, features)], axis=1)
    grad_hidden = (joined * silu_slope(preact)).astype(jnp.bfloat16)
    grad_w_in = jnp.dot(normed.T, grad_hidden, preferred_element_type=jnp.float32)
    grad_w_out = jnp.dot(mixed.T, upstream, preferred_element_type=jnp.float32)
    grad_normed, = norm_back(jnp.dot(grad_hidden, w_in.T, preferred_element_type=jnp.float32))
    grad_inputs = (upstream.astype(jnp.float32) + grad_normed).astype(jnp.bfloat16)
    return (outputs, grad_inputs, grad_w_in, grad_w_out)

def reference(events, route, block_offset, hist_length, cotangent, w_in, w_out, rab):
    devices = N_GROUP * N_MEMBER
    features = events.shape[1]
    pieces = events.reshape(N_GROUP, N_MEMBER * PIECES_DEV, PIECE, features)
    routes = route.reshape(N_GROUP, N_MEMBER * PIECES_DEV)

    def place(group_pieces, group_route):
        return jnp.zeros_like(group_pieces).at[group_route].set(group_pieces)
    balanced = jax.vmap(place)(pieces, routes).reshape(devices, BLK_DEV, BLOCK, features)
    upstream = cotangent.reshape(devices, BLK_DEV, BLOCK, features)
    offsets = block_offset.reshape(devices, BLK_DEV)
    lengths = hist_length.reshape(devices, BLK_DEV)

    def per_device(running, element):
        inputs, grads_in, device_offsets, device_lengths = element
        pairs = listed_pairs(device_offsets)
        layer_out, grad_inputs, grad_in, grad_out = layer(inputs, grads_in, device_offsets, device_lengths, w_in, w_out, rab, pairs)
        return ((running[0] + grad_in, running[1] + grad_out), (layer_out, grad_inputs))
    start = (jnp.zeros((features, 4 * features), jnp.float32), jnp.zeros((features, features), jnp.float32))
    sums, stacked = lax.scan(per_device, start, (balanced, upstream, offsets, lengths))
    outputs, grad_balanced = stacked
    scaling = 1.0 / math.sqrt(ROWS)

    def fetch(group_grads, group_route):
        return group_grads[group_route]
    grad_pieces = grad_balanced.reshape(N_GROUP, N_MEMBER * PIECES_DEV, PIECE, features)
    events_grad = jax.vmap(fetch)(grad_pieces, routes).reshape(ROWS, features)
    return (outputs.reshape(ROWS, features), events_grad, sums[0] * scaling, sums[1] * scaling)
```

```python
import functools
import math

import jax
import jax.numpy as jnp
from jax import lax
from jax.experimental import pallas as pl
from jax.experimental.pallas import tpu as pltpu
from jax.sharding import PartitionSpec as P

EPS = 1e-05
BF16 = jnp.bfloat16
F32 = jnp.float32
VMEM_LIMIT = 48 * 1024 * 1024

ROWS, D, HID = 512, 512, 2048
BLOCK, BLOCKS, HEADS, BUCKETS = 128, 4, 4, 12
PIECE, PIECES, MEMBERS = 16, 32, 64
LABEL = 128
CHUNK = 640
SCALE = 1.0 / math.sqrt(128)


def dot(a, b):
    return jnp.dot(a, b, preferred_element_type=F32)


def dot_nt(a, b):
    return lax.dot_general(a, b, (((1,), (1,)), ((), ())), preferred_element_type=F32)


def dot_tn(a, b):
    return lax.dot_general(a, b, (((0,), (0,)), ((), ())), preferred_element_type=F32)


def sigmoid(v):
    return 0.5 * jnp.tanh(0.5 * v) + 0.5


def full_spec(memory=pltpu.VMEM):
    return pl.BlockSpec(memory_space=memory)


def pack_kernel(route_ref, events_ref, out_ref):
    out_ref[...] = jnp.zeros_like(out_ref)
    for j in range(PIECES):
        target = route_ref[j]
        device = lax.shift_right_logical(target, 5)
        place = lax.bitwise_and(target, PIECES - 1)
        out_ref[device, :, :D] = events_ref[j * PIECE : (j + 1) * PIECE, :]
        label = jnp.full((PIECE, LABEL), (place + 1).astype(F32), F32)
        out_ref[device, :, D:] = label.astype(BF16)


def pack(route, events):
    return pl.pallas_call(
        pack_kernel,
        out_shape=jax.ShapeDtypeStruct((MEMBERS, PIECE, D + LABEL), BF16),
        in_specs=[full_spec(pltpu.SMEM), full_spec()],
        out_specs=full_spec(),
        compiler_params=pltpu.CompilerParams(vmem_limit_bytes=VMEM_LIMIT),
        name="pack_pieces",
    )(route, events)


def layer_kernel(
    core_ref,
    offset_ref,
    length_ref,
    rab_ref,
    arrived_ref,
    cot_ref,
    w_in_ref,
    w_out_ref,
    out_ref,
    own_ref,
    other_ref,
    back_ref,
    place_s,
    bal_s,
    norm_s,
    xhat_s,
    rstd_s,
    hid_s,
    slope_s,
    att_s,
    asl_s,
    ctx_s,
    gm_s,
    mixed_s,
    up_s,
    gctx_s,
    g_s,
    gh_s,
    normt_s,
    gb_s,
):
    core = core_ref[0]
    pick = (lax.broadcasted_iota(jnp.int32, (8, LABEL), 1) == 0).astype(BF16)
    labels = dot_nt(pick, arrived_ref[:, D:])[0:1, :]
    cell_row = lax.bitwise_and(
        lax.broadcasted_iota(jnp.int32, (1, MEMBERS * PIECE), 1), PIECE - 1
    ).astype(F32)
    goal = (labels - 1.0) * PIECE + cell_row
    for b in range(BLOCKS):
        rows = lax.broadcasted_iota(jnp.int32, (BLOCK, 1), 0).astype(F32) + float(b * BLOCK)
        place_s[b * BLOCK : (b + 1) * BLOCK, :] = jnp.where(goal == rows, 1.0, 0.0).astype(BF16)
    for n in range(0, D, 256):
        bal_s[:, n : n + 256] = dot(place_s[...], arrived_ref[:, n : n + 256]).astype(BF16)

    for r in range(0, ROWS, 64):
        sl = slice(r, r + 64)
        x = bal_s[sl, :].astype(F32)
        centered = x - jnp.mean(x, axis=-1, keepdims=True)
        variance = jnp.mean(centered * centered, axis=-1, keepdims=True)
        rstd = lax.rsqrt(variance + EPS)
        xhat = centered * rstd
        xhat_s[sl, :] = xhat
        rstd_s[sl, :] = jnp.broadcast_to(rstd, (64, 128))
        norm_s[sl, :] = xhat.astype(BF16)

    for n in range(0, HID, 256):
        cols = slice(n, n + 256)
        v = dot(norm_s[...], w_in_ref[:, cols])
        g = sigmoid(v)
        h = v * g
        hid_s[:, cols] = h.astype(BF16)
        slope_s[:, cols] = g + h * (1.0 - g)

    row_id = lax.broadcasted_iota(jnp.int32, (BLOCK, BLOCK), 0)
    col_id = lax.broadcasted_iota(jnp.int32, (BLOCK, BLOCK), 1)

    def bias(head, distance):
        total = jnp.full((BLOCK, BLOCK), rab_ref[head, 0], F32)
        for bucket in range(1, 9):
            total = jnp.where(distance >= 2 ** (bucket - 1), rab_ref[head, bucket], total)
        return total

    def head_cols(part, head):
        return slice(part * D + head * 128, part * D + head * 128 + 128)

    second = jnp.int32(0)
    for b in range(1, BLOCKS):
        second = jnp.where(offset_ref[b] == 1, b, second)
    first = jnp.maximum(second - 1, 0)
    second_rows = pl.ds(pl.multiple_of(second * BLOCK, BLOCK), BLOCK)
    first_rows = pl.ds(pl.multiple_of(first * BLOCK, BLOCK), BLOCK)

    def live_rows(block):
        position = row_id + offset_ref[block] * BLOCK
        return position < length_ref[block]

    def attend(q_rows, k_rows, allowed, relative, head, tile):
        q = hid_s[q_rows, head_cols(2, head)]
        k = hid_s[k_rows, head_cols(3, head)]
        s = dot_nt(q, k) * SCALE + relative
        g = sigmoid(s)
        a = s * g
        asl_s[tile, head] = jnp.where(allowed, g + a * (1.0 - g), 0.0)
        a = jnp.where(allowed, a, 0.0).astype(BF16)
        att_s[tile, head] = a
        return dot(a, hid_s[k_rows, head_cols(1, head)])

    own_distance = row_id - col_id
    for head in range(HEADS):
        relative = bias(head, own_distance)
        for b in range(BLOCKS):
            rows = slice(b * BLOCK, (b + 1) * BLOCK)
            allowed = (own_distance >= 0) & live_rows(b)
            ctx_s[rows, head_cols(0, head)] = attend(rows, rows, allowed, relative, head, b)
    far_allowed = live_rows(second)
    for head in range(HEADS):
        relative = bias(head, own_distance + BLOCK)
        cols = head_cols(0, head)
        ctx_s[second_rows, cols] += attend(
            second_rows, first_rows, far_allowed, relative, head, BLOCKS
        )

    for b in range(BLOCKS):
        rows = slice(b * BLOCK, (b + 1) * BLOCK)
        live = (
            lax.broadcasted_iota(jnp.int32, (BLOCK, 1), 0) + offset_ref[b] * BLOCK < length_ref[b]
        )
        up_s[rows, :] = jnp.where(live, cot_ref[rows, :].astype(F32), 0.0).astype(BF16)
    gm_s[...] = dot_nt(up_s[...], w_out_ref[...])
    for r in range(0, ROWS, 64):
        sl = slice(r, r + 64)
        c = ctx_s[sl, :]
        centered = c - jnp.mean(c, axis=-1, keepdims=True)
        variance = jnp.mean(centered * centered, axis=-1, keepdims=True)
        rstd = lax.rsqrt(variance + EPS)
        n = centered * rstd
        u = hid_s[sl, 0:D].astype(F32)
        mixed_s[sl, :] = (n * u).astype(BF16)
        gm = gm_s[sl, :]
        gh_s[sl, 0:D] = (gm * n * slope_s[sl, 0:D]).astype(BF16)
        gn = gm * u
        gctx = rstd * (
            gn
            - jnp.mean(gn, axis=-1, keepdims=True)
            - n * jnp.mean(gn * n, axis=-1, keepdims=True)
        )
        gctx_s[sl, :] = gctx.astype(BF16)
    gm_s[...] = dot(mixed_s[...], w_out_ref[...])
    for b in range(BLOCKS):
        rows = slice(b * BLOCK, (b + 1) * BLOCK)
        live = (
            lax.broadcasted_iota(jnp.int32, (BLOCK, 1), 0) + offset_ref[b] * BLOCK < length_ref[b]
        )
        out_ref[rows, :] = jnp.where(live, bal_s[rows, :].astype(F32) + gm_s[rows, :], 0.0).astype(
            BF16
        )

    def attend_back(q_rows, k_rows, head, tile):
        gc = gctx_s[q_rows, head_cols(0, head)]
        q = hid_s[q_rows, head_cols(2, head)]
        k = hid_s[k_rows, head_cols(3, head)]
        v = hid_s[k_rows, head_cols(1, head)]
        ds = (dot_nt(gc, v) * asl_s[tile, head]).astype(BF16)
        gv = dot_tn(att_s[tile, head], gc)
        gq = dot(ds, k) * SCALE
        gk = dot_tn(ds, q) * SCALE
        return gv, gq, gk

    for head in range(HEADS):
        for b in range(BLOCKS):
            rows = slice(b * BLOCK, (b + 1) * BLOCK)
            gv, gq, gk = attend_back(rows, rows, head, b)
            g_s[rows, head_cols(0, head)] = gv
            g_s[rows, head_cols(1, head)] = gq
            g_s[rows, head_cols(2, head)] = gk
    for head in range(HEADS):
        gv, gq, gk = attend_back(second_rows, first_rows, head, BLOCKS)
        g_s[first_rows, head_cols(0, head)] += gv
        g_s[second_rows, head_cols(1, head)] += gq
        g_s[first_rows, head_cols(2, head)] += gk
    for r in range(0, ROWS, 64):
        sl = slice(r, r + 64)
        for n in range(0, 3 * D, D):
            gh_s[sl, D + n : 2 * D + n] = (
                g_s[sl, n : n + D] * slope_s[sl, D + n : 2 * D + n]
            ).astype(BF16)

    normt_s[...] = norm_s[...].T

    def store(quarter, start, value):
        half, side = quarter // 2, quarter % 2
        value = value.astype(BF16).reshape(PIECES, PIECE, value.shape[1])
        stop = start + value.shape[2]

        @pl.when(core == half)
        def _():
            own_ref[:, side, :, start:stop] = value

        @pl.when(core != half)
        def _():
            other_ref[:, side, :, start:stop] = value

    for quarter in range(4):
        for n in range(0, CHUNK, 128):
            at = quarter * CHUNK + n
            if at < HID:
                store(quarter, n, dot(normt_s[...], gh_s[:, at : at + 128]))
    normt_s[...] = mixed_s[...].T
    store(3, 128, dot(normt_s[...], up_s[...]))

    gm_s[...] = dot_nt(gh_s[...], w_in_ref[...])
    for r in range(0, ROWS, 64):
        sl = slice(r, r + 64)
        gx = gm_s[sl, :]
        xhat = xhat_s[sl, :]
        rstd = rstd_s[sl, 0:1]
        gx = rstd * (
            gx
            - jnp.mean(gx, axis=-1, keepdims=True)
            - xhat * jnp.mean(gx * xhat, axis=-1, keepdims=True)
        )
        gb_s[sl, :] = (up_s[sl, :].astype(F32) + gx).astype(BF16)
    for n in range(0, D, 256):
        back_ref[:, n : n + 256] = dot_tn(place_s[...], gb_s[:, n : n + 256]).astype(BF16)


def layer(core, offsets, lengths, rab, arrived, cotangent, w_in, w_out):
    half = jax.ShapeDtypeStruct((PIECES, 2, PIECE, CHUNK), BF16)
    scratch = [
        ((ROWS, MEMBERS * PIECE), BF16),
        ((ROWS, D), BF16),
        ((ROWS, D), BF16),
        ((ROWS, D), F32),
        ((ROWS, 128), F32),
        ((ROWS, HID), BF16),
        ((ROWS, HID), F32),
        ((BLOCKS + 1, HEADS, BLOCK, BLOCK), BF16),
        ((BLOCKS + 1, HEADS, BLOCK, BLOCK), F32),
        ((ROWS, D), F32),
        ((ROWS, D), F32),
        ((ROWS, D), BF16),
        ((ROWS, D), BF16),
        ((ROWS, D), BF16),
        ((ROWS, 3 * D), F32),
        ((ROWS, HID), BF16),
        ((ROWS, D), BF16),
        ((ROWS, D), BF16),
    ]
    return pl.pallas_call(
        layer_kernel,
        out_shape=(
            jax.ShapeDtypeStruct((ROWS, D), BF16),
            half,
            half,
            jax.ShapeDtypeStruct((MEMBERS * PIECE, D), BF16),
        ),
        in_specs=[full_spec(pltpu.SMEM)] * 4 + [full_spec()] * 4,
        out_specs=(full_spec(),) * 4,
        scratch_shapes=[pltpu.VMEM(shape, kind) for shape, kind in scratch],
        compiler_params=pltpu.CompilerParams(vmem_limit_bytes=VMEM_LIMIT),
        cost_estimate=pl.CostEstimate(
            flops=5_000_000_000, bytes_accessed=9_000_000, transcendentals=1_500_000
        ),
        name="layer",
    )(core, offsets, lengths, rab, arrived, cotangent, w_in, w_out)


def join_kernel(own_ref, got_ref, back_ref, out_ref):
    out_ref[:, :, :CHUNK] = (own_ref[...].astype(F32) + got_ref[...].astype(F32)).astype(BF16)
    out_ref[:, :, CHUNK:] = back_ref[...]


def join(own, got, back):
    step = 16
    spec = lambda width: pl.BlockSpec((step, PIECE, width), lambda i: (i, 0, 0))
    return pl.pallas_call(
        join_kernel,
        out_shape=jax.ShapeDtypeStruct((MEMBERS, PIECE, CHUNK + D), BF16),
        grid=(MEMBERS // step,),
        in_specs=[spec(CHUNK), spec(CHUNK), spec(D)],
        out_specs=spec(CHUNK + D),
        compiler_params=pltpu.CompilerParams(vmem_limit_bytes=VMEM_LIMIT),
        name="join",
    )(own, got, back)


def total_kernel(route_ref, mixed_ref, share_ref, events_ref):
    total = mixed_ref[0, :, :CHUNK].astype(F32)
    for m in range(1, MEMBERS):
        total += mixed_ref[m, :, :CHUNK].astype(F32)
    total = (total * (1.0 / 256.0)).astype(BF16)
    share_ref[...] = jnp.broadcast_to(total[None], (MEMBERS, PIECE, CHUNK))
    for j in range(PIECES):
        device = lax.shift_right_logical(route_ref[j], 5)
        events_ref[j * PIECE : (j + 1) * PIECE, :] = mixed_ref[device, :, CHUNK:]


def total(route, received):
    return pl.pallas_call(
        total_kernel,
        out_shape=(
            jax.ShapeDtypeStruct((MEMBERS, PIECE, CHUNK), BF16),
            jax.ShapeDtypeStruct((ROWS, D), BF16),
        ),
        in_specs=[full_spec(pltpu.SMEM), full_spec()],
        out_specs=(full_spec(),) * 2,
        compiler_params=pltpu.CompilerParams(vmem_limit_bytes=VMEM_LIMIT),
        name="total",
    )(route, received)


def spread_kernel(core_ref, own_ref, other_ref, w_in_ref, w_out_ref):
    core = core_ref[0]
    rows = w_in_ref.shape[0]

    def put(source, half):
        for side in range(2):
            value = source[:, side].astype(F32).reshape(rows, CHUNK)
            at = (2 * half + side) * CHUNK
            keep = min(CHUNK, HID - at)
            w_in_ref[:, at : at + keep] = value[:, :keep]
            if keep < CHUNK:
                w_out_ref[...] = value[:, keep:]

    @pl.when(core == 0)
    def _():
        put(own_ref, 0)
        put(other_ref, 1)

    @pl.when(core != 0)
    def _():
        put(other_ref, 0)
        put(own_ref, 1)


def spread(core, own, other):
    step = 8
    shape = (PIECES, 2, PIECE, CHUNK)
    half = pl.BlockSpec((step, 2, PIECE, CHUNK), lambda i: (i, 0, 0, 0))
    rows = step * PIECE
    return pl.pallas_call(
        spread_kernel,
        out_shape=(
            jax.ShapeDtypeStruct((D, HID), F32),
            jax.ShapeDtypeStruct((D, D), F32),
        ),
        grid=(PIECES // step,),
        in_specs=[full_spec(pltpu.SMEM), half, half],
        out_specs=(
            pl.BlockSpec((rows, HID), lambda i: (i, 0)),
            pl.BlockSpec((rows, D), lambda i: (i, 0)),
        ),
        compiler_params=pltpu.CompilerParams(vmem_limit_bytes=VMEM_LIMIT),
        name="spread",
    )(core, own.reshape(shape), other.reshape(shape))


def body(events, route, block_offset, hist_length, cotangent, w_in, w_out, rab):
    core = lax.axis_index("group").astype(jnp.int32).reshape(1)
    exchange = functools.partial(
        lax.all_to_all, axis_name="member", split_axis=0, concat_axis=0, tiled=True
    )
    swap = functools.partial(lax.ppermute, axis_name="group", perm=[(0, 1), (1, 0)])
    arrived = exchange(pack(route, events))
    outputs, own, other, back = layer(
        core,
        block_offset,
        hist_length,
        rab,
        arrived.reshape(MEMBERS * PIECE, D + LABEL),
        cotangent,
        w_in,
        w_out,
    )
    got = swap(other)
    slots = (MEMBERS, PIECE, CHUNK)
    received = exchange(
        join(own.reshape(slots), got.reshape(slots), back.reshape(MEMBERS, PIECE, D))
    )
    share, events_grad = total(route, received)
    mine = exchange(share)
    theirs = swap(mine)
    w_in_grad, w_out_grad = spread(core, mine, theirs)
    return outputs, events_grad, w_in_grad, w_out_grad


def solution(mesh):
    placed = (
        P(("group", "member"), None),
        P(("group", "member")),
        P(("group", "member")),
        P(("group", "member")),
        P(("group", "member"), None),
        P(),
        P(),
        P(),
    )
    return jax.shard_map(
        body,
        mesh=mesh,
        in_specs=placed,
        out_specs=(P(("group", "member"), None), P(("group", "member"), None), P(), P()),
        check_vma=False,
    )
```

```python
import functools
import math

import jax
import jax.numpy as jnp
from jax import lax
from jax.experimental import pallas as pl
from jax.experimental.pallas import tpu as pltpu
from jax.sharding import PartitionSpec as P

EPS = 1e-05
BF16 = jnp.bfloat16
F32 = jnp.float32
VMEM_LIMIT = 32 * 1024 * 1024
VMEM_SMALL = 16 * 1024 * 1024
VMEM_MOST = 56 * 1024 * 1024

ROWS, D, HID = 512, 512, 2048
BLOCK, BLOCKS, HEADS, BUCKETS = 128, 4, 4, 12
PIECE, PIECES, MEMBERS = 16, 32, 64
SLOT = 72
CHUNK = 640
SCALE = 1.0 / math.sqrt(128)
HALF = D // 2
SHARES = (HALF // PIECE, 4, PIECE, CHUNK)


def dot(a, b):
    return jnp.dot(a, b, preferred_element_type=F32)


def dot_nt(a, b):
    return lax.dot_general(a, b, (((1,), (1,)), ((), ())), preferred_element_type=F32)


def dot_tn(a, b):
    return lax.dot_general(a, b, (((0,), (0,)), ((), ())), preferred_element_type=F32)


def sigmoid(v):
    return 0.5 * jnp.tanh(0.5 * v) + 0.5


def in_hbm(array):
    return pltpu.with_memory_space_constraint(array, pltpu.HBM)


def full_spec(memory=pltpu.VMEM):
    return pl.BlockSpec(memory_space=memory)


def pack_kernel(route_hbm, events_hbm, out_ref, route_s, events_s, sems):
    copies = [
        pltpu.make_async_copy(route_hbm, route_s, sems.at[0]),
        pltpu.make_async_copy(events_hbm, events_s, sems.at[1]),
    ]
    for copy in copies:
        copy.start()
    out_ref[...] = jnp.zeros_like(out_ref)
    for copy in copies:
        copy.wait()
    for j in range(PIECES):
        target = route_s[j]
        device = lax.shift_right_logical(target, 5)
        place = lax.bitwise_and(target, PIECES - 1)
        for k in range(D // 128):
            out_ref[device, k * PIECE : (k + 1) * PIECE, :] = events_s[
                j * PIECE : (j + 1) * PIECE, k * 128 : (k + 1) * 128
            ]
        label = jnp.full((SLOT - 4 * PIECE, 128), (place + 1).astype(F32), F32)
        out_ref[device, 4 * PIECE :, :] = label.astype(BF16)


def pack(route, events):
    return pl.pallas_call(
        pack_kernel,
        out_shape=jax.ShapeDtypeStruct((MEMBERS, SLOT, 128), BF16),
        in_specs=[full_spec(pltpu.HBM)] * 2,
        out_specs=full_spec(),
        scratch_shapes=[
            pltpu.SMEM((PIECES,), jnp.int32),
            pltpu.VMEM((ROWS, D), BF16),
            pltpu.SemaphoreType.DMA((2,)),
        ],
        compiler_params=pltpu.CompilerParams(vmem_limit_bytes=VMEM_MOST),
        name="pack_pieces",
    )(in_hbm(route), in_hbm(events))


def cell_goals(arrived_ref):
    labels = arrived_ref[:, 4 * PIECE :, :].astype(F32)
    if labels.shape[1] < PIECE:
        labels = jnp.concatenate([labels, labels], axis=1)
    within = lax.broadcasted_iota(jnp.int32, labels.shape, 1).astype(F32)
    return ((labels - 1.0) * PIECE + within).reshape(MEMBERS * PIECE, 128)


def layer_kernel(
    core_ref,
    offset_ref,
    length_ref,
    rab_ref,
    arrived_ref,
    cot_hbm,
    w_in_hbm,
    w_out_hbm,
    out_ref,
    other_ref,
    left_ref,
    up_s,
    gh_s,
    bal_s,
    place_s,
    norm_s,
    hid_s,
    slope_s,
    att_s,
    asl_s,
    ctx_s,
    gm_s,
    mixed_s,
    gctx_s,
    g_s,
    trans_s,
    cot_ref,
    w_in_ref,
    w_out_ref,
    sems,
):
    copies = [
        pltpu.make_async_copy(w_in_hbm, w_in_ref, sems.at[0]),
        pltpu.make_async_copy(cot_hbm, cot_ref, sems.at[1]),
        pltpu.make_async_copy(w_out_hbm, w_out_ref, sems.at[2]),
    ]
    for copy in copies:
        copy.start()
    core = core_ref[0]
    goals = cell_goals(arrived_ref)
    pick = (lax.broadcasted_iota(jnp.int32, (8, 128), 1) == 0).astype(BF16)
    tens = dot_nt(pick, jnp.floor(goals * (1.0 / 16.0)).astype(BF16))[0:1, :]
    ones = lax.bitwise_and(
        lax.broadcasted_iota(jnp.int32, (1, MEMBERS * PIECE), 1), PIECE - 1
    ).astype(F32)
    goal = tens * PIECE + ones
    for b in range(BLOCKS):
        rows = lax.broadcasted_iota(jnp.int32, (BLOCK, 1), 0).astype(F32) + float(b * BLOCK)
        place_s[b * BLOCK : (b + 1) * BLOCK, :] = jnp.where(goal == rows, 1.0, 0.0).astype(BF16)
    for k in range(0, D // 128, 2):
        cells = jnp.concatenate(
            [
                arrived_ref[:, n * PIECE : (n + 1) * PIECE, :].reshape(MEMBERS * PIECE, 128)
                for n in (k, k + 1)
            ],
            axis=1,
        )
        bal_s[:, k * 128 : k * 128 + 256] = dot(place_s[...], cells).astype(BF16)

    for r in range(0, ROWS, 64):
        sl = slice(r, r + 64)
        x = bal_s[sl, :].astype(F32)
        centered = x - jnp.mean(x, axis=-1, keepdims=True)
        variance = jnp.mean(centered * centered, axis=-1, keepdims=True)
        rstd = lax.rsqrt(variance + EPS)
        xhat = centered * rstd
        norm_s[sl, :] = xhat.astype(BF16)

    copies[0].wait()
    for n in range(0, HID, 256):
        cols = slice(n, n + 256)
        v = dot(norm_s[...], w_in_ref[:, cols])
        g = sigmoid(v)
        h = v * g
        hid_s[:, cols] = h.astype(BF16)
        slope_s[:, cols] = g + h * (1.0 - g)

    row_id = lax.broadcasted_iota(jnp.int32, (BLOCK, BLOCK), 0)
    col_id = lax.broadcasted_iota(jnp.int32, (BLOCK, BLOCK), 1)

    def bias(head, distance):
        total = jnp.full((BLOCK, BLOCK), rab_ref[head, 0], F32)
        for bucket in range(1, 9):
            total = jnp.where(distance >= 2 ** (bucket - 1), rab_ref[head, bucket], total)
        return total

    def head_cols(part, head):
        return slice(part * D + head * 128, part * D + head * 128 + 128)

    second = jnp.int32(0)
    for b in range(1, BLOCKS):
        second = jnp.where(offset_ref[b] == 1, b, second)
    first = jnp.maximum(second - 1, 0)
    second_rows = pl.ds(pl.multiple_of(second * BLOCK, BLOCK), BLOCK)
    first_rows = pl.ds(pl.multiple_of(first * BLOCK, BLOCK), BLOCK)

    def live_rows(block):
        position = row_id + offset_ref[block] * BLOCK
        return position < length_ref[block]

    def attend(q_rows, k_rows, allowed, relative, head, tile):
        q = hid_s[q_rows, head_cols(2, head)]
        k = hid_s[k_rows, head_cols(3, head)]
        s = dot_nt(q, k) * SCALE + relative
        g = sigmoid(s)
        a = s * g
        asl_s[tile, head] = jnp.where(allowed, g + a * (1.0 - g), 0.0)
        a = jnp.where(allowed, a, 0.0).astype(BF16)
        att_s[tile, head] = a
        return dot(a, hid_s[k_rows, head_cols(1, head)])

    own_distance = row_id - col_id
    for head in range(HEADS):
        relative = bias(head, own_distance)
        for b in range(BLOCKS):
            rows = slice(b * BLOCK, (b + 1) * BLOCK)
            allowed = (own_distance >= 0) & live_rows(b)
            ctx_s[rows, head_cols(0, head)] = attend(rows, rows, allowed, relative, head, b)
    far_allowed = live_rows(second)
    for head in range(HEADS):
        relative = bias(head, own_distance + BLOCK)
        cols = head_cols(0, head)
        ctx_s[second_rows, cols] += attend(
            second_rows, first_rows, far_allowed, relative, head, BLOCKS
        )

    for copy in copies[1:]:
        copy.wait()
    for b in range(BLOCKS):
        rows = slice(b * BLOCK, (b + 1) * BLOCK)
        live = (
            lax.broadcasted_iota(jnp.int32, (BLOCK, 1), 0) + offset_ref[b] * BLOCK < length_ref[b]
        )
        up_s[rows, :] = jnp.where(live, cot_ref[rows, :].astype(F32), 0.0).astype(BF16)
    gm_s[...] = dot_nt(up_s[...], w_out_ref[...])
    for r in range(0, ROWS, 64):
        sl = slice(r, r + 64)
        c = ctx_s[sl, :]
        centered = c - jnp.mean(c, axis=-1, keepdims=True)
        variance = jnp.mean(centered * centered, axis=-1, keepdims=True)
        rstd = lax.rsqrt(variance + EPS)
        n = centered * rstd
        u = hid_s[sl, 0:D].astype(F32)
        mixed_s[sl, :] = (n * u).astype(BF16)
        gm = gm_s[sl, :]
        gh_s[sl, 0:D] = (gm * n * slope_s[sl, 0:D]).astype(BF16)
        gn = gm * u
        gctx = rstd * (
            gn
            - jnp.mean(gn, axis=-1, keepdims=True)
            - n * jnp.mean(gn * n, axis=-1, keepdims=True)
        )
        gctx_s[sl, :] = gctx.astype(BF16)
    gm_s[...] = dot(mixed_s[...], w_out_ref[...])
    for b in range(BLOCKS):
        rows = slice(b * BLOCK, (b + 1) * BLOCK)
        live = (
            lax.broadcasted_iota(jnp.int32, (BLOCK, 1), 0) + offset_ref[b] * BLOCK < length_ref[b]
        )
        out_ref[rows, :] = jnp.where(live, bal_s[rows, :].astype(F32) + gm_s[rows, :], 0.0).astype(
            BF16
        )

    def attend_back(q_rows, k_rows, head, tile):
        gc = gctx_s[q_rows, head_cols(0, head)]
        q = hid_s[q_rows, head_cols(2, head)]
        k = hid_s[k_rows, head_cols(3, head)]
        v = hid_s[k_rows, head_cols(1, head)]
        ds = (dot_nt(gc, v) * asl_s[tile, head]).astype(BF16)
        gv = dot_tn(att_s[tile, head], gc)
        gq = dot(ds, k) * SCALE
        gk = dot_tn(ds, q) * SCALE
        return gv, gq, gk

    for head in range(HEADS):
        for b in range(BLOCKS):
            rows = slice(b * BLOCK, (b + 1) * BLOCK)
            gv, gq, gk = attend_back(rows, rows, head, b)
            g_s[rows, head_cols(0, head)] = gv
            g_s[rows, head_cols(1, head)] = gq
            g_s[rows, head_cols(2, head)] = gk
    for head in range(HEADS):
        gv, gq, gk = attend_back(second_rows, first_rows, head, BLOCKS)
        g_s[first_rows, head_cols(0, head)] += gv
        g_s[second_rows, head_cols(1, head)] += gq
        g_s[first_rows, head_cols(2, head)] += gk
    for r in range(0, ROWS, 64):
        sl = slice(r, r + 64)
        for n in range(0, 3 * D, D):
            gh_s[sl, D + n : 2 * D + n] = (
                g_s[sl, n : n + D] * slope_s[sl, D + n : 2 * D + n]
            ).astype(BF16)

    own_rows = pl.ds(pl.multiple_of(core * HALF, HALF), HALF)
    other_rows = pl.ds(pl.multiple_of((1 - core) * HALF, HALF), HALF)
    trans_s[0] = norm_s[...].T
    trans_s[1] = mixed_s[...].T
    left_ref[0] = trans_s[0, own_rows, :]
    left_ref[1] = trans_s[1, own_rows, :]

    def store(at, value):
        other_ref[at] = value.astype(BF16)

    weight_grads(trans_s[0, other_rows, :], trans_s[1, other_rows, :], gh_s, up_s, store)


def weight_grads(normed_t, mixed_t, gh_ref, up_ref, store):
    for at in range(0, HID + D, 256):
        if at < HID:
            value = dot(normed_t, gh_ref[:, at : at + 256])
        else:
            value = dot(mixed_t, up_ref[:, at - HID : at - HID + 256])
        for n in (0, 128):
            side, start = (at + n) // CHUNK, (at + n) % CHUNK
            shares = value[:, n : n + 128].reshape(HALF // PIECE, PIECE, 128)
            store((slice(None), side, slice(None), slice(start, start + 128)), shares)


def own_kernel(left_ref, up_ref, gh_ref, out_ref):
    def store(at, value):
        out_ref[at] = value.astype(BF16)

    weight_grads(left_ref[0], left_ref[1], gh_ref, up_ref, store)


def own_part(left, up, gh):
    return pl.pallas_call(
        own_kernel,
        out_shape=jax.ShapeDtypeStruct(SHARES, BF16),
        in_specs=[full_spec()] * 3,
        out_specs=full_spec(),
        compiler_params=pltpu.CompilerParams(vmem_limit_bytes=VMEM_SMALL),
        cost_estimate=pl.CostEstimate(
            flops=700_000_000, bytes_accessed=6_000_000, transcendentals=0
        ),
        name="own_part",
    )(left, up, gh)


def join_kernel(own_ref, got_ref, out_ref):
    out_ref[...] = (own_ref[...].astype(F32) + got_ref[...].astype(F32)).astype(BF16)


def join(own, got):
    return pl.pallas_call(
        join_kernel,
        out_shape=jax.ShapeDtypeStruct(SHARES, BF16),
        in_specs=[full_spec()] * 2,
        out_specs=full_spec(),
        compiler_params=pltpu.CompilerParams(vmem_limit_bytes=VMEM_SMALL),
        cost_estimate=pl.CostEstimate(flops=1_000_000, bytes_accessed=4_000_000, transcendentals=0),
        name="join",
    )(own, got)


def rest_kernel(
    arrived_hbm,
    up_hbm,
    gh_hbm,
    bal_hbm,
    w_in_hbm,
    back_hbm,
    arrived_ref,
    up_ref,
    gh_ref,
    bal_ref,
    w_in_ref,
    back_ref,
    gx_s,
    gb_s,
    place_s,
    sems,
):
    loads = [
        pltpu.make_async_copy(source, target, sems.at[n])
        for n, (source, target) in enumerate(
            (
                (gh_hbm, gh_ref),
                (w_in_hbm, w_in_ref),
                (bal_hbm, bal_ref),
                (up_hbm, up_ref),
                (arrived_hbm, arrived_ref),
            )
        )
    ]
    for load in loads:
        load.start()
    loads[0].wait()
    loads[1].wait()
    gx_s[...] = dot_nt(gh_ref[...], w_in_ref[...])
    loads[2].wait()
    loads[3].wait()
    for r in range(0, ROWS, 64):
        sl = slice(r, r + 64)
        x = bal_ref[sl, :].astype(F32)
        centered = x - jnp.mean(x, axis=-1, keepdims=True)
        variance = jnp.mean(centered * centered, axis=-1, keepdims=True)
        rstd = lax.rsqrt(variance + EPS)
        xhat = centered * rstd
        gx = gx_s[sl, :]
        gx = rstd * (
            gx
            - jnp.mean(gx, axis=-1, keepdims=True)
            - xhat * jnp.mean(gx * xhat, axis=-1, keepdims=True)
        )
        gb_s[sl, :] = (up_ref[sl, :].astype(F32) + gx).astype(BF16)
    loads[4].wait()
    goals = cell_goals(arrived_ref)
    for b in range(BLOCKS):
        row = lax.broadcasted_iota(jnp.int32, (1, BLOCK), 1).astype(F32) + float(b * BLOCK)
        place_s[:, b * BLOCK : (b + 1) * BLOCK] = jnp.where(goals == row, 1.0, 0.0).astype(BF16)
    for n in range(0, D, 256):
        back_ref[:, n : n + 256] = dot(place_s[...], gb_s[:, n : n + 256]).astype(BF16)
    out = pltpu.make_async_copy(back_ref, back_hbm, sems.at[5])
    out.start()
    out.wait()


def rest(arrived, up, gh, bal, w_in):
    shapes = [(MEMBERS, SLOT, 128), (ROWS, D), (ROWS, HID), (ROWS, D), (D, HID)]
    shapes += [(MEMBERS * PIECE, D)]
    return pl.pallas_call(
        rest_kernel,
        out_shape=pltpu.HBM((MEMBERS * PIECE, D), BF16),
        in_specs=[full_spec(pltpu.HBM)] * 5,
        out_specs=full_spec(pltpu.HBM),
        scratch_shapes=[pltpu.VMEM(shape, BF16) for shape in shapes]
        + [
            pltpu.VMEM((ROWS, D), F32),
            pltpu.VMEM((ROWS, D), BF16),
            pltpu.VMEM((MEMBERS * PIECE, ROWS), BF16),
            pltpu.SemaphoreType.DMA((6,)),
        ],
        compiler_params=pltpu.CompilerParams(vmem_limit_bytes=VMEM_SMALL),
        cost_estimate=pl.CostEstimate(
            flops=2_500_000_000, bytes_accessed=9_000_000, transcendentals=1_000
        ),
        name="rest",
    )(*map(in_hbm, (arrived, up, gh, bal, w_in)))


def layer(core, offsets, lengths, rab, arrived, cotangent, w_in, w_out):
    scratch = [
        ((ROWS, MEMBERS * PIECE), BF16),
        ((ROWS, D), BF16),
        ((ROWS, HID), BF16),
        ((ROWS, HID), F32),
        ((BLOCKS + 1, HEADS, BLOCK, BLOCK), BF16),
        ((BLOCKS + 1, HEADS, BLOCK, BLOCK), F32),
        ((ROWS, D), F32),
        ((ROWS, D), F32),
        ((ROWS, D), BF16),
        ((ROWS, D), BF16),
        ((ROWS, 3 * D), F32),
        ((2, D, ROWS), BF16),
        ((ROWS, D), BF16),
        ((D, HID), BF16),
        ((D, D), BF16),
    ]
    return pl.pallas_call(
        layer_kernel,
        out_shape=(
            jax.ShapeDtypeStruct((ROWS, D), BF16),
            jax.ShapeDtypeStruct(SHARES, BF16),
            jax.ShapeDtypeStruct((2, HALF, ROWS), BF16),
            jax.ShapeDtypeStruct((ROWS, D), BF16),
            jax.ShapeDtypeStruct((ROWS, HID), BF16),
            jax.ShapeDtypeStruct((ROWS, D), BF16),
        ),
        in_specs=[full_spec(pltpu.SMEM)] * 4
        + [full_spec()]
        + [full_spec(pltpu.HBM)] * 3,
        out_specs=(full_spec(),) * 6,
        scratch_shapes=[pltpu.VMEM(shape, kind) for shape, kind in scratch]
        + [pltpu.SemaphoreType.DMA((3,))],
        compiler_params=pltpu.CompilerParams(vmem_limit_bytes=VMEM_LIMIT),
        cost_estimate=pl.CostEstimate(
            flops=4_000_000_000, bytes_accessed=9_000_000, transcendentals=1_500_000
        ),
        name="layer",
    )(core, offsets, lengths, rab, arrived, in_hbm(cotangent), in_hbm(w_in), in_hbm(w_out))


def total_kernel(received_ref, back_hbm, out_ref, sem):
    copy = pltpu.make_async_copy(back_hbm, out_ref.at[:, :, CHUNK:], sem)
    copy.start()
    total = received_ref[0].astype(F32)
    for m in range(1, MEMBERS):
        total += received_ref[m].astype(F32)
    total = (total * (1.0 / 256.0)).astype(BF16)
    out_ref[:, :, :CHUNK] = jnp.broadcast_to(total[None], (MEMBERS, PIECE, CHUNK))
    copy.wait()


def total(received, back):
    return pl.pallas_call(
        total_kernel,
        out_shape=jax.ShapeDtypeStruct((MEMBERS, PIECE, CHUNK + D), BF16),
        in_specs=[full_spec(), full_spec(pltpu.HBM)],
        out_specs=full_spec(),
        scratch_shapes=[pltpu.SemaphoreType.DMA],
        compiler_params=pltpu.CompilerParams(vmem_limit_bytes=VMEM_SMALL),
        cost_estimate=pl.CostEstimate(flops=1_000_000, bytes_accessed=4_000_000, transcendentals=0),
        name="total",
    )(received, in_hbm(back))


def put_shares(source, rows_s, groups):
    for side in range(4):
        at = side * CHUNK
        for g in groups:
            value = source[g, side, :, :CHUNK].astype(F32)
            rows_s[g * PIECE : (g + 1) * PIECE, at : at + CHUNK] = value


def put_rows(rows_s, half, w_in_hbm, w_out_hbm, sems, source):
    copies = []
    parts = 4
    height = HALF // parts
    for part in range(parts):
        put_shares(source, rows_s, range(part * height // PIECE, (part + 1) * height // PIECE))
        here = slice(part * height, (part + 1) * height)
        there = pl.ds(pl.multiple_of(half * HALF + part * height, height), height)
        for n, copy in enumerate(
            (
                (rows_s.at[here, :HID], w_in_hbm.at[there]),
                (rows_s.at[here, HID:], w_out_hbm.at[there]),
            )
        ):
            copies.append(pltpu.make_async_copy(*copy, sems.at[2 * part + n]))
            copies[-1].start()
    return copies


def mine_kernel(
    core_ref, route_ref, received_ref, events_hbm, w_in_hbm, w_out_hbm, rows_s, events_s, sems
):
    copies = put_rows(rows_s, core_ref[0], w_in_hbm, w_out_hbm, sems, received_ref)
    for j in range(PIECES):
        slot = lax.shift_right_logical(route_ref[j], 5)
        piece = received_ref[lax.shift_right_logical(slot, 2), lax.bitwise_and(slot, 3)]
        events_s[j * PIECE : (j + 1) * PIECE, :] = piece[:, CHUNK:]
    copies.append(pltpu.make_async_copy(events_s, events_hbm, sems.at[8]))
    copies[-1].start()
    for copy in copies:
        copy.wait()


def mine_out(core, route, received):
    return pl.pallas_call(
        mine_kernel,
        out_shape=(
            jax.ShapeDtypeStruct((ROWS, D), BF16),
            jax.ShapeDtypeStruct((D, HID), F32),
            jax.ShapeDtypeStruct((D, D), F32),
        ),
        in_specs=[full_spec(pltpu.SMEM)] * 2 + [full_spec()],
        out_specs=(full_spec(pltpu.HBM),) * 3,
        scratch_shapes=[
            pltpu.VMEM((HALF, HID + D), F32),
            pltpu.VMEM((ROWS, D), BF16),
            pltpu.SemaphoreType.DMA((9,)),
        ],
        compiler_params=pltpu.CompilerParams(vmem_limit_bytes=VMEM_SMALL),
        cost_estimate=pl.CostEstimate(flops=0, bytes_accessed=6_000_000, transcendentals=0),
        name="mine_out",
    )(core, route, received)


def theirs_kernel(core_ref, theirs_ref, _, __, w_in_hbm, w_out_hbm, rows_s, sems):
    for copy in put_rows(rows_s, 1 - core_ref[0], w_in_hbm, w_out_hbm, sems, theirs_ref):
        copy.wait()


def theirs_out(core, theirs, w_in_grad, w_out_grad):
    return pl.pallas_call(
        theirs_kernel,
        out_shape=(
            jax.ShapeDtypeStruct((D, HID), F32),
            jax.ShapeDtypeStruct((D, D), F32),
        ),
        in_specs=[full_spec(pltpu.SMEM), full_spec()] + [full_spec(pltpu.HBM)] * 2,
        out_specs=(full_spec(pltpu.HBM),) * 2,
        scratch_shapes=[
            pltpu.VMEM((HALF, HID + D), F32),
            pltpu.SemaphoreType.DMA((8,)),
        ],
        input_output_aliases={2: 0, 3: 1},
        compiler_params=pltpu.CompilerParams(vmem_limit_bytes=VMEM_SMALL),
        cost_estimate=pl.CostEstimate(flops=0, bytes_accessed=4_000_000, transcendentals=0),
        name="theirs_out",
    )(core, theirs, w_in_grad, w_out_grad)


def body(events, route, block_offset, hist_length, cotangent, w_in, w_out, rab):
    core = lax.axis_index("group").astype(jnp.int32).reshape(1)
    exchange = functools.partial(
        lax.all_to_all, axis_name="member", split_axis=0, concat_axis=0, tiled=True
    )
    swap = functools.partial(lax.ppermute, axis_name="group", perm=[(0, 1), (1, 0)])
    arrived = exchange(pack(route, events))
    outputs, other, left, up, gh, bal = layer(
        core, block_offset, hist_length, rab, arrived, cotangent, w_in, w_out
    )
    got = swap(other)
    joined = join(own_part(left, up, gh), got)
    received = exchange(joined.reshape(MEMBERS, PIECE, CHUNK))
    back = rest(arrived, up, gh, bal, w_in)
    received = exchange(total(received, back.reshape(MEMBERS, PIECE, D)))
    theirs = swap(received[:, :, :CHUNK])
    events_grad, w_in_grad, w_out_grad = mine_out(
        core, route, received.reshape(*SHARES[:3], CHUNK + D)
    )
    w_in_grad, w_out_grad = theirs_out(core, theirs.reshape(SHARES), w_in_grad, w_out_grad)
    return outputs, events_grad, w_in_grad, w_out_grad


def solution(mesh):
    placed = (
        P(("group", "member"), None),
        P(("group", "member")),
        P(("group", "member")),
        P(("group", "member")),
        P(("group", "member"), None),
        P(),
        P(),
        P(),
    )
    return jax.shard_map(
        body,
        mesh=mesh,
        in_specs=placed,
        out_specs=(P(("group", "member"), None), P(("group", "member"), None), P(), P()),
        check_vma=False,
    )
```

```python
import functools
import math

import jax
import jax.numpy as jnp
from jax import lax
from jax.experimental import pallas as pl
from jax.experimental.pallas import tpu as pltpu
from jax.sharding import PartitionSpec as P

EPS = 1e-05
BF16 = jnp.bfloat16
F32 = jnp.float32
VMEM_LIMIT = 32 * 1024 * 1024
VMEM_SMALL = 16 * 1024 * 1024
VMEM_MOST = 56 * 1024 * 1024

ROWS, D, HID = 512, 512, 2048
BLOCK, BLOCKS, HEADS, BUCKETS = 128, 4, 4, 12
PIECE, PIECES, MEMBERS = 16, 32, 64
SLOT = 72
CHUNK = 640
SCALE = 1.0 / math.sqrt(128)
HALF = D // 2
SHARES = (HALF // PIECE, 4, PIECE, CHUNK)


def dot(a, b):
    return jnp.dot(a, b, preferred_element_type=F32)


def dot_nt(a, b):
    return lax.dot_general(a, b, (((1,), (1,)), ((), ())), preferred_element_type=F32)


def dot_tn(a, b):
    return lax.dot_general(a, b, (((0,), (0,)), ((), ())), preferred_element_type=F32)


def sigmoid(v):
    return 0.5 * jnp.tanh(0.5 * v) + 0.5


def in_hbm(array):
    return pltpu.with_memory_space_constraint(array, pltpu.HBM)


def full_spec(memory=pltpu.VMEM):
    return pl.BlockSpec(memory_space=memory)


def pack_kernel(route_hbm, events_hbm, out_hbm, route_s, events_s, out_s, sems):
    half = ROWS // 2
    loads = [pltpu.make_async_copy(route_hbm, route_s, sems.at[0])]
    for n in range(2):
        rows = pl.ds(n * half, half)
        loads.append(
            pltpu.make_async_copy(events_hbm.at[rows], events_s.at[rows], sems.at[1 + n])
        )
    for load in loads:
        load.start()
    out_s[...] = jnp.zeros_like(out_s)
    for load in loads:
        load.wait()
    for j in range(PIECES):
        target = route_s[j]
        device = lax.shift_right_logical(target, 5)
        place = lax.bitwise_and(target, PIECES - 1)
        for k in range(D // 128):
            out_s[device, k * PIECE : (k + 1) * PIECE, :] = events_s[
                j * PIECE : (j + 1) * PIECE, k * 128 : (k + 1) * 128
            ]
        label = jnp.full((SLOT - 4 * PIECE, 128), (place + 1).astype(F32), F32)
        out_s[device, 4 * PIECE :, :] = label.astype(BF16)
    stores = []
    for n in range(4):
        part = pl.ds(n * (MEMBERS // 4), MEMBERS // 4)
        stores.append(pltpu.make_async_copy(out_s.at[part], out_hbm.at[part], sems.at[3 + n]))
        stores[-1].start()
    for store in stores:
        store.wait()


def pack(route, events):
    slots = (MEMBERS, SLOT, 128)
    return pl.pallas_call(
        pack_kernel,
        out_shape=pltpu.HBM(slots, BF16),
        in_specs=[full_spec(pltpu.HBM)] * 2,
        out_specs=full_spec(pltpu.HBM),
        scratch_shapes=[
            pltpu.SMEM((PIECES,), jnp.int32),
            pltpu.VMEM((ROWS, D), BF16),
            pltpu.VMEM(slots, BF16),
            pltpu.SemaphoreType.DMA((7,)),
        ],
        compiler_params=pltpu.CompilerParams(vmem_limit_bytes=VMEM_MOST),
        name="pack_pieces",
    )(in_hbm(route), in_hbm(events))


def cell_goals(arrived_ref):
    labels = arrived_ref[:, 4 * PIECE :, :].astype(F32)
    if labels.shape[1] < PIECE:
        labels = jnp.concatenate([labels, labels], axis=1)
    within = lax.broadcasted_iota(jnp.int32, labels.shape, 1).astype(F32)
    return ((labels - 1.0) * PIECE + within).reshape(MEMBERS * PIECE, 128)


def block_order(offset_ref):
    second = jnp.int32(1)
    for b in range(2, BLOCKS):
        second = jnp.where(offset_ref[b] == 1, b, second)
    return (
        second - 1,
        second,
        jnp.where(second == 1, 2, 0),
        jnp.where(second == 3, 1, 3),
    )


def block_rows(order, i):
    return pl.ds(pl.multiple_of(order[i] * BLOCK, BLOCK), BLOCK)


def inner_goals(goals, order):
    block = jnp.floor(goals * (1.0 / BLOCK))
    moved = goals
    for i in range(BLOCKS):
        at = order[i].astype(F32)
        moved = jnp.where(block == at, goals + (float(i) - at) * BLOCK, moved)
    return moved


def live_column(length_ref, order, i):
    first = BLOCK if i == 1 else 0
    return lax.broadcasted_iota(jnp.int32, (BLOCK, 1), 0) + first < length_ref[order[i]]


def normalized(x):
    centered = x - jnp.mean(x, axis=-1, keepdims=True)
    variance = jnp.mean(centered * centered, axis=-1, keepdims=True)
    rstd = lax.rsqrt(variance + EPS)
    return centered * rstd, rstd


def normalized_back(grad, hat, rstd):
    return rstd * (
        grad
        - jnp.mean(grad, axis=-1, keepdims=True)
        - hat * jnp.mean(grad * hat, axis=-1, keepdims=True)
    )


def head_cols(part, head):
    return slice(part * D + head * 128, part * D + head * 128 + 128)


def layer_kernel(
    offset_ref,
    length_ref,
    rab_ref,
    arrived_ref,
    cot_hbm,
    w_in_hbm,
    w_out_hbm,
    other_ref,
    left_ref,
    up_ref,
    gh_ref,
    bal_ref,
    mixed_ref,
    place_s,
    norm_s,
    hid_s,
    slope_s,
    long_att_s,
    long_ds_s,
    long_slope_s,
    short_att_s,
    short_slope_s,
    ctx_s,
    gm_s,
    gctx_s,
    trans_s,
    cot_ref,
    w_in_ref,
    w_out_ref,
    sems,
):
    copies = [
        pltpu.make_async_copy(w_in_hbm, w_in_ref, sems.at[0]),
        pltpu.make_async_copy(cot_hbm, cot_ref, sems.at[1]),
        pltpu.make_async_copy(w_out_hbm, w_out_ref, sems.at[2]),
    ]
    for copy in copies:
        copy.start()
    core = lax.axis_index("group")
    order = block_order(offset_ref)
    long_rows, short_rows = slice(0, 2 * BLOCK), slice(2 * BLOCK, 4 * BLOCK)

    tens = jnp.floor(cell_goals(arrived_ref) * (1.0 / PIECE)).astype(BF16)
    pick = (lax.broadcasted_iota(jnp.int32, (8, 128), 1) == 0).astype(BF16)
    ones = lax.bitwise_and(
        lax.broadcasted_iota(jnp.int32, (1, MEMBERS * PIECE), 1), PIECE - 1
    ).astype(F32)
    goal = inner_goals(dot_nt(pick, tens)[0:1, :] * PIECE + ones, order)

    def gather(rows):
        for r in range(rows.start, rows.stop, BLOCK):
            row = lax.broadcasted_iota(jnp.int32, (BLOCK, 1), 0).astype(F32) + float(r)
            place_s[r : r + BLOCK, :] = jnp.where(goal == row, 1.0, 0.0).astype(BF16)
        for k in range(0, D // 128, 2):
            cells = jnp.concatenate(
                [
                    arrived_ref[:, n * PIECE : (n + 1) * PIECE, :].reshape(MEMBERS * PIECE, 128)
                    for n in (k, k + 1)
                ],
                axis=1,
            )
            bal_ref[rows, k * 128 : k * 128 + 256] = dot(place_s[rows, :], cells).astype(BF16)

    def norm(r):
        sl = slice(r, r + 64)
        norm_s[sl, :] = normalized(bal_ref[sl, :].astype(F32))[0].astype(BF16)

    def project(rows, n):
        cols = slice(n, n + 256)
        v = dot(norm_s[rows, :], w_in_ref[:, cols])
        g = sigmoid(v)
        h = v * g
        hid_s[rows, cols] = h.astype(BF16)
        slope_s[rows, cols] = g + h * (1.0 - g)

    row_id = lax.broadcasted_iota(jnp.int32, (BLOCK, BLOCK), 0)
    col_id = lax.broadcasted_iota(jnp.int32, (BLOCK, BLOCK), 1)
    distance = row_id - col_id
    near_pairs = distance >= 0

    def bias(head, apart, buckets):
        total = jnp.full((BLOCK, BLOCK), rab_ref[head, 0], F32)
        for bucket in range(1, buckets):
            total = jnp.where(apart >= 2 ** (bucket - 1), rab_ref[head, bucket], total)
        return total

    def weigh(scores, relative, allowed):
        s = scores * SCALE + relative
        g = sigmoid(s)
        a = s * g
        return (
            jnp.where(allowed, a, 0.0).astype(BF16),
            jnp.where(allowed, g + a * (1.0 - g), 0.0),
        )

    def live_rows(i):
        return row_id + (BLOCK if i == 1 else 0) < length_ref[order[i]]

    allowed = [near_pairs & live_rows(i) for i in range(BLOCKS)] + [live_rows(1)]
    near = [None] * HEADS
    low, high = slice(0, BLOCK), slice(BLOCK, 2 * BLOCK)
    long_tiles = ((low, low, 0), (high, high, 1), (high, low, BLOCKS))

    def long_attend(head):
        near[head] = bias(head, distance, 8)
        far = bias(head, distance + BLOCK, 9)
        scores = dot_nt(hid_s[long_rows, head_cols(2, head)], hid_s[long_rows, head_cols(3, head)])
        long_att_s[head, low, high] = jnp.zeros((BLOCK, BLOCK), BF16)
        long_ds_s[head, low, high] = jnp.zeros((BLOCK, BLOCK), BF16)
        for tile, (i, j, pairs) in enumerate(long_tiles):
            a, slope = weigh(scores[i, j], far if tile == 2 else near[head], allowed[pairs])
            long_att_s[head, i, j] = a
            long_slope_s[head, tile] = slope
        ctx_s[long_rows, head_cols(0, head)] = dot(
            long_att_s[head], hid_s[long_rows, head_cols(1, head)]
        )

    def short_attend(head):
        for i in (2, 3):
            rows = slice(i * BLOCK, (i + 1) * BLOCK)
            scores = dot_nt(hid_s[rows, head_cols(2, head)], hid_s[rows, head_cols(3, head)])
            a, slope = weigh(scores, near[head], allowed[i])
            short_att_s[head, i - 2] = a
            short_slope_s[head, i - 2] = slope
            ctx_s[rows, head_cols(0, head)] = dot(a, hid_s[rows, head_cols(1, head)])

    def upstream(i):
        kept = jnp.where(
            live_column(length_ref, order, i), cot_ref[block_rows(order, i), :].astype(F32), 0.0
        )
        up_ref[i * BLOCK : (i + 1) * BLOCK, :] = kept.astype(BF16)

    def middle(r):
        sl = slice(r, r + 64)
        n, rstd = normalized(ctx_s[sl, :])
        u = hid_s[sl, 0:D].astype(F32)
        mixed_ref[sl, :] = (n * u).astype(BF16)
        gm = gm_s[sl, :]
        gh_ref[sl, 0:D] = (gm * n * slope_s[sl, 0:D]).astype(BF16)
        gctx_s[sl, :] = normalized_back(gm * u, n, rstd).astype(BF16)

    def finish_grads(rows, head, gv, gq, gk):
        for part, grad in ((1, gv), (2, gq * SCALE), (3, gk * SCALE)):
            cols = head_cols(part, head)
            gh_ref[rows, cols] = (grad * slope_s[rows, cols]).astype(BF16)

    def long_back(head):
        gc = gctx_s[long_rows, head_cols(0, head)]
        grads = dot_nt(gc, hid_s[long_rows, head_cols(1, head)])
        for tile, (i, j, _) in enumerate(long_tiles):
            long_ds_s[head, i, j] = (grads[i, j] * long_slope_s[head, tile]).astype(BF16)
        ds = long_ds_s[head]
        finish_grads(
            long_rows,
            head,
            dot_tn(long_att_s[head], gc),
            dot(ds, hid_s[long_rows, head_cols(3, head)]),
            dot_tn(ds, hid_s[long_rows, head_cols(2, head)]),
        )

    def short_back(head):
        for i in (2, 3):
            rows = slice(i * BLOCK, (i + 1) * BLOCK)
            gc = gctx_s[rows, head_cols(0, head)]
            grads = dot_nt(gc, hid_s[rows, head_cols(1, head)])
            ds = (grads * short_slope_s[head, i - 2]).astype(BF16)
            finish_grads(
                rows,
                head,
                dot_tn(short_att_s[head, i - 2], gc),
                dot(ds, hid_s[rows, head_cols(3, head)]),
                dot_tn(ds, hid_s[rows, head_cols(2, head)]),
            )

    parts = (1024, 1536, 1280, 1792, 512, 768, 0, 256)
    gather(long_rows)
    gather(short_rows)
    for r in range(0, 256, 64):
        norm(r)
    copies[0].wait()
    for k, n in enumerate(parts):
        project(long_rows, n)
        if k < 4:
            norm(256 + 64 * k)
    for copy in copies[1:]:
        copy.wait()
    for i in range(BLOCKS):
        upstream(i)
    gm_s[...] = dot_nt(up_ref[...], w_out_ref[...])
    for k, n in enumerate(parts):
        if k % 2 == 0:
            long_attend(k // 2)
        project(short_rows, n)
    for head in range(HEADS):
        middle(64 * head)
        short_attend(head)
    trans_s[0] = norm_s[...].T
    for head in range(HEADS):
        long_back(head)
        middle(256 + 64 * head)
    trans_s[1] = mixed_ref[...].T
    for head in range(HEADS):
        short_back(head)

    own_rows = pl.ds(pl.multiple_of(core * HALF, HALF), HALF)
    other_rows = pl.ds(pl.multiple_of((1 - core) * HALF, HALF), HALF)
    left_ref[0] = trans_s[0, own_rows, :]
    left_ref[1] = trans_s[1, own_rows, :]

    def store(at, value):
        other_ref[at] = value.astype(BF16)

    weight_grads(trans_s[0, other_rows, :], trans_s[1, other_rows, :], gh_ref, up_ref, store)


def weight_grads(normed_t, mixed_t, gh_ref, up_ref, store):
    for at in range(0, HID + D, 256):
        if at < HID:
            value = dot(normed_t, gh_ref[:, at : at + 256])
        else:
            value = dot(mixed_t, up_ref[:, at - HID : at - HID + 256])
        for n in (0, 128):
            side, start = (at + n) // CHUNK, (at + n) % CHUNK
            shares = value[:, n : n + 128].reshape(HALF // PIECE, PIECE, 128)
            store((slice(None), side, slice(None), slice(start, start + 128)), shares)


def own_kernel(left_ref, up_ref, gh_ref, out_ref):
    def store(at, value):
        out_ref[at] = value.astype(BF16)

    weight_grads(left_ref[0], left_ref[1], gh_ref, up_ref, store)


def own_part(left, up, gh):
    return pl.pallas_call(
        own_kernel,
        out_shape=jax.ShapeDtypeStruct(SHARES, BF16),
        in_specs=[full_spec()] * 3,
        out_specs=full_spec(),
        compiler_params=pltpu.CompilerParams(vmem_limit_bytes=VMEM_SMALL),
        cost_estimate=pl.CostEstimate(
            flops=700_000_000, bytes_accessed=6_000_000, transcendentals=0
        ),
        name="own_part",
    )(left, up, gh)


def join_kernel(own_ref, got_ref, out_hbm, out_s, sems):
    parts = 4
    step = SHARES[0] // parts
    copies = []
    for n in range(parts):
        part = pl.ds(n * step, step)
        out_s[part] = (own_ref[part].astype(F32) + got_ref[part].astype(F32)).astype(BF16)
        copies.append(pltpu.make_async_copy(out_s.at[part], out_hbm.at[part], sems.at[n]))
        copies[-1].start()
    for copy in copies:
        copy.wait()


def join(own, got):
    return pl.pallas_call(
        join_kernel,
        out_shape=pltpu.HBM(SHARES, BF16),
        in_specs=[full_spec()] * 2,
        out_specs=full_spec(pltpu.HBM),
        scratch_shapes=[pltpu.VMEM(SHARES, BF16), pltpu.SemaphoreType.DMA((4,))],
        compiler_params=pltpu.CompilerParams(vmem_limit_bytes=VMEM_SMALL),
        cost_estimate=pl.CostEstimate(flops=1_000_000, bytes_accessed=4_000_000, transcendentals=0),
        name="join",
    )(own, got)


def rest_kernel(offset_ref, length_ref, *refs):
    hbm, (out_hbm, back_hbm) = refs[:7], refs[7:9]
    here, (out_ref, back_ref, gx_s, gb_s, place_s, sems) = refs[9:16], refs[16:]
    loads = [pltpu.make_async_copy(hbm[n], here[n], sems.at[n]) for n in range(7)]
    for load in loads:
        load.start()
    gh_ref, w_in_ref, bal_ref, up_ref, arrived_ref, mixed_ref, w_out_ref = here
    order = block_order(offset_ref)
    loads[0].wait()
    loads[1].wait()
    gx_s[...] = dot_nt(gh_ref[...], w_in_ref[...])
    loads[2].wait()
    loads[3].wait()
    for r in range(0, ROWS, 64):
        sl = slice(r, r + 64)
        hat, rstd = normalized(bal_ref[sl, :].astype(F32))
        grad = normalized_back(gx_s[sl, :], hat, rstd)
        gb_s[sl, :] = (up_ref[sl, :].astype(F32) + grad).astype(BF16)
    loads[4].wait()
    goals = inner_goals(cell_goals(arrived_ref), order)
    for b in range(BLOCKS):
        row = lax.broadcasted_iota(jnp.int32, (1, BLOCK), 1).astype(F32) + float(b * BLOCK)
        place_s[:, b * BLOCK : (b + 1) * BLOCK] = jnp.where(goals == row, 1.0, 0.0).astype(BF16)
    for n in range(0, D, 256):
        back_ref[:, n : n + 256] = dot(place_s[...], gb_s[:, n : n + 256]).astype(BF16)
    stores = [pltpu.make_async_copy(back_ref, back_hbm, sems.at[7])]
    stores[0].start()
    loads[5].wait()
    loads[6].wait()
    gx_s[...] = dot(mixed_ref[...], w_out_ref[...])
    for i in range(BLOCKS):
        rows = slice(i * BLOCK, (i + 1) * BLOCK)
        value = bal_ref[rows, :].astype(F32) + gx_s[rows, :]
        value = jnp.where(live_column(length_ref, order, i), value, 0.0)
        out_ref[block_rows(order, i), :] = value.astype(BF16)
    stores.append(pltpu.make_async_copy(out_ref, out_hbm, sems.at[8]))
    stores[1].start()
    for store in stores:
        store.wait()


def rest(offsets, lengths, gh, w_in, bal, up, arrived, mixed, w_out):
    operands = (gh, w_in, bal, up, arrived, mixed, w_out)
    rows, cells = (ROWS, D), (MEMBERS * PIECE, D)
    return pl.pallas_call(
        rest_kernel,
        out_shape=(pltpu.HBM(rows, BF16), pltpu.HBM(cells, BF16)),
        in_specs=[full_spec(pltpu.SMEM)] * 2 + [full_spec(pltpu.HBM)] * 7,
        out_specs=(full_spec(pltpu.HBM),) * 2,
        scratch_shapes=[pltpu.VMEM(x.shape, BF16) for x in operands]
        + [
            pltpu.VMEM(rows, BF16),
            pltpu.VMEM(cells, BF16),
            pltpu.VMEM(rows, F32),
            pltpu.VMEM(rows, BF16),
            pltpu.VMEM((MEMBERS * PIECE, ROWS), BF16),
            pltpu.SemaphoreType.DMA((9,)),
        ],
        compiler_params=pltpu.CompilerParams(vmem_limit_bytes=VMEM_SMALL),
        cost_estimate=pl.CostEstimate(
            flops=2_500_000_000, bytes_accessed=9_000_000, transcendentals=1_000
        ),
        name="rest",
    )(offsets, lengths, *map(in_hbm, operands))


def layer(offsets, lengths, rab, arrived, cotangent, w_in, w_out):
    scratch = [
        ((ROWS, MEMBERS * PIECE), BF16),
        ((ROWS, D), BF16),
        ((ROWS, HID), BF16),
        ((ROWS, HID), F32),
        ((HEADS, 2 * BLOCK, 2 * BLOCK), BF16),
        ((HEADS, 2 * BLOCK, 2 * BLOCK), BF16),
        ((HEADS, 3, BLOCK, BLOCK), F32),
        ((HEADS, 2, BLOCK, BLOCK), BF16),
        ((HEADS, 2, BLOCK, BLOCK), F32),
        ((ROWS, D), F32),
        ((ROWS, D), F32),
        ((ROWS, D), BF16),
        ((2, D, ROWS), BF16),
        ((ROWS, D), BF16),
        ((D, HID), BF16),
        ((D, D), BF16),
    ]
    rows = jax.ShapeDtypeStruct((ROWS, D), BF16)
    return pl.pallas_call(
        layer_kernel,
        out_shape=(
            jax.ShapeDtypeStruct(SHARES, BF16),
            jax.ShapeDtypeStruct((2, HALF, ROWS), BF16),
            rows,
            jax.ShapeDtypeStruct((ROWS, HID), BF16),
            rows,
            rows,
        ),
        in_specs=[full_spec(pltpu.SMEM)] * 3 + [full_spec()] + [full_spec(pltpu.HBM)] * 3,
        out_specs=(full_spec(),) * 6,
        scratch_shapes=[pltpu.VMEM(shape, kind) for shape, kind in scratch]
        + [pltpu.SemaphoreType.DMA((3,))],
        compiler_params=pltpu.CompilerParams(vmem_limit_bytes=VMEM_LIMIT),
        cost_estimate=pl.CostEstimate(
            flops=4_000_000_000, bytes_accessed=9_000_000, transcendentals=1_500_000
        ),
        name="layer",
    )(offsets, lengths, rab, arrived, *map(in_hbm, (cotangent, w_in, w_out)))


def total_kernel(received_ref, back_hbm, out_ref, sems):
    parts = 4
    step = MEMBERS // parts
    copies = []
    for n in range(parts):
        part = pl.ds(n * step, step)
        copies.append(
            pltpu.make_async_copy(back_hbm.at[part], out_ref.at[part, :, CHUNK:], sems.at[n])
        )
        copies[-1].start()
    total = received_ref[0].astype(F32)
    for m in range(1, MEMBERS):
        total += received_ref[m].astype(F32)
    total = (total * (1.0 / 256.0)).astype(BF16)
    out_ref[:, :, :CHUNK] = jnp.broadcast_to(total[None], (MEMBERS, PIECE, CHUNK))
    for copy in copies:
        copy.wait()


def total(received, back):
    return pl.pallas_call(
        total_kernel,
        out_shape=jax.ShapeDtypeStruct((MEMBERS, PIECE, CHUNK + D), BF16),
        in_specs=[full_spec(), full_spec(pltpu.HBM)],
        out_specs=full_spec(),
        scratch_shapes=[pltpu.SemaphoreType.DMA((4,))],
        compiler_params=pltpu.CompilerParams(vmem_limit_bytes=VMEM_SMALL),
        cost_estimate=pl.CostEstimate(flops=1_000_000, bytes_accessed=4_000_000, transcendentals=0),
        name="total",
    )(received, in_hbm(back))


def put_shares(source, rows_s, groups):
    for side in range(4):
        at = side * CHUNK
        for g in groups:
            value = source[g, side, :, :CHUNK].astype(F32)
            rows_s[g * PIECE : (g + 1) * PIECE, at : at + CHUNK] = value


def put_rows(rows_s, half, w_in_hbm, w_out_hbm, sems, source):
    copies = []
    parts = 4
    height = HALF // parts
    for part in range(parts):
        put_shares(source, rows_s, range(part * height // PIECE, (part + 1) * height // PIECE))
        here = slice(part * height, (part + 1) * height)
        there = pl.ds(pl.multiple_of(half * HALF + part * height, height), height)
        for n, copy in enumerate(
            (
                (rows_s.at[here, :HID], w_in_hbm.at[there]),
                (rows_s.at[here, HID:], w_out_hbm.at[there]),
            )
        ):
            copies.append(pltpu.make_async_copy(*copy, sems.at[2 * part + n]))
            copies[-1].start()
    return copies


def mine_kernel(
    route_ref, received_ref, events_hbm, w_in_hbm, w_out_hbm, rows_s, events_s, sems
):
    copies = put_rows(rows_s, lax.axis_index("group"), w_in_hbm, w_out_hbm, sems, received_ref)
    for j in range(PIECES):
        slot = lax.shift_right_logical(route_ref[j], 5)
        piece = received_ref[lax.shift_right_logical(slot, 2), lax.bitwise_and(slot, 3)]
        events_s[j * PIECE : (j + 1) * PIECE, :] = piece[:, CHUNK:]
    copies.append(pltpu.make_async_copy(events_s, events_hbm, sems.at[8]))
    copies[-1].start()
    for copy in copies:
        copy.wait()


def mine_out(route, received):
    return pl.pallas_call(
        mine_kernel,
        out_shape=(
            jax.ShapeDtypeStruct((ROWS, D), BF16),
            jax.ShapeDtypeStruct((D, HID), F32),
            jax.ShapeDtypeStruct((D, D), F32),
        ),
        in_specs=[full_spec(pltpu.SMEM), full_spec()],
        out_specs=(full_spec(pltpu.HBM),) * 3,
        scratch_shapes=[
            pltpu.VMEM((HALF, HID + D), F32),
            pltpu.VMEM((ROWS, D), BF16),
            pltpu.SemaphoreType.DMA((9,)),
        ],
        compiler_params=pltpu.CompilerParams(vmem_limit_bytes=VMEM_SMALL),
        cost_estimate=pl.CostEstimate(flops=0, bytes_accessed=6_000_000, transcendentals=0),
        name="mine_out",
    )(route, received)


def theirs_kernel(theirs_ref, _, __, w_in_hbm, w_out_hbm, rows_s, sems):
    for copy in put_rows(rows_s, 1 - lax.axis_index("group"), w_in_hbm, w_out_hbm, sems, theirs_ref):
        copy.wait()


def theirs_out(theirs, w_in_grad, w_out_grad):
    return pl.pallas_call(
        theirs_kernel,
        out_shape=(
            jax.ShapeDtypeStruct((D, HID), F32),
            jax.ShapeDtypeStruct((D, D), F32),
        ),
        in_specs=[full_spec()] + [full_spec(pltpu.HBM)] * 2,
        out_specs=(full_spec(pltpu.HBM),) * 2,
        scratch_shapes=[
            pltpu.VMEM((HALF, HID + D), F32),
            pltpu.SemaphoreType.DMA((8,)),
        ],
        input_output_aliases={1: 0, 2: 1},
        compiler_params=pltpu.CompilerParams(vmem_limit_bytes=VMEM_SMALL),
        cost_estimate=pl.CostEstimate(flops=0, bytes_accessed=4_000_000, transcendentals=0),
        name="theirs_out",
    )(theirs, w_in_grad, w_out_grad)


def body(events, route, block_offset, hist_length, cotangent, w_in, w_out, rab):
    exchange = functools.partial(
        lax.all_to_all, axis_name="member", split_axis=0, concat_axis=0, tiled=True
    )
    swap = functools.partial(lax.ppermute, axis_name="group", perm=[(0, 1), (1, 0)])
    arrived = exchange(pack(route, events))
    other, left, up, gh, bal, mixed = layer(
        block_offset, hist_length, rab, arrived, cotangent, w_in, w_out
    )
    got = swap(other)
    joined = join(own_part(left, up, gh), got)
    received = exchange(joined.reshape(MEMBERS, PIECE, CHUNK))
    outputs, back = rest(block_offset, hist_length, gh, w_in, bal, up, arrived, mixed, w_out)
    received = exchange(total(received, back.reshape(MEMBERS, PIECE, D)))
    theirs = swap(received[:, :, :CHUNK])
    events_grad, w_in_grad, w_out_grad = mine_out(
        route, received.reshape(*SHARES[:3], CHUNK + D)
    )
    w_in_grad, w_out_grad = theirs_out(theirs.reshape(SHARES), w_in_grad, w_out_grad)
    return outputs, events_grad, w_in_grad, w_out_grad


def solution(mesh):
    placed = (
        P(("group", "member"), None),
        P(("group", "member")),
        P(("group", "member")),
        P(("group", "member")),
        P(("group", "member"), None),
        P(),
        P(),
        P(),
    )
    return jax.shard_map(
        body,
        mesh=mesh,
        in_specs=placed,
        out_specs=(P(("group", "member"), None), P(("group", "member"), None), P(), P()),
        check_vma=False,
    )
```

```python
import functools
import math

import jax
import jax.numpy as jnp
from jax import lax
from jax.experimental import pallas as pl
from jax.experimental.pallas import tpu as pltpu
from jax.sharding import PartitionSpec as P

EPS = 1e-05
BF16 = jnp.bfloat16
F32 = jnp.float32
VMEM_LIMIT = 32 * 1024 * 1024
VMEM_SMALL = 16 * 1024 * 1024

ROWS, D, HID = 512, 512, 2048
BLOCK, BLOCKS, HEADS, BUCKETS = 128, 4, 4, 12
PIECE, PIECES, MEMBERS = 16, 32, 64
SLOT = 72
CHUNK = 640
SCALE = 1.0 / math.sqrt(128)
HALF = D // 2
SHARES = (HALF // PIECE, 4, PIECE, CHUNK)


def dot(a, b):
    return jnp.dot(a, b, preferred_element_type=F32)


def dot_nt(a, b):
    return lax.dot_general(a, b, (((1,), (1,)), ((), ())), preferred_element_type=F32)


def dot_tn(a, b):
    return lax.dot_general(a, b, (((0,), (0,)), ((), ())), preferred_element_type=F32)


def sigmoid(v):
    return 0.5 * jnp.tanh(0.5 * v) + 0.5


def in_hbm(array):
    return pltpu.with_memory_space_constraint(array, pltpu.HBM)


def full_spec(memory=pltpu.VMEM):
    return pl.BlockSpec(memory_space=memory)


def pack_kernel(route_hbm, events_hbm, out_ref, route_s, events_s, sems):
    half = ROWS // 2
    loads = [pltpu.make_async_copy(route_hbm, route_s, sems.at[0])]
    for n in range(2):
        rows = pl.ds(n * half, half)
        loads.append(
            pltpu.make_async_copy(events_hbm.at[rows], events_s.at[rows], sems.at[1 + n])
        )
    for load in loads:
        load.start()
    out_ref[...] = jnp.zeros_like(out_ref)
    for load in loads:
        load.wait()
    for j in range(PIECES):
        target = route_s[j]
        device = lax.shift_right_logical(target, 5)
        place = lax.bitwise_and(target, PIECES - 1)
        for k in range(D // 128):
            out_ref[device, k * PIECE : (k + 1) * PIECE, :] = events_s[
                j * PIECE : (j + 1) * PIECE, k * 128 : (k + 1) * 128
            ]
        label = jnp.full((SLOT - 4 * PIECE, 128), (place + 1).astype(F32), F32)
        out_ref[device, 4 * PIECE :, :] = label.astype(BF16)


def pack(route, events):
    return pl.pallas_call(
        pack_kernel,
        out_shape=jax.ShapeDtypeStruct((MEMBERS, SLOT, 128), BF16),
        in_specs=[full_spec(pltpu.HBM)] * 2,
        out_specs=full_spec(),
        scratch_shapes=[
            pltpu.SMEM((PIECES,), jnp.int32),
            pltpu.VMEM((ROWS, D), BF16),
            pltpu.SemaphoreType.DMA((3,)),
        ],
        compiler_params=pltpu.CompilerParams(vmem_limit_bytes=VMEM_SMALL),
        name="pack_pieces",
    )(in_hbm(route), in_hbm(events))


def cell_goals(arrived_ref):
    labels = arrived_ref[:, 4 * PIECE :, :].astype(F32)
    if labels.shape[1] < PIECE:
        labels = jnp.concatenate([labels, labels], axis=1)
    within = lax.broadcasted_iota(jnp.int32, labels.shape, 1).astype(F32)
    return ((labels - 1.0) * PIECE + within).reshape(MEMBERS * PIECE, 128)


def block_order(offset_ref):
    second = jnp.int32(1)
    for b in range(2, BLOCKS):
        second = jnp.where(offset_ref[b] == 1, b, second)
    return (
        second - 1,
        second,
        jnp.where(second == 1, 2, 0),
        jnp.where(second == 3, 1, 3),
    )


def block_rows(order, i):
    return pl.ds(pl.multiple_of(order[i] * BLOCK, BLOCK), BLOCK)


def inner_goals(goals, order):
    block = jnp.floor(goals * (1.0 / BLOCK))
    moved = goals
    for i in range(BLOCKS):
        at = order[i].astype(F32)
        moved = jnp.where(block == at, goals + (float(i) - at) * BLOCK, moved)
    return moved


def live_column(length_ref, order, i):
    first = BLOCK if i == 1 else 0
    return lax.broadcasted_iota(jnp.int32, (BLOCK, 1), 0) + first < length_ref[order[i]]


def normalized(x):
    centered = x - jnp.mean(x, axis=-1, keepdims=True)
    variance = jnp.mean(centered * centered, axis=-1, keepdims=True)
    rstd = lax.rsqrt(variance + EPS)
    return centered * rstd, rstd


def normalized_back(grad, hat, rstd):
    return rstd * (
        grad
        - jnp.mean(grad, axis=-1, keepdims=True)
        - hat * jnp.mean(grad * hat, axis=-1, keepdims=True)
    )


def head_cols(part, head):
    return slice(part * D + head * 128, part * D + head * 128 + 128)


def layer_kernel(
    offset_ref,
    length_ref,
    rab_ref,
    arrived_ref,
    cot_hbm,
    w_in_hbm,
    w_out_hbm,
    other_ref,
    left_ref,
    up_ref,
    gh_ref,
    bal_ref,
    mixed_ref,
    place_s,
    norm_s,
    hid_s,
    slope_s,
    long_att_s,
    long_ds_s,
    long_slope_s,
    short_att_s,
    short_slope_s,
    ctx_s,
    gm_s,
    gctx_s,
    trans_s,
    cot_ref,
    w_in_ref,
    w_out_ref,
    sems,
):
    copies = []
    for n, start in enumerate((1024, 1536, 512, 0)):
        cols = pl.ds(start, D)
        copies.append(
            pltpu.make_async_copy(w_in_hbm.at[:, cols], w_in_ref.at[:, cols], sems.at[n])
        )
    copies.append(pltpu.make_async_copy(cot_hbm, cot_ref, sems.at[4]))
    copies.append(pltpu.make_async_copy(w_out_hbm, w_out_ref, sems.at[5]))
    for copy in copies:
        copy.start()
    core = lax.axis_index("group")
    order = block_order(offset_ref)
    long_rows, short_rows = slice(0, 2 * BLOCK), slice(2 * BLOCK, 4 * BLOCK)

    tens = jnp.floor(cell_goals(arrived_ref) * (1.0 / PIECE)).astype(BF16)
    pick = (lax.broadcasted_iota(jnp.int32, (8, 128), 1) == 0).astype(BF16)
    ones = lax.bitwise_and(
        lax.broadcasted_iota(jnp.int32, (1, MEMBERS * PIECE), 1), PIECE - 1
    ).astype(F32)
    goal = inner_goals(dot_nt(pick, tens)[0:1, :] * PIECE + ones, order)

    def gather(rows):
        for r in range(rows.start, rows.stop, BLOCK):
            row = lax.broadcasted_iota(jnp.int32, (BLOCK, 1), 0).astype(F32) + float(r)
            place_s[r : r + BLOCK, :] = jnp.where(goal == row, 1.0, 0.0).astype(BF16)
        for k in range(0, D // 128, 2):
            cells = jnp.concatenate(
                [
                    arrived_ref[:, n * PIECE : (n + 1) * PIECE, :].reshape(MEMBERS * PIECE, 128)
                    for n in (k, k + 1)
                ],
                axis=1,
            )
            bal_ref[rows, k * 128 : k * 128 + 256] = dot(place_s[rows, :], cells).astype(BF16)

    def norm(r):
        sl = slice(r, r + 64)
        norm_s[sl, :] = normalized(bal_ref[sl, :].astype(F32))[0].astype(BF16)

    def project(rows, n):
        cols = slice(n, n + 256)
        v = dot(norm_s[rows, :], w_in_ref[:, cols])
        g = sigmoid(v)
        h = v * g
        hid_s[rows, cols] = h.astype(BF16)
        slope_s[rows, cols] = g + h * (1.0 - g)

    row_id = lax.broadcasted_iota(jnp.int32, (BLOCK, BLOCK), 0)
    col_id = lax.broadcasted_iota(jnp.int32, (BLOCK, BLOCK), 1)
    distance = row_id - col_id
    near_pairs = distance >= 0

    def bias(head, apart, buckets):
        total = jnp.full((BLOCK, BLOCK), rab_ref[head, 0], F32)
        for bucket in range(1, buckets):
            total = jnp.where(apart >= 2 ** (bucket - 1), rab_ref[head, bucket], total)
        return total

    def weigh(scores, relative, allowed):
        s = scores * SCALE + relative
        g = sigmoid(s)
        a = s * g
        return (
            jnp.where(allowed, a, 0.0).astype(BF16),
            jnp.where(allowed, g + a * (1.0 - g), 0.0),
        )

    def live_rows(i):
        return row_id + (BLOCK if i == 1 else 0) < length_ref[order[i]]

    allowed = [near_pairs & live_rows(i) for i in range(BLOCKS)] + [live_rows(1)]
    near = [None] * HEADS
    low, high = slice(0, BLOCK), slice(BLOCK, 2 * BLOCK)
    long_tiles = ((low, low, 0), (high, high, 1), (high, low, BLOCKS))

    def long_attend(head):
        near[head] = bias(head, distance, 8)
        far = bias(head, distance + BLOCK, 9)
        scores = dot_nt(hid_s[long_rows, head_cols(2, head)], hid_s[long_rows, head_cols(3, head)])
        long_att_s[head, low, high] = jnp.zeros((BLOCK, BLOCK), BF16)
        long_ds_s[head, low, high] = jnp.zeros((BLOCK, BLOCK), BF16)
        for tile, (i, j, pairs) in enumerate(long_tiles):
            a, slope = weigh(scores[i, j], far if tile == 2 else near[head], allowed[pairs])
            long_att_s[head, i, j] = a
            long_slope_s[head, tile] = slope
        ctx_s[long_rows, head_cols(0, head)] = dot(
            long_att_s[head], hid_s[long_rows, head_cols(1, head)]
        )

    def short_attend(head):
        for i in (2, 3):
            rows = slice(i * BLOCK, (i + 1) * BLOCK)
            scores = dot_nt(hid_s[rows, head_cols(2, head)], hid_s[rows, head_cols(3, head)])
            a, slope = weigh(scores, near[head], allowed[i])
            short_att_s[head, i - 2] = a
            short_slope_s[head, i - 2] = slope
            ctx_s[rows, head_cols(0, head)] = dot(a, hid_s[rows, head_cols(1, head)])

    def upstream(i):
        kept = jnp.where(
            live_column(length_ref, order, i), cot_ref[block_rows(order, i), :].astype(F32), 0.0
        )
        up_ref[i * BLOCK : (i + 1) * BLOCK, :] = kept.astype(BF16)

    def middle(r):
        sl = slice(r, r + 64)
        n, rstd = normalized(ctx_s[sl, :])
        u = hid_s[sl, 0:D].astype(F32)
        mixed_ref[sl, :] = (n * u).astype(BF16)
        gm = gm_s[sl, :]
        gh_ref[sl, 0:D] = (gm * n * slope_s[sl, 0:D]).astype(BF16)
        gctx_s[sl, :] = normalized_back(gm * u, n, rstd).astype(BF16)

    def finish_grads(rows, head, gv, gq, gk):
        for part, grad in ((1, gv), (2, gq * SCALE), (3, gk * SCALE)):
            cols = head_cols(part, head)
            gh_ref[rows, cols] = (grad * slope_s[rows, cols]).astype(BF16)

    def long_back(head):
        gc = gctx_s[long_rows, head_cols(0, head)]
        grads = dot_nt(gc, hid_s[long_rows, head_cols(1, head)])
        for tile, (i, j, _) in enumerate(long_tiles):
            long_ds_s[head, i, j] = (grads[i, j] * long_slope_s[head, tile]).astype(BF16)
        ds = long_ds_s[head]
        finish_grads(
            long_rows,
            head,
            dot_tn(long_att_s[head], gc),
            dot(ds, hid_s[long_rows, head_cols(3, head)]),
            dot_tn(ds, hid_s[long_rows, head_cols(2, head)]),
        )

    def short_back(head):
        for i in (2, 3):
            rows = slice(i * BLOCK, (i + 1) * BLOCK)
            gc = gctx_s[rows, head_cols(0, head)]
            grads = dot_nt(gc, hid_s[rows, head_cols(1, head)])
            ds = (grads * short_slope_s[head, i - 2]).astype(BF16)
            finish_grads(
                rows,
                head,
                dot_tn(short_att_s[head, i - 2], gc),
                dot(ds, hid_s[rows, head_cols(3, head)]),
                dot_tn(ds, hid_s[rows, head_cols(2, head)]),
            )

    parts = (1024, 1536, 1280, 1792, 512, 768, 0, 256)
    gather(long_rows)
    gather(short_rows)
    for r in range(0, 256, 64):
        norm(r)
    for k, n in enumerate(parts):
        if k in (0, 1, 4, 6):
            copies[(0, 1, 4, 6).index(k)].wait()
        project(long_rows, n)
        if k < 4:
            norm(256 + 64 * k)
    for copy in copies[4:]:
        copy.wait()
    for i in range(BLOCKS):
        upstream(i)
    gm_s[...] = dot_nt(up_ref[...], w_out_ref[...])
    for k, n in enumerate(parts):
        if k % 2 == 0:
            long_attend(k // 2)
        project(short_rows, n)
    for head in range(HEADS):
        middle(64 * head)
        short_attend(head)
    trans_s[0] = norm_s[...].T
    for head in range(HEADS):
        long_back(head)
        middle(256 + 64 * head)
    trans_s[1] = mixed_ref[...].T
    for head in range(HEADS):
        short_back(head)

    own_rows = pl.ds(pl.multiple_of(core * HALF, HALF), HALF)
    other_rows = pl.ds(pl.multiple_of((1 - core) * HALF, HALF), HALF)
    left_ref[0] = trans_s[0, own_rows, :]
    left_ref[1] = trans_s[1, own_rows, :]

    def store(at, value):
        other_ref[at] = value.astype(BF16)

    weight_grads(trans_s[0, other_rows, :], trans_s[1, other_rows, :], gh_ref, up_ref, store)


def weight_grads(normed_t, mixed_t, gh_ref, up_ref, store):
    for at in range(0, HID + D, 256):
        if at < HID:
            value = dot(normed_t, gh_ref[:, at : at + 256])
        else:
            value = dot(mixed_t, up_ref[:, at - HID : at - HID + 256])
        for n in (0, 128):
            side, start = (at + n) // CHUNK, (at + n) % CHUNK
            shares = value[:, n : n + 128].reshape(HALF // PIECE, PIECE, 128)
            store((slice(None), side, slice(None), slice(start, start + 128)), shares)


def own_kernel(left_ref, up_ref, gh_ref, out_ref):
    def store(at, value):
        out_ref[at] = value.astype(BF16)

    weight_grads(left_ref[0], left_ref[1], gh_ref, up_ref, store)


def own_part(left, up, gh):
    return pl.pallas_call(
        own_kernel,
        out_shape=jax.ShapeDtypeStruct(SHARES, BF16),
        in_specs=[full_spec()] * 3,
        out_specs=full_spec(),
        compiler_params=pltpu.CompilerParams(vmem_limit_bytes=VMEM_SMALL),
        cost_estimate=pl.CostEstimate(
            flops=700_000_000, bytes_accessed=6_000_000, transcendentals=0
        ),
        name="own_part",
    )(left, up, gh)


def join_kernel(own_ref, got_ref, out_hbm, out_s, sems):
    parts = 4
    step = SHARES[0] // parts
    copies = []
    for n in range(parts):
        part = pl.ds(n * step, step)
        out_s[part] = (own_ref[part].astype(F32) + got_ref[part].astype(F32)).astype(BF16)
        copies.append(pltpu.make_async_copy(out_s.at[part], out_hbm.at[part], sems.at[n]))
        copies[-1].start()
    for copy in copies:
        copy.wait()


def join(own, got):
    return pl.pallas_call(
        join_kernel,
        out_shape=pltpu.HBM(SHARES, BF16),
        in_specs=[full_spec()] * 2,
        out_specs=full_spec(pltpu.HBM),
        scratch_shapes=[pltpu.VMEM(SHARES, BF16), pltpu.SemaphoreType.DMA((4,))],
        compiler_params=pltpu.CompilerParams(vmem_limit_bytes=VMEM_SMALL),
        cost_estimate=pl.CostEstimate(flops=1_000_000, bytes_accessed=4_000_000, transcendentals=0),
        name="join",
    )(own, got)


def rest_kernel(offset_ref, length_ref, *refs):
    hbm, (out_hbm, back_hbm) = refs[:7], refs[7:9]
    here, (out_ref, back_ref, gx_s, gb_s, place_s, sems) = refs[9:16], refs[16:]
    loads = [pltpu.make_async_copy(hbm[n], here[n], sems.at[n]) for n in range(7)]
    for load in loads:
        load.start()
    gh_ref, w_in_ref, bal_ref, up_ref, arrived_ref, mixed_ref, w_out_ref = here
    order = block_order(offset_ref)
    loads[0].wait()
    loads[1].wait()
    gx_s[...] = dot_nt(gh_ref[...], w_in_ref[...])
    loads[2].wait()
    loads[3].wait()
    for r in range(0, ROWS, 64):
        sl = slice(r, r + 64)
        hat, rstd = normalized(bal_ref[sl, :].astype(F32))
        grad = normalized_back(gx_s[sl, :], hat, rstd)
        gb_s[sl, :] = (up_ref[sl, :].astype(F32) + grad).astype(BF16)
    loads[4].wait()
    goals = inner_goals(cell_goals(arrived_ref), order)
    for b in range(BLOCKS):
        row = lax.broadcasted_iota(jnp.int32, (1, BLOCK), 1).astype(F32) + float(b * BLOCK)
        place_s[:, b * BLOCK : (b + 1) * BLOCK] = jnp.where(goals == row, 1.0, 0.0).astype(BF16)
    for n in range(0, D, 256):
        back_ref[:, n : n + 256] = dot(place_s[...], gb_s[:, n : n + 256]).astype(BF16)
    stores = [pltpu.make_async_copy(back_ref, back_hbm, sems.at[7])]
    stores[0].start()
    loads[5].wait()
    loads[6].wait()
    gx_s[...] = dot(mixed_ref[...], w_out_ref[...])
    for i in range(BLOCKS):
        rows = slice(i * BLOCK, (i + 1) * BLOCK)
        value = bal_ref[rows, :].astype(F32) + gx_s[rows, :]
        value = jnp.where(live_column(length_ref, order, i), value, 0.0)
        out_ref[block_rows(order, i), :] = value.astype(BF16)
    stores.append(pltpu.make_async_copy(out_ref, out_hbm, sems.at[8]))
    stores[1].start()
    for store in stores:
        store.wait()


def rest(offsets, lengths, gh, w_in, bal, up, arrived, mixed, w_out):
    operands = (gh, w_in, bal, up, arrived, mixed, w_out)
    rows, cells = (ROWS, D), (MEMBERS * PIECE, D)
    return pl.pallas_call(
        rest_kernel,
        out_shape=(pltpu.HBM(rows, BF16), pltpu.HBM(cells, BF16)),
        in_specs=[full_spec(pltpu.SMEM)] * 2 + [full_spec(pltpu.HBM)] * 7,
        out_specs=(full_spec(pltpu.HBM),) * 2,
        scratch_shapes=[pltpu.VMEM(x.shape, BF16) for x in operands]
        + [
            pltpu.VMEM(rows, BF16),
            pltpu.VMEM(cells, BF16),
            pltpu.VMEM(rows, F32),
            pltpu.VMEM(rows, BF16),
            pltpu.VMEM((MEMBERS * PIECE, ROWS), BF16),
            pltpu.SemaphoreType.DMA((9,)),
        ],
        compiler_params=pltpu.CompilerParams(vmem_limit_bytes=VMEM_SMALL),
        cost_estimate=pl.CostEstimate(
            flops=2_500_000_000, bytes_accessed=9_000_000, transcendentals=1_000
        ),
        name="rest",
    )(offsets, lengths, *map(in_hbm, operands))


def layer(offsets, lengths, rab, arrived, cotangent, w_in, w_out):
    scratch = [
        ((ROWS, MEMBERS * PIECE), BF16),
        ((ROWS, D), BF16),
        ((ROWS, HID), BF16),
        ((ROWS, HID), F32),
        ((HEADS, 2 * BLOCK, 2 * BLOCK), BF16),
        ((HEADS, 2 * BLOCK, 2 * BLOCK), BF16),
        ((HEADS, 3, BLOCK, BLOCK), F32),
        ((HEADS, 2, BLOCK, BLOCK), BF16),
        ((HEADS, 2, BLOCK, BLOCK), F32),
        ((ROWS, D), F32),
        ((ROWS, D), F32),
        ((ROWS, D), BF16),
        ((2, D, ROWS), BF16),
        ((ROWS, D), BF16),
        ((D, HID), BF16),
        ((D, D), BF16),
    ]
    rows = jax.ShapeDtypeStruct((ROWS, D), BF16)
    return pl.pallas_call(
        layer_kernel,
        out_shape=(
            jax.ShapeDtypeStruct(SHARES, BF16),
            jax.ShapeDtypeStruct((2, HALF, ROWS), BF16),
            rows,
            jax.ShapeDtypeStruct((ROWS, HID), BF16),
            rows,
            rows,
        ),
        in_specs=[full_spec(pltpu.SMEM)] * 3 + [full_spec()] + [full_spec(pltpu.HBM)] * 3,
        out_specs=(full_spec(),) * 6,
        scratch_shapes=[pltpu.VMEM(shape, kind) for shape, kind in scratch]
        + [pltpu.SemaphoreType.DMA((6,))],
        compiler_params=pltpu.CompilerParams(vmem_limit_bytes=VMEM_LIMIT),
        cost_estimate=pl.CostEstimate(
            flops=4_000_000_000, bytes_accessed=9_000_000, transcendentals=1_500_000
        ),
        name="layer",
    )(offsets, lengths, rab, arrived, *map(in_hbm, (cotangent, w_in, w_out)))


def total_kernel(received_ref, back_hbm, out_ref, sems):
    parts = 4
    step = MEMBERS // parts
    copies = []
    for n in range(parts):
        part = pl.ds(n * step, step)
        copies.append(
            pltpu.make_async_copy(back_hbm.at[part], out_ref.at[part, :, CHUNK:], sems.at[n])
        )
        copies[-1].start()
    total = received_ref[0].astype(F32)
    for m in range(1, MEMBERS):
        total += received_ref[m].astype(F32)
    total = (total * (1.0 / 256.0)).astype(BF16)
    out_ref[:, :, :CHUNK] = jnp.broadcast_to(total[None], (MEMBERS, PIECE, CHUNK))
    for copy in copies:
        copy.wait()


def total(received, back):
    return pl.pallas_call(
        total_kernel,
        out_shape=jax.ShapeDtypeStruct((MEMBERS, PIECE, CHUNK + D), BF16),
        in_specs=[full_spec(), full_spec(pltpu.HBM)],
        out_specs=full_spec(),
        scratch_shapes=[pltpu.SemaphoreType.DMA((4,))],
        compiler_params=pltpu.CompilerParams(vmem_limit_bytes=VMEM_SMALL),
        cost_estimate=pl.CostEstimate(flops=1_000_000, bytes_accessed=4_000_000, transcendentals=0),
        name="total",
    )(received, in_hbm(back))


def put_shares(source, rows_s, groups):
    for side in range(4):
        at = side * CHUNK
        for g in groups:
            value = source[g, side, :, :CHUNK].astype(F32)
            rows_s[g * PIECE : (g + 1) * PIECE, at : at + CHUNK] = value


def put_rows(rows_s, half, w_in_hbm, w_out_hbm, sems, source):
    copies = []
    parts = 4
    height = HALF // parts
    for part in range(parts):
        put_shares(source, rows_s, range(part * height // PIECE, (part + 1) * height // PIECE))
        here = slice(part * height, (part + 1) * height)
        there = pl.ds(pl.multiple_of(half * HALF + part * height, height), height)
        for n, copy in enumerate(
            (
                (rows_s.at[here, :HID], w_in_hbm.at[there]),
                (rows_s.at[here, HID:], w_out_hbm.at[there]),
            )
        ):
            copies.append(pltpu.make_async_copy(*copy, sems.at[2 * part + n]))
            copies[-1].start()
    return copies


def mine_kernel(
    route_ref, received_ref, events_hbm, w_in_hbm, w_out_hbm, rows_s, events_s, sems
):
    copies = put_rows(rows_s, lax.axis_index("group"), w_in_hbm, w_out_hbm, sems, received_ref)
    for j in range(PIECES):
        slot = lax.shift_right_logical(route_ref[j], 5)
        piece = received_ref[lax.shift_right_logical(slot, 2), lax.bitwise_and(slot, 3)]
        events_s[j * PIECE : (j + 1) * PIECE, :] = piece[:, CHUNK:]
    copies.append(pltpu.make_async_copy(events_s, events_hbm, sems.at[8]))
    copies[-1].start()
    for copy in copies:
        copy.wait()


def mine_out(route, received):
    return pl.pallas_call(
        mine_kernel,
        out_shape=(
            jax.ShapeDtypeStruct((ROWS, D), BF16),
            jax.ShapeDtypeStruct((D, HID), F32),
            jax.ShapeDtypeStruct((D, D), F32),
        ),
        in_specs=[full_spec(pltpu.SMEM), full_spec()],
        out_specs=(full_spec(pltpu.HBM),) * 3,
        scratch_shapes=[
            pltpu.VMEM((HALF, HID + D), F32),
            pltpu.VMEM((ROWS, D), BF16),
            pltpu.SemaphoreType.DMA((9,)),
        ],
        compiler_params=pltpu.CompilerParams(vmem_limit_bytes=VMEM_SMALL),
        cost_estimate=pl.CostEstimate(flops=0, bytes_accessed=6_000_000, transcendentals=0),
        name="mine_out",
    )(route, received)


def theirs_kernel(theirs_ref, _, __, w_in_hbm, w_out_hbm, rows_s, sems):
    for copy in put_rows(rows_s, 1 - lax.axis_index("group"), w_in_hbm, w_out_hbm, sems, theirs_ref):
        copy.wait()


def theirs_out(theirs, w_in_grad, w_out_grad):
    return pl.pallas_call(
        theirs_kernel,
        out_shape=(
            jax.ShapeDtypeStruct((D, HID), F32),
            jax.ShapeDtypeStruct((D, D), F32),
        ),
        in_specs=[full_spec()] + [full_spec(pltpu.HBM)] * 2,
        out_specs=(full_spec(pltpu.HBM),) * 2,
        scratch_shapes=[
            pltpu.VMEM((HALF, HID + D), F32),
            pltpu.SemaphoreType.DMA((8,)),
        ],
        input_output_aliases={1: 0, 2: 1},
        compiler_params=pltpu.CompilerParams(vmem_limit_bytes=VMEM_SMALL),
        cost_estimate=pl.CostEstimate(flops=0, bytes_accessed=4_000_000, transcendentals=0),
        name="theirs_out",
    )(theirs, w_in_grad, w_out_grad)


def body(events, route, block_offset, hist_length, cotangent, w_in, w_out, rab):
    exchange = functools.partial(
        lax.all_to_all, axis_name="member", split_axis=0, concat_axis=0, tiled=True
    )
    swap = functools.partial(lax.ppermute, axis_name="group", perm=[(0, 1), (1, 0)])
    arrived = exchange(pack(route, events))
    other, left, up, gh, bal, mixed = layer(
        block_offset, hist_length, rab, arrived, cotangent, w_in, w_out
    )
    got = swap(other)
    joined = join(own_part(left, up, gh), got)
    received = exchange(joined.reshape(MEMBERS, PIECE, CHUNK))
    outputs, back = rest(block_offset, hist_length, gh, w_in, bal, up, arrived, mixed, w_out)
    received = exchange(total(received, back.reshape(MEMBERS, PIECE, D)))
    theirs = swap(received[:, :, :CHUNK])
    events_grad, w_in_grad, w_out_grad = mine_out(
        route, received.reshape(*SHARES[:3], CHUNK + D)
    )
    w_in_grad, w_out_grad = theirs_out(theirs.reshape(SHARES), w_in_grad, w_out_grad)
    return outputs, events_grad, w_in_grad, w_out_grad


def solution(mesh):
    placed = (
        P(("group", "member"), None),
        P(("group", "member")),
        P(("group", "member")),
        P(("group", "member")),
        P(("group", "member"), None),
        P(),
        P(),
        P(),
    )
    return jax.shard_map(
        body,
        mesh=mesh,
        in_specs=placed,
        out_specs=(P(("group", "member"), None), P(("group", "member"), None), P(), P()),
        check_vma=False,
    )
```

```python
import functools
import math

import jax
import jax.numpy as jnp
from jax import lax
from jax.experimental import pallas as pl
from jax.experimental.pallas import tpu as pltpu
from jax.sharding import PartitionSpec as P

EPS = 1e-05
BF16 = jnp.bfloat16
F32 = jnp.float32
VMEM_LIMIT = 32 * 1024 * 1024
VMEM_SMALL = 16 * 1024 * 1024

ROWS, D, HID = 512, 512, 2048
BLOCK, BLOCKS, HEADS, BUCKETS = 128, 4, 4, 12
PIECE, PIECES, MEMBERS = 16, 32, 64
SLOT = 72
CHUNK = 640
SCALE = 1.0 / math.sqrt(128)
HALF = D // 2
SHARES = (HALF // PIECE, 4, PIECE, CHUNK)


def dot(a, b):
    return jnp.dot(a, b, preferred_element_type=F32)


def dot_nt(a, b):
    return lax.dot_general(a, b, (((1,), (1,)), ((), ())), preferred_element_type=F32)


def dot_tn(a, b):
    return lax.dot_general(a, b, (((0,), (0,)), ((), ())), preferred_element_type=F32)


def sigmoid(v):
    return 0.5 * jnp.tanh(0.5 * v) + 0.5


def in_hbm(array):
    return pltpu.with_memory_space_constraint(array, pltpu.HBM)


def full_spec(memory=pltpu.VMEM):
    return pl.BlockSpec(memory_space=memory)


def pack_kernel(route_hbm, events_hbm, out_ref, route_s, events_s, sems):
    half = ROWS // 2
    loads = [pltpu.make_async_copy(route_hbm, route_s, sems.at[0])]
    for n in range(2):
        rows = pl.ds(n * half, half)
        loads.append(
            pltpu.make_async_copy(events_hbm.at[rows], events_s.at[rows], sems.at[1 + n])
        )
    for load in loads:
        load.start()
    out_ref[...] = jnp.zeros_like(out_ref)
    for load in loads:
        load.wait()
    for j in range(PIECES):
        target = route_s[j]
        device = lax.shift_right_logical(target, 5)
        place = lax.bitwise_and(target, PIECES - 1)
        for k in range(D // 128):
            out_ref[device, k * PIECE : (k + 1) * PIECE, :] = events_s[
                j * PIECE : (j + 1) * PIECE, k * 128 : (k + 1) * 128
            ]
        label = jnp.full((SLOT - 4 * PIECE, 128), (place + 1).astype(F32), F32)
        out_ref[device, 4 * PIECE :, :] = label.astype(BF16)


def pack(route, events):
    return pl.pallas_call(
        pack_kernel,
        out_shape=jax.ShapeDtypeStruct((MEMBERS, SLOT, 128), BF16),
        in_specs=[full_spec(pltpu.HBM)] * 2,
        out_specs=full_spec(),
        scratch_shapes=[
            pltpu.SMEM((PIECES,), jnp.int32),
            pltpu.VMEM((ROWS, D), BF16),
            pltpu.SemaphoreType.DMA((3,)),
        ],
        compiler_params=pltpu.CompilerParams(vmem_limit_bytes=VMEM_SMALL),
        name="pack_pieces",
    )(in_hbm(route), in_hbm(events))


def cell_goals(arrived_ref):
    labels = arrived_ref[:, 4 * PIECE :, :].astype(F32)
    if labels.shape[1] < PIECE:
        labels = jnp.concatenate([labels, labels], axis=1)
    within = lax.broadcasted_iota(jnp.int32, labels.shape, 1).astype(F32)
    return ((labels - 1.0) * PIECE + within).reshape(MEMBERS * PIECE, 128)


def block_order(offset_ref):
    second = jnp.int32(1)
    for b in range(2, BLOCKS):
        second = jnp.where(offset_ref[b] == 1, b, second)
    return (
        second - 1,
        second,
        jnp.where(second == 1, 2, 0),
        jnp.where(second == 3, 1, 3),
    )


def block_rows(order, i):
    return pl.ds(pl.multiple_of(order[i] * BLOCK, BLOCK), BLOCK)


def inner_goals(goals, order):
    block = jnp.floor(goals * (1.0 / BLOCK))
    moved = goals
    for i in range(BLOCKS):
        at = order[i].astype(F32)
        moved = jnp.where(block == at, goals + (float(i) - at) * BLOCK, moved)
    return moved


def live_column(length_ref, order, i):
    first = BLOCK if i == 1 else 0
    return lax.broadcasted_iota(jnp.int32, (BLOCK, 1), 0) + first < length_ref[order[i]]


def normalized(x):
    centered = x - jnp.mean(x, axis=-1, keepdims=True)
    variance = jnp.mean(centered * centered, axis=-1, keepdims=True)
    rstd = lax.rsqrt(variance + EPS)
    return centered * rstd, rstd


def normalized_back(grad, hat, rstd):
    return rstd * (
        grad
        - jnp.mean(grad, axis=-1, keepdims=True)
        - hat * jnp.mean(grad * hat, axis=-1, keepdims=True)
    )


def head_cols(part, head):
    return slice(part * D + head * 128, part * D + head * 128 + 128)


def layer_kernel(
    offset_ref,
    length_ref,
    rab_ref,
    arrived_ref,
    cot_hbm,
    w_in_hbm,
    w_out_hbm,
    other_ref,
    left_ref,
    up_ref,
    gh_ref,
    bal_ref,
    w_in_ref,
    out_hbm,
    place_s,
    norm_s,
    hid_s,
    slope_s,
    long_att_s,
    long_ds_s,
    long_slope_s,
    short_att_s,
    short_slope_s,
    ctx_s,
    gm_s,
    gctx_s,
    trans_s,
    cot_ref,
    w_out_ref,
    mixed_ref,
    out_s,
    sems,
):
    copies = []
    for n, start in enumerate((1024, 1536, 512, 0)):
        cols = pl.ds(start, D)
        copies.append(
            pltpu.make_async_copy(w_in_hbm.at[:, cols], w_in_ref.at[:, cols], sems.at[n])
        )
    copies.append(pltpu.make_async_copy(cot_hbm, cot_ref, sems.at[4]))
    copies.append(pltpu.make_async_copy(w_out_hbm, w_out_ref, sems.at[5]))
    for copy in copies:
        copy.start()
    core = lax.axis_index("group")
    order = block_order(offset_ref)
    long_rows, short_rows = slice(0, 2 * BLOCK), slice(2 * BLOCK, 4 * BLOCK)

    tens = jnp.floor(cell_goals(arrived_ref) * (1.0 / PIECE)).astype(BF16)
    pick = (lax.broadcasted_iota(jnp.int32, (8, 128), 1) == 0).astype(BF16)
    ones = lax.bitwise_and(
        lax.broadcasted_iota(jnp.int32, (1, MEMBERS * PIECE), 1), PIECE - 1
    ).astype(F32)
    goal = inner_goals(dot_nt(pick, tens)[0:1, :] * PIECE + ones, order)

    def gather(rows):
        for r in range(rows.start, rows.stop, BLOCK):
            row = lax.broadcasted_iota(jnp.int32, (BLOCK, 1), 0).astype(F32) + float(r)
            place_s[r : r + BLOCK, :] = jnp.where(goal == row, 1.0, 0.0).astype(BF16)
        for k in range(0, D // 128, 2):
            cells = jnp.concatenate(
                [
                    arrived_ref[:, n * PIECE : (n + 1) * PIECE, :].reshape(MEMBERS * PIECE, 128)
                    for n in (k, k + 1)
                ],
                axis=1,
            )
            bal_ref[rows, k * 128 : k * 128 + 256] = dot(place_s[rows, :], cells).astype(BF16)

    def norm(r):
        sl = slice(r, r + 64)
        norm_s[sl, :] = normalized(bal_ref[sl, :].astype(F32))[0].astype(BF16)

    def project(rows, n):
        cols = slice(n, n + 256)
        v = dot(norm_s[rows, :], w_in_ref[:, cols])
        g = sigmoid(v)
        h = v * g
        hid_s[rows, cols] = h.astype(BF16)
        slope_s[rows, cols] = g + h * (1.0 - g)

    row_id = lax.broadcasted_iota(jnp.int32, (BLOCK, BLOCK), 0)
    col_id = lax.broadcasted_iota(jnp.int32, (BLOCK, BLOCK), 1)
    distance = row_id - col_id
    near_pairs = distance >= 0

    def bias(head, apart, buckets):
        total = jnp.full((BLOCK, BLOCK), rab_ref[head, 0], F32)
        for bucket in range(1, buckets):
            total = jnp.where(apart >= 2 ** (bucket - 1), rab_ref[head, bucket], total)
        return total

    def weigh(scores, relative, allowed):
        s = scores * SCALE + relative
        g = sigmoid(s)
        a = s * g
        return (
            jnp.where(allowed, a, 0.0).astype(BF16),
            jnp.where(allowed, g + a * (1.0 - g), 0.0),
        )

    def live_rows(i):
        return row_id + (BLOCK if i == 1 else 0) < length_ref[order[i]]

    allowed = [near_pairs & live_rows(i) for i in range(BLOCKS)] + [live_rows(1)]
    near = [None] * HEADS
    low, high = slice(0, BLOCK), slice(BLOCK, 2 * BLOCK)
    long_tiles = ((low, low, 0), (high, high, 1), (high, low, BLOCKS))

    def long_attend(head):
        near[head] = bias(head, distance, 8)
        far = bias(head, distance + BLOCK, 9)
        scores = dot_nt(hid_s[long_rows, head_cols(2, head)], hid_s[long_rows, head_cols(3, head)])
        long_att_s[head, low, high] = jnp.zeros((BLOCK, BLOCK), BF16)
        long_ds_s[head, low, high] = jnp.zeros((BLOCK, BLOCK), BF16)
        for tile, (i, j, pairs) in enumerate(long_tiles):
            a, slope = weigh(scores[i, j], far if tile == 2 else near[head], allowed[pairs])
            long_att_s[head, i, j] = a
            long_slope_s[head, tile] = slope
        ctx_s[long_rows, head_cols(0, head)] = dot(
            long_att_s[head], hid_s[long_rows, head_cols(1, head)]
        )

    def short_attend(head):
        for i in (2, 3):
            rows = slice(i * BLOCK, (i + 1) * BLOCK)
            scores = dot_nt(hid_s[rows, head_cols(2, head)], hid_s[rows, head_cols(3, head)])
            a, slope = weigh(scores, near[head], allowed[i])
            short_att_s[head, i - 2] = a
            short_slope_s[head, i - 2] = slope
            ctx_s[rows, head_cols(0, head)] = dot(a, hid_s[rows, head_cols(1, head)])

    def upstream(i):
        kept = jnp.where(
            live_column(length_ref, order, i), cot_ref[block_rows(order, i), :].astype(F32), 0.0
        )
        up_ref[i * BLOCK : (i + 1) * BLOCK, :] = kept.astype(BF16)

    def middle(r):
        sl = slice(r, r + 64)
        n, rstd = normalized(ctx_s[sl, :])
        u = hid_s[sl, 0:D].astype(F32)
        mixed_ref[sl, :] = (n * u).astype(BF16)
        gm = gm_s[sl, :]
        gh_ref[sl, 0:D] = (gm * n * slope_s[sl, 0:D]).astype(BF16)
        gctx_s[sl, :] = normalized_back(gm * u, n, rstd).astype(BF16)

    def output(rows):
        product = dot(mixed_ref[rows, :], w_out_ref[...])
        for i in range(rows.start // BLOCK, rows.stop // BLOCK):
            here = slice(i * BLOCK, (i + 1) * BLOCK)
            there = slice(here.start - rows.start, here.stop - rows.start)
            value = bal_ref[here, :].astype(F32) + product[there, :]
            value = jnp.where(live_column(length_ref, order, i), value, 0.0)
            out_s[block_rows(order, i), :] = value.astype(BF16)

    def finish_grads(rows, head, gv, gq, gk):
        for part, grad in ((1, gv), (2, gq * SCALE), (3, gk * SCALE)):
            cols = head_cols(part, head)
            gh_ref[rows, cols] = (grad * slope_s[rows, cols]).astype(BF16)

    def long_back(head):
        gc = gctx_s[long_rows, head_cols(0, head)]
        grads = dot_nt(gc, hid_s[long_rows, head_cols(1, head)])
        for tile, (i, j, _) in enumerate(long_tiles):
            long_ds_s[head, i, j] = (grads[i, j] * long_slope_s[head, tile]).astype(BF16)
        ds = long_ds_s[head]
        finish_grads(
            long_rows,
            head,
            dot_tn(long_att_s[head], gc),
            dot(ds, hid_s[long_rows, head_cols(3, head)]),
            dot_tn(ds, hid_s[long_rows, head_cols(2, head)]),
        )

    def short_back(head):
        for i in (2, 3):
            rows = slice(i * BLOCK, (i + 1) * BLOCK)
            gc = gctx_s[rows, head_cols(0, head)]
            grads = dot_nt(gc, hid_s[rows, head_cols(1, head)])
            ds = (grads * short_slope_s[head, i - 2]).astype(BF16)
            finish_grads(
                rows,
                head,
                dot_tn(short_att_s[head, i - 2], gc),
                dot(ds, hid_s[rows, head_cols(3, head)]),
                dot_tn(ds, hid_s[rows, head_cols(2, head)]),
            )

    parts = (1024, 1536, 1280, 1792, 512, 768, 0, 256)
    gather(long_rows)
    gather(short_rows)
    for r in range(0, 256, 64):
        norm(r)
    for k, n in enumerate(parts):
        if k in (0, 1, 4, 6):
            copies[(0, 1, 4, 6).index(k)].wait()
        project(long_rows, n)
        if k < 4:
            norm(256 + 64 * k)
    for copy in copies[4:]:
        copy.wait()
    for i in range(BLOCKS):
        upstream(i)
    gm_s[...] = dot_nt(up_ref[...], w_out_ref[...])
    for k, n in enumerate(parts):
        if k % 2 == 0:
            long_attend(k // 2)
        project(short_rows, n)
    for head in range(HEADS):
        middle(64 * head)
        short_attend(head)
    trans_s[0] = norm_s[...].T
    output(long_rows)
    for head in range(HEADS):
        long_back(head)
        middle(256 + 64 * head)
    trans_s[1] = mixed_ref[...].T
    output(short_rows)
    copies.append(pltpu.make_async_copy(out_s, out_hbm, sems.at[6]))
    copies[-1].start()
    for head in range(HEADS):
        short_back(head)

    own_rows = pl.ds(pl.multiple_of(core * HALF, HALF), HALF)
    other_rows = pl.ds(pl.multiple_of((1 - core) * HALF, HALF), HALF)
    left_ref[0] = trans_s[0, own_rows, :]
    left_ref[1] = trans_s[1, own_rows, :]

    def store(at, value):
        other_ref[at] = value.astype(BF16)

    weight_grads(trans_s[0, other_rows, :], trans_s[1, other_rows, :], gh_ref, up_ref, store)
    copies[-1].wait()


def weight_grads(normed_t, mixed_t, gh_ref, up_ref, store):
    for at in range(0, HID + D, 256):
        if at < HID:
            value = dot(normed_t, gh_ref[:, at : at + 256])
        else:
            value = dot(mixed_t, up_ref[:, at - HID : at - HID + 256])
        for n in (0, 128):
            side, start = (at + n) // CHUNK, (at + n) % CHUNK
            shares = value[:, n : n + 128].reshape(HALF // PIECE, PIECE, 128)
            store((slice(None), side, slice(None), slice(start, start + 128)), shares)


def beside_kernel(
    offset_ref,
    arrived_ref,
    left_ref,
    up_ref,
    gh_ref,
    bal_ref,
    w_in_ref,
    own_ref,
    back_ref,
    gx_s,
    gb_s,
    place_s,
):
    gx_s[...] = dot_nt(gh_ref[...], w_in_ref[...])

    def store(at, value):
        own_ref[at] = value.astype(BF16)

    weight_grads(left_ref[0], left_ref[1], gh_ref, up_ref, store)
    for r in range(0, ROWS, 64):
        sl = slice(r, r + 64)
        hat, rstd = normalized(bal_ref[sl, :].astype(F32))
        grad = normalized_back(gx_s[sl, :], hat, rstd)
        gb_s[sl, :] = (up_ref[sl, :].astype(F32) + grad).astype(BF16)
    goals = inner_goals(cell_goals(arrived_ref), block_order(offset_ref))
    for b in range(BLOCKS):
        row = lax.broadcasted_iota(jnp.int32, (1, BLOCK), 1).astype(F32) + float(b * BLOCK)
        place_s[:, b * BLOCK : (b + 1) * BLOCK] = jnp.where(goals == row, 1.0, 0.0).astype(BF16)
    for n in range(0, D, 256):
        back_ref[:, n : n + 256] = dot(place_s[...], gb_s[:, n : n + 256]).astype(BF16)


def beside(offsets, arrived, left, up, gh, bal, w_in):
    return pl.pallas_call(
        beside_kernel,
        out_shape=(
            jax.ShapeDtypeStruct(SHARES, BF16),
            jax.ShapeDtypeStruct((MEMBERS * PIECE, D), BF16),
        ),
        in_specs=[full_spec(pltpu.SMEM)] + [full_spec()] * 6,
        out_specs=(full_spec(),) * 2,
        scratch_shapes=[
            pltpu.VMEM((ROWS, D), F32),
            pltpu.VMEM((ROWS, D), BF16),
            pltpu.VMEM((MEMBERS * PIECE, ROWS), BF16),
        ],
        compiler_params=pltpu.CompilerParams(vmem_limit_bytes=VMEM_SMALL),
        cost_estimate=pl.CostEstimate(
            flops=3_000_000_000, bytes_accessed=2_000_000, transcendentals=1_000
        ),
        name="beside",
    )(offsets, arrived, left, up, gh, bal, w_in)


def join_kernel(own_ref, got_ref, out_ref):
    out_ref[...] = (own_ref[...].astype(F32) + got_ref[...].astype(F32)).astype(BF16)


def join(own, got):
    return pl.pallas_call(
        join_kernel,
        out_shape=jax.ShapeDtypeStruct(SHARES, BF16),
        in_specs=[full_spec()] * 2,
        out_specs=full_spec(),
        compiler_params=pltpu.CompilerParams(vmem_limit_bytes=VMEM_SMALL),
        cost_estimate=pl.CostEstimate(flops=1_000_000, bytes_accessed=4_000_000, transcendentals=0),
        name="join",
    )(own, got)


def layer(offsets, lengths, rab, arrived, cotangent, w_in, w_out):
    scratch = [
        ((ROWS, MEMBERS * PIECE), BF16),
        ((ROWS, D), BF16),
        ((ROWS, HID), BF16),
        ((ROWS, HID), F32),
        ((HEADS, 2 * BLOCK, 2 * BLOCK), BF16),
        ((HEADS, 2 * BLOCK, 2 * BLOCK), BF16),
        ((HEADS, 3, BLOCK, BLOCK), F32),
        ((HEADS, 2, BLOCK, BLOCK), BF16),
        ((HEADS, 2, BLOCK, BLOCK), F32),
        ((ROWS, D), F32),
        ((ROWS, D), F32),
        ((ROWS, D), BF16),
        ((2, D, ROWS), BF16),
        ((ROWS, D), BF16),
        ((D, D), BF16),
        ((ROWS, D), BF16),
        ((ROWS, D), BF16),
    ]
    rows = jax.ShapeDtypeStruct((ROWS, D), BF16)
    return pl.pallas_call(
        layer_kernel,
        out_shape=(
            jax.ShapeDtypeStruct(SHARES, BF16),
            jax.ShapeDtypeStruct((2, HALF, ROWS), BF16),
            rows,
            jax.ShapeDtypeStruct((ROWS, HID), BF16),
            rows,
            jax.ShapeDtypeStruct((D, HID), BF16),
            pltpu.HBM((ROWS, D), BF16),
        ),
        in_specs=[full_spec(pltpu.SMEM)] * 3 + [full_spec()] + [full_spec(pltpu.HBM)] * 3,
        out_specs=(full_spec(),) * 6 + (full_spec(pltpu.HBM),),
        scratch_shapes=[pltpu.VMEM(shape, kind) for shape, kind in scratch]
        + [pltpu.SemaphoreType.DMA((7,))],
        compiler_params=pltpu.CompilerParams(vmem_limit_bytes=VMEM_LIMIT),
        cost_estimate=pl.CostEstimate(
            flops=4_000_000_000, bytes_accessed=9_000_000, transcendentals=1_500_000
        ),
        name="layer",
    )(offsets, lengths, rab, arrived, *map(in_hbm, (cotangent, w_in, w_out)))


def total_kernel(received_ref, back_ref, out_ref):
    total = received_ref[0].astype(F32)
    for m in range(1, MEMBERS):
        total += received_ref[m].astype(F32)
    total = (total * (1.0 / 256.0)).astype(BF16)
    out_ref[:, :, :CHUNK] = jnp.broadcast_to(total[None], (MEMBERS, PIECE, CHUNK))
    out_ref[:, :, CHUNK:] = back_ref[...]


def total(received, back):
    return pl.pallas_call(
        total_kernel,
        out_shape=jax.ShapeDtypeStruct((MEMBERS, PIECE, CHUNK + D), BF16),
        in_specs=[full_spec()] * 2,
        out_specs=full_spec(),
        compiler_params=pltpu.CompilerParams(vmem_limit_bytes=VMEM_SMALL),
        cost_estimate=pl.CostEstimate(flops=1_000_000, bytes_accessed=4_000_000, transcendentals=0),
        name="total",
    )(received, back)


def put_shares(source, rows_s, groups):
    for side in range(4):
        at = side * CHUNK
        for g in groups:
            value = source[g, side, :, :CHUNK].astype(F32)
            rows_s[g * PIECE : (g + 1) * PIECE, at : at + CHUNK] = value


def put_rows(rows_s, half, w_in_hbm, w_out_hbm, sems, source):
    copies = []
    parts = 4
    height = HALF // parts
    for part in range(parts):
        put_shares(source, rows_s, range(part * height // PIECE, (part + 1) * height // PIECE))
        here = slice(part * height, (part + 1) * height)
        there = pl.ds(pl.multiple_of(half * HALF + part * height, height), height)
        for n, copy in enumerate(
            (
                (rows_s.at[here, :HID], w_in_hbm.at[there]),
                (rows_s.at[here, HID:], w_out_hbm.at[there]),
            )
        ):
            copies.append(pltpu.make_async_copy(*copy, sems.at[2 * part + n]))
            copies[-1].start()
    return copies


def mine_kernel(
    route_hbm, received_ref, events_hbm, w_in_hbm, w_out_hbm, route_s, rows_s, events_s, sems
):
    load = pltpu.make_async_copy(route_hbm, route_s, sems.at[9])
    load.start()
    copies = put_rows(
        rows_s, lax.axis_index("group"), w_in_hbm, w_out_hbm, sems, received_ref
    )
    load.wait()
    for j in range(PIECES):
        slot = lax.shift_right_logical(route_s[j], 5)
        piece = received_ref[lax.shift_right_logical(slot, 2), lax.bitwise_and(slot, 3)]
        events_s[j * PIECE : (j + 1) * PIECE, :] = piece[:, CHUNK:]
    copies.append(pltpu.make_async_copy(events_s, events_hbm, sems.at[8]))
    copies[-1].start()
    for copy in copies:
        copy.wait()


def mine_out(route, received):
    return pl.pallas_call(
        mine_kernel,
        out_shape=(
            jax.ShapeDtypeStruct((ROWS, D), BF16),
            jax.ShapeDtypeStruct((D, HID), F32),
            jax.ShapeDtypeStruct((D, D), F32),
        ),
        in_specs=[full_spec(pltpu.HBM), full_spec()],
        out_specs=(full_spec(pltpu.HBM),) * 3,
        scratch_shapes=[
            pltpu.SMEM((PIECES,), jnp.int32),
            pltpu.VMEM((HALF, HID + D), F32),
            pltpu.VMEM((ROWS, D), BF16),
            pltpu.SemaphoreType.DMA((10,)),
        ],
        compiler_params=pltpu.CompilerParams(vmem_limit_bytes=VMEM_SMALL),
        cost_estimate=pl.CostEstimate(flops=0, bytes_accessed=6_000_000, transcendentals=0),
        name="mine_out",
    )(in_hbm(route), received)


def theirs_kernel(theirs_ref, _, __, w_in_hbm, w_out_hbm, rows_s, sems):
    for copy in put_rows(rows_s, 1 - lax.axis_index("group"), w_in_hbm, w_out_hbm, sems, theirs_ref):
        copy.wait()


def theirs_out(theirs, w_in_grad, w_out_grad):
    return pl.pallas_call(
        theirs_kernel,
        out_shape=(
            jax.ShapeDtypeStruct((D, HID), F32),
            jax.ShapeDtypeStruct((D, D), F32),
        ),
        in_specs=[full_spec()] + [full_spec(pltpu.HBM)] * 2,
        out_specs=(full_spec(pltpu.HBM),) * 2,
        scratch_shapes=[
            pltpu.VMEM((HALF, HID + D), F32),
            pltpu.SemaphoreType.DMA((8,)),
        ],
        input_output_aliases={1: 0, 2: 1},
        compiler_params=pltpu.CompilerParams(vmem_limit_bytes=VMEM_SMALL),
        cost_estimate=pl.CostEstimate(flops=0, bytes_accessed=4_000_000, transcendentals=0),
        name="theirs_out",
    )(theirs, w_in_grad, w_out_grad)


def body(events, route, block_offset, hist_length, cotangent, w_in, w_out, rab):
    exchange = functools.partial(
        lax.all_to_all, axis_name="member", split_axis=0, concat_axis=0, tiled=True
    )
    swap = functools.partial(lax.ppermute, axis_name="group", perm=[(0, 1), (1, 0)])
    arrived = exchange(pack(route, events))
    other, left, up, gh, bal, w_in_here, outputs = layer(
        block_offset, hist_length, rab, arrived, cotangent, w_in, w_out
    )
    got = swap(other)
    own, back = beside(block_offset, arrived, left, up, gh, bal, w_in_here)
    received = exchange(join(own, got).reshape(MEMBERS, PIECE, CHUNK))
    received = exchange(total(received, back.reshape(MEMBERS, PIECE, D)))
    theirs = swap(received[:, :, :CHUNK])
    events_grad, w_in_grad, w_out_grad = mine_out(
        route, received.reshape(*SHARES[:3], CHUNK + D)
    )
    w_in_grad, w_out_grad = theirs_out(theirs.reshape(SHARES), w_in_grad, w_out_grad)
    return outputs, events_grad, w_in_grad, w_out_grad


def solution(mesh):
    placed = (
        P(("group", "member"), None),
        P(("group", "member")),
        P(("group", "member")),
        P(("group", "member")),
        P(("group", "member"), None),
        P(),
        P(),
        P(),
    )
    return jax.shard_map(
        body,
        mesh=mesh,
        in_specs=placed,
        out_specs=(P(("group", "member"), None), P(("group", "member"), None), P(), P()),
        check_vma=False,
    )
```

```python
import functools
import math

import jax
import jax.numpy as jnp
from jax import lax
from jax.experimental import pallas as pl
from jax.experimental.pallas import tpu as pltpu
from jax.sharding import PartitionSpec as P

EPS = 1e-05
BF16 = jnp.bfloat16
F32 = jnp.float32
VMEM_LIMIT = 32 * 1024 * 1024
VMEM_SMALL = 16 * 1024 * 1024

ROWS, D, HID = 512, 512, 2048
BLOCK, BLOCKS, HEADS, BUCKETS = 128, 4, 4, 12
PIECE, PIECES, MEMBERS = 16, 32, 64
SLOT = 72
CHUNK = 640
SCALE = 1.0 / math.sqrt(128)
HALF = D // 2
SHARES = (HALF // PIECE, 4, PIECE, CHUNK)


def dot(a, b):
    return jnp.dot(a, b, preferred_element_type=F32)


def dot_nt(a, b):
    return lax.dot_general(a, b, (((1,), (1,)), ((), ())), preferred_element_type=F32)


def dot_tn(a, b):
    return lax.dot_general(a, b, (((0,), (0,)), ((), ())), preferred_element_type=F32)


def sigmoid(v):
    return 0.5 * jnp.tanh(0.5 * v) + 0.5


def in_hbm(array):
    return pltpu.with_memory_space_constraint(array, pltpu.HBM)


def full_spec(memory=pltpu.VMEM):
    return pl.BlockSpec(memory_space=memory)


def pack_kernel(route_hbm, events_hbm, out_ref, route_s, events_s, sems):
    half = ROWS // 2
    loads = [pltpu.make_async_copy(route_hbm, route_s, sems.at[0])]
    for n in range(2):
        rows = pl.ds(n * half, half)
        loads.append(
            pltpu.make_async_copy(events_hbm.at[rows], events_s.at[rows], sems.at[1 + n])
        )
    for load in loads:
        load.start()
    out_ref[...] = jnp.zeros_like(out_ref)
    for load in loads:
        load.wait()
    for j in range(PIECES):
        target = route_s[j]
        device = lax.shift_right_logical(target, 5)
        place = lax.bitwise_and(target, PIECES - 1)
        for k in range(D // 128):
            out_ref[device, k * PIECE : (k + 1) * PIECE, :] = events_s[
                j * PIECE : (j + 1) * PIECE, k * 128 : (k + 1) * 128
            ]
        label = jnp.full((SLOT - 4 * PIECE, 128), (place + 1).astype(F32), F32)
        out_ref[device, 4 * PIECE :, :] = label.astype(BF16)


def pack(route, events):
    return pl.pallas_call(
        pack_kernel,
        out_shape=jax.ShapeDtypeStruct((MEMBERS, SLOT, 128), BF16),
        in_specs=[full_spec(pltpu.HBM)] * 2,
        out_specs=full_spec(),
        scratch_shapes=[
            pltpu.SMEM((PIECES,), jnp.int32),
            pltpu.VMEM((ROWS, D), BF16),
            pltpu.SemaphoreType.DMA((3,)),
        ],
        compiler_params=pltpu.CompilerParams(vmem_limit_bytes=VMEM_SMALL),
        name="pack_pieces",
    )(in_hbm(route), in_hbm(events))


def cell_goals(arrived_ref):
    labels = arrived_ref[:, 4 * PIECE :, :].astype(F32)
    if labels.shape[1] < PIECE:
        labels = jnp.concatenate([labels, labels], axis=1)
    within = lax.broadcasted_iota(jnp.int32, labels.shape, 1).astype(F32)
    return ((labels - 1.0) * PIECE + within).reshape(MEMBERS * PIECE, 128)


def block_order(offset_ref):
    second = jnp.int32(1)
    for b in range(2, BLOCKS):
        second = jnp.where(offset_ref[b] == 1, b, second)
    return (
        second - 1,
        second,
        jnp.where(second == 1, 2, 0),
        jnp.where(second == 3, 1, 3),
    )


def block_rows(order, i):
    return pl.ds(pl.multiple_of(order[i] * BLOCK, BLOCK), BLOCK)


def inner_goals(goals, order):
    block = jnp.floor(goals * (1.0 / BLOCK))
    moved = goals
    for i in range(BLOCKS):
        at = order[i].astype(F32)
        moved = jnp.where(block == at, goals + (float(i) - at) * BLOCK, moved)
    return moved


def live_column(length_ref, order, i):
    first = BLOCK if i == 1 else 0
    return lax.broadcasted_iota(jnp.int32, (BLOCK, 1), 0) + first < length_ref[order[i]]


def normalized(x):
    centered = x - jnp.mean(x, axis=-1, keepdims=True)
    variance = jnp.mean(centered * centered, axis=-1, keepdims=True)
    rstd = lax.rsqrt(variance + EPS)
    return centered * rstd, rstd


def normalized_back(grad, hat, rstd):
    return rstd * (
        grad
        - jnp.mean(grad, axis=-1, keepdims=True)
        - hat * jnp.mean(grad * hat, axis=-1, keepdims=True)
    )


def head_cols(part, head):
    return slice(part * D + head * 128, part * D + head * 128 + 128)


def layer_kernel(
    offset_ref,
    length_ref,
    rab_ref,
    arrived_ref,
    cot_ref,
    w_in_ref,
    w_out_ref,
    other_ref,
    left_ref,
    up_ref,
    gh_ref,
    bal_ref,
    out_hbm,
    place_s,
    norm_s,
    hid_s,
    slope_s,
    long_att_s,
    long_ds_s,
    long_slope_s,
    short_att_s,
    short_slope_s,
    ctx_s,
    gm_s,
    gctx_s,
    trans_s,
    mixed_ref,
    out_s,
    sem,
):
    core = lax.axis_index("group")
    order = block_order(offset_ref)
    long_rows, short_rows = slice(0, 2 * BLOCK), slice(2 * BLOCK, 4 * BLOCK)

    tens = jnp.floor(cell_goals(arrived_ref) * (1.0 / PIECE)).astype(BF16)
    pick = (lax.broadcasted_iota(jnp.int32, (8, 128), 1) == 0).astype(BF16)
    ones = lax.bitwise_and(
        lax.broadcasted_iota(jnp.int32, (1, MEMBERS * PIECE), 1), PIECE - 1
    ).astype(F32)
    goal = inner_goals(dot_nt(pick, tens)[0:1, :] * PIECE + ones, order)

    def gather(rows):
        for r in range(rows.start, rows.stop, BLOCK):
            row = lax.broadcasted_iota(jnp.int32, (BLOCK, 1), 0).astype(F32) + float(r)
            place_s[r : r + BLOCK, :] = jnp.where(goal == row, 1.0, 0.0).astype(BF16)
        for k in range(0, D // 128, 2):
            cells = jnp.concatenate(
                [
                    arrived_ref[:, n * PIECE : (n + 1) * PIECE, :].reshape(MEMBERS * PIECE, 128)
                    for n in (k, k + 1)
                ],
                axis=1,
            )
            bal_ref[rows, k * 128 : k * 128 + 256] = dot(place_s[rows, :], cells).astype(BF16)

    def norm(r):
        sl = slice(r, r + 64)
        norm_s[sl, :] = normalized(bal_ref[sl, :].astype(F32))[0].astype(BF16)

    def project(rows, n):
        cols = slice(n, n + 256)
        v = dot(norm_s[rows, :], w_in_ref[:, cols])
        g = sigmoid(v)
        h = v * g
        hid_s[rows, cols] = h.astype(BF16)
        slope_s[rows, cols] = g + h * (1.0 - g)

    row_id = lax.broadcasted_iota(jnp.int32, (BLOCK, BLOCK), 0)
    col_id = lax.broadcasted_iota(jnp.int32, (BLOCK, BLOCK), 1)
    distance = row_id - col_id
    near_pairs = distance >= 0

    def bias(head, apart, buckets):
        total = jnp.full((BLOCK, BLOCK), rab_ref[head, 0], F32)
        for bucket in range(1, buckets):
            total = jnp.where(apart >= 2 ** (bucket - 1), rab_ref[head, bucket], total)
        return total

    def weigh(scores, relative, allowed):
        s = scores * SCALE + relative
        g = sigmoid(s)
        a = s * g
        return (
            jnp.where(allowed, a, 0.0).astype(BF16),
            jnp.where(allowed, g + a * (1.0 - g), 0.0),
        )

    def live_rows(i):
        return row_id + (BLOCK if i == 1 else 0) < length_ref[order[i]]

    allowed = [near_pairs & live_rows(i) for i in range(BLOCKS)] + [live_rows(1)]
    near = [None] * HEADS
    low, high = slice(0, BLOCK), slice(BLOCK, 2 * BLOCK)
    long_tiles = ((low, low, 0), (high, high, 1), (high, low, BLOCKS))

    def long_attend(head):
        near[head] = bias(head, distance, 8)
        far = bias(head, distance + BLOCK, 9)
        scores = dot_nt(hid_s[long_rows, head_cols(2, head)], hid_s[long_rows, head_cols(3, head)])
        long_att_s[head, low, high] = jnp.zeros((BLOCK, BLOCK), BF16)
        long_ds_s[head, low, high] = jnp.zeros((BLOCK, BLOCK), BF16)
        for tile, (i, j, pairs) in enumerate(long_tiles):
            a, slope = weigh(scores[i, j], far if tile == 2 else near[head], allowed[pairs])
            long_att_s[head, i, j] = a
            long_slope_s[head, tile] = slope
        ctx_s[long_rows, head_cols(0, head)] = dot(
            long_att_s[head], hid_s[long_rows, head_cols(1, head)]
        )

    def short_attend(head):
        for i in (2, 3):
            rows = slice(i * BLOCK, (i + 1) * BLOCK)
            scores = dot_nt(hid_s[rows, head_cols(2, head)], hid_s[rows, head_cols(3, head)])
            a, slope = weigh(scores, near[head], allowed[i])
            short_att_s[head, i - 2] = a
            short_slope_s[head, i - 2] = slope
            ctx_s[rows, head_cols(0, head)] = dot(a, hid_s[rows, head_cols(1, head)])

    def upstream(i):
        kept = jnp.where(
            live_column(length_ref, order, i), cot_ref[block_rows(order, i), :].astype(F32), 0.0
        )
        up_ref[i * BLOCK : (i + 1) * BLOCK, :] = kept.astype(BF16)

    def middle(r):
        sl = slice(r, r + 64)
        n, rstd = normalized(ctx_s[sl, :])
        u = hid_s[sl, 0:D].astype(F32)
        mixed_ref[sl, :] = (n * u).astype(BF16)
        gm = gm_s[sl, :]
        gh_ref[sl, 0:D] = (gm * n * slope_s[sl, 0:D]).astype(BF16)
        gctx_s[sl, :] = normalized_back(gm * u, n, rstd).astype(BF16)

    def output(rows):
        product = dot(mixed_ref[rows, :], w_out_ref[...])
        for i in range(rows.start // BLOCK, rows.stop // BLOCK):
            here = slice(i * BLOCK, (i + 1) * BLOCK)
            there = slice(here.start - rows.start, here.stop - rows.start)
            value = bal_ref[here, :].astype(F32) + product[there, :]
            value = jnp.where(live_column(length_ref, order, i), value, 0.0)
            out_s[block_rows(order, i), :] = value.astype(BF16)

    def finish_grads(rows, head, gv, gq, gk):
        for part, grad in ((1, gv), (2, gq * SCALE), (3, gk * SCALE)):
            cols = head_cols(part, head)
            gh_ref[rows, cols] = (grad * slope_s[rows, cols]).astype(BF16)

    def long_back(head):
        gc = gctx_s[long_rows, head_cols(0, head)]
        grads = dot_nt(gc, hid_s[long_rows, head_cols(1, head)])
        for tile, (i, j, _) in enumerate(long_tiles):
            long_ds_s[head, i, j] = (grads[i, j] * long_slope_s[head, tile]).astype(BF16)
        ds = long_ds_s[head]
        finish_grads(
            long_rows,
            head,
            dot_tn(long_att_s[head], gc),
            dot(ds, hid_s[long_rows, head_cols(3, head)]),
            dot_tn(ds, hid_s[long_rows, head_cols(2, head)]),
        )

    def short_back(head):
        for i in (2, 3):
            rows = slice(i * BLOCK, (i + 1) * BLOCK)
            gc = gctx_s[rows, head_cols(0, head)]
            grads = dot_nt(gc, hid_s[rows, head_cols(1, head)])
            ds = (grads * short_slope_s[head, i - 2]).astype(BF16)
            finish_grads(
                rows,
                head,
                dot_tn(short_att_s[head, i - 2], gc),
                dot(ds, hid_s[rows, head_cols(3, head)]),
                dot_tn(ds, hid_s[rows, head_cols(2, head)]),
            )

    parts = (1024, 1536, 1280, 1792, 512, 768, 0, 256)
    gather(long_rows)
    gather(short_rows)
    for r in range(0, 256, 64):
        norm(r)
    for k, n in enumerate(parts):
        project(long_rows, n)
        if k < 4:
            norm(256 + 64 * k)
    for i in range(BLOCKS):
        upstream(i)
    gm_s[...] = dot_nt(up_ref[...], w_out_ref[...])
    for k, n in enumerate(parts):
        if k % 2 == 0:
            long_attend(k // 2)
        project(short_rows, n)
    for head in range(HEADS):
        middle(64 * head)
        short_attend(head)
    trans_s[0] = norm_s[...].T
    output(long_rows)
    for head in range(HEADS):
        long_back(head)
        middle(256 + 64 * head)
    trans_s[1] = mixed_ref[...].T
    output(short_rows)
    out_copy = pltpu.make_async_copy(out_s, out_hbm, sem)
    out_copy.start()
    for head in range(HEADS):
        short_back(head)

    own_rows = pl.ds(pl.multiple_of(core * HALF, HALF), HALF)
    other_rows = pl.ds(pl.multiple_of((1 - core) * HALF, HALF), HALF)
    left_ref[0] = trans_s[0, own_rows, :]
    left_ref[1] = trans_s[1, own_rows, :]

    def store(at, value):
        other_ref[at] = value.astype(BF16)

    weight_grads(trans_s[0, other_rows, :], trans_s[1, other_rows, :], gh_ref, up_ref, store)
    out_copy.wait()


def weight_grads(normed_t, mixed_t, gh_ref, up_ref, store):
    for at in range(0, HID + D, 256):
        if at < HID:
            value = dot(normed_t, gh_ref[:, at : at + 256])
        else:
            value = dot(mixed_t, up_ref[:, at - HID : at - HID + 256])
        for n in (0, 128):
            side, start = (at + n) // CHUNK, (at + n) % CHUNK
            shares = value[:, n : n + 128].reshape(HALF // PIECE, PIECE, 128)
            store((slice(None), side, slice(None), slice(start, start + 128)), shares)


def beside_kernel(
    offset_ref,
    arrived_ref,
    left_ref,
    up_ref,
    gh_ref,
    bal_ref,
    w_in_ref,
    own_ref,
    back_ref,
    gx_s,
    gb_s,
    place_s,
):
    gx_s[...] = dot_nt(gh_ref[...], w_in_ref[...])

    def store(at, value):
        own_ref[at] = value.astype(BF16)

    weight_grads(left_ref[0], left_ref[1], gh_ref, up_ref, store)
    for r in range(0, ROWS, 64):
        sl = slice(r, r + 64)
        hat, rstd = normalized(bal_ref[sl, :].astype(F32))
        grad = normalized_back(gx_s[sl, :], hat, rstd)
        gb_s[sl, :] = (up_ref[sl, :].astype(F32) + grad).astype(BF16)
    goals = inner_goals(cell_goals(arrived_ref), block_order(offset_ref))
    for b in range(BLOCKS):
        row = lax.broadcasted_iota(jnp.int32, (1, BLOCK), 1).astype(F32) + float(b * BLOCK)
        place_s[:, b * BLOCK : (b + 1) * BLOCK] = jnp.where(goals == row, 1.0, 0.0).astype(BF16)
    for n in range(0, D, 256):
        back_ref[:, n : n + 256] = dot(place_s[...], gb_s[:, n : n + 256]).astype(BF16)


def beside(offsets, arrived, left, up, gh, bal, w_in):
    return pl.pallas_call(
        beside_kernel,
        out_shape=(
            jax.ShapeDtypeStruct(SHARES, BF16),
            jax.ShapeDtypeStruct((MEMBERS * PIECE, D), BF16),
        ),
        in_specs=[full_spec(pltpu.SMEM)] + [full_spec()] * 6,
        out_specs=(full_spec(),) * 2,
        scratch_shapes=[
            pltpu.VMEM((ROWS, D), F32),
            pltpu.VMEM((ROWS, D), BF16),
            pltpu.VMEM((MEMBERS * PIECE, ROWS), BF16),
        ],
        compiler_params=pltpu.CompilerParams(vmem_limit_bytes=VMEM_SMALL),
        cost_estimate=pl.CostEstimate(
            flops=3_000_000_000, bytes_accessed=2_000_000, transcendentals=1_000
        ),
        name="beside",
    )(offsets, arrived, left, up, gh, bal, w_in)


def join_kernel(own_ref, got_ref, out_ref):
    out_ref[...] = (own_ref[...].astype(F32) + got_ref[...].astype(F32)).astype(BF16)


def join(own, got):
    return pl.pallas_call(
        join_kernel,
        out_shape=jax.ShapeDtypeStruct(SHARES, BF16),
        in_specs=[full_spec()] * 2,
        out_specs=full_spec(),
        compiler_params=pltpu.CompilerParams(vmem_limit_bytes=VMEM_SMALL),
        cost_estimate=pl.CostEstimate(flops=1_000_000, bytes_accessed=4_000_000, transcendentals=0),
        name="join",
    )(own, got)


def layer(offsets, lengths, rab, arrived, cotangent, w_in, w_out):
    scratch = [
        ((ROWS, MEMBERS * PIECE), BF16),
        ((ROWS, D), BF16),
        ((ROWS, HID), BF16),
        ((ROWS, HID), F32),
        ((HEADS, 2 * BLOCK, 2 * BLOCK), BF16),
        ((HEADS, 2 * BLOCK, 2 * BLOCK), BF16),
        ((HEADS, 3, BLOCK, BLOCK), F32),
        ((HEADS, 2, BLOCK, BLOCK), BF16),
        ((HEADS, 2, BLOCK, BLOCK), F32),
        ((ROWS, D), F32),
        ((ROWS, D), F32),
        ((ROWS, D), BF16),
        ((2, D, ROWS), BF16),
        ((ROWS, D), BF16),
        ((ROWS, D), BF16),
    ]
    rows = jax.ShapeDtypeStruct((ROWS, D), BF16)
    return pl.pallas_call(
        layer_kernel,
        out_shape=(
            jax.ShapeDtypeStruct(SHARES, BF16),
            jax.ShapeDtypeStruct((2, HALF, ROWS), BF16),
            rows,
            jax.ShapeDtypeStruct((ROWS, HID), BF16),
            rows,
            pltpu.HBM((ROWS, D), BF16),
        ),
        in_specs=[full_spec(pltpu.SMEM)] * 3 + [full_spec()] * 4,
        out_specs=(full_spec(),) * 5 + (full_spec(pltpu.HBM),),
        scratch_shapes=[pltpu.VMEM(shape, kind) for shape, kind in scratch]
        + [pltpu.SemaphoreType.DMA],
        compiler_params=pltpu.CompilerParams(vmem_limit_bytes=VMEM_LIMIT),
        cost_estimate=pl.CostEstimate(
            flops=4_000_000_000, bytes_accessed=9_000_000, transcendentals=1_500_000
        ),
        name="layer",
    )(offsets, lengths, rab, arrived, cotangent, w_in, w_out)


def total_kernel(received_ref, back_ref, out_ref):
    total = received_ref[0].astype(F32)
    for m in range(1, MEMBERS):
        total += received_ref[m].astype(F32)
    total = (total * (1.0 / 256.0)).astype(BF16)
    out_ref[:, :, :CHUNK] = jnp.broadcast_to(total[None], (MEMBERS, PIECE, CHUNK))
    out_ref[:, :, CHUNK:] = back_ref[...]


def total(received, back):
    return pl.pallas_call(
        total_kernel,
        out_shape=jax.ShapeDtypeStruct((MEMBERS, PIECE, CHUNK + D), BF16),
        in_specs=[full_spec()] * 2,
        out_specs=full_spec(),
        compiler_params=pltpu.CompilerParams(vmem_limit_bytes=VMEM_SMALL),
        cost_estimate=pl.CostEstimate(flops=1_000_000, bytes_accessed=4_000_000, transcendentals=0),
        name="total",
    )(received, back)


def put_shares(source, rows_s, groups):
    for side in range(4):
        at = side * CHUNK
        for g in groups:
            value = source[g, side, :, :CHUNK].astype(F32)
            rows_s[g * PIECE : (g + 1) * PIECE, at : at + CHUNK] = value


def put_rows(rows_s, half, w_in_hbm, w_out_hbm, sems, source):
    copies = []
    parts = 4
    height = HALF // parts
    for part in range(parts):
        put_shares(source, rows_s, range(part * height // PIECE, (part + 1) * height // PIECE))
        here = slice(part * height, (part + 1) * height)
        there = pl.ds(pl.multiple_of(half * HALF + part * height, height), height)
        for n, copy in enumerate(
            (
                (rows_s.at[here, :HID], w_in_hbm.at[there]),
                (rows_s.at[here, HID:], w_out_hbm.at[there]),
            )
        ):
            copies.append(pltpu.make_async_copy(*copy, sems.at[2 * part + n]))
            copies[-1].start()
    return copies


def mine_kernel(
    route_hbm, received_ref, events_hbm, w_in_hbm, w_out_hbm, route_s, rows_s, events_s, sems
):
    load = pltpu.make_async_copy(route_hbm, route_s, sems.at[9])
    load.start()
    copies = put_rows(
        rows_s, lax.axis_index("group"), w_in_hbm, w_out_hbm, sems, received_ref
    )
    load.wait()
    for j in range(PIECES):
        slot = lax.shift_right_logical(route_s[j], 5)
        piece = received_ref[lax.shift_right_logical(slot, 2), lax.bitwise_and(slot, 3)]
        events_s[j * PIECE : (j + 1) * PIECE, :] = piece[:, CHUNK:]
    copies.append(pltpu.make_async_copy(events_s, events_hbm, sems.at[8]))
    copies[-1].start()
    for copy in copies:
        copy.wait()


def mine_out(route, received):
    return pl.pallas_call(
        mine_kernel,
        out_shape=(
            jax.ShapeDtypeStruct((ROWS, D), BF16),
            jax.ShapeDtypeStruct((D, HID), F32),
            jax.ShapeDtypeStruct((D, D), F32),
        ),
        in_specs=[full_spec(pltpu.HBM), full_spec()],
        out_specs=(full_spec(pltpu.HBM),) * 3,
        scratch_shapes=[
            pltpu.SMEM((PIECES,), jnp.int32),
            pltpu.VMEM((HALF, HID + D), F32),
            pltpu.VMEM((ROWS, D), BF16),
            pltpu.SemaphoreType.DMA((10,)),
        ],
        compiler_params=pltpu.CompilerParams(vmem_limit_bytes=VMEM_SMALL),
        cost_estimate=pl.CostEstimate(flops=0, bytes_accessed=6_000_000, transcendentals=0),
        name="mine_out",
    )(in_hbm(route), received)


def theirs_kernel(theirs_ref, _, __, w_in_hbm, w_out_hbm, rows_s, sems):
    for copy in put_rows(rows_s, 1 - lax.axis_index("group"), w_in_hbm, w_out_hbm, sems, theirs_ref):
        copy.wait()


def theirs_out(theirs, w_in_grad, w_out_grad):
    return pl.pallas_call(
        theirs_kernel,
        out_shape=(
            jax.ShapeDtypeStruct((D, HID), F32),
            jax.ShapeDtypeStruct((D, D), F32),
        ),
        in_specs=[full_spec()] + [full_spec(pltpu.HBM)] * 2,
        out_specs=(full_spec(pltpu.HBM),) * 2,
        scratch_shapes=[
            pltpu.VMEM((HALF, HID + D), F32),
            pltpu.SemaphoreType.DMA((8,)),
        ],
        input_output_aliases={1: 0, 2: 1},
        compiler_params=pltpu.CompilerParams(vmem_limit_bytes=VMEM_SMALL),
        cost_estimate=pl.CostEstimate(flops=0, bytes_accessed=4_000_000, transcendentals=0),
        name="theirs_out",
    )(theirs, w_in_grad, w_out_grad)


def body(events, route, block_offset, hist_length, cotangent, w_in, w_out, rab):
    exchange = functools.partial(
        lax.all_to_all, axis_name="member", split_axis=0, concat_axis=0, tiled=True
    )
    swap = functools.partial(lax.ppermute, axis_name="group", perm=[(0, 1), (1, 0)])
    arrived = exchange(pack(route, events))
    other, left, up, gh, bal, outputs = layer(
        block_offset, hist_length, rab, arrived, cotangent, w_in, w_out
    )
    got = swap(other)
    own, back = beside(block_offset, arrived, left, up, gh, bal, w_in)
    received = exchange(join(own, got).reshape(MEMBERS, PIECE, CHUNK))
    received = exchange(total(received, back.reshape(MEMBERS, PIECE, D)))
    theirs = swap(received[:, :, :CHUNK])
    events_grad, w_in_grad, w_out_grad = mine_out(
        route, received.reshape(*SHARES[:3], CHUNK + D)
    )
    w_in_grad, w_out_grad = theirs_out(theirs.reshape(SHARES), w_in_grad, w_out_grad)
    return outputs, events_grad, w_in_grad, w_out_grad


def solution(mesh):
    placed = (
        P(("group", "member"), None),
        P(("group", "member")),
        P(("group", "member")),
        P(("group", "member")),
        P(("group", "member"), None),
        P(),
        P(),
        P(),
    )
    return jax.shard_map(
        body,
        mesh=mesh,
        in_specs=placed,
        out_specs=(P(("group", "member"), None), P(("group", "member"), None), P(), P()),
        check_vma=False,
    )
```

```python
import functools
import math

import jax
import jax.numpy as jnp
from jax import lax
from jax.experimental import pallas as pl
from jax.experimental.pallas import tpu as pltpu
from jax.sharding import PartitionSpec as P

EPS = 1e-05
BF16 = jnp.bfloat16
F32 = jnp.float32
VMEM_LIMIT = 32 * 1024 * 1024
VMEM_SMALL = 16 * 1024 * 1024

ROWS, D, HID = 512, 512, 2048
BLOCK, BLOCKS, HEADS, BUCKETS = 128, 4, 4, 12
PIECE, PIECES, MEMBERS = 16, 32, 64
SLOT = 72
CHUNK = 640
SCALE = 1.0 / math.sqrt(128)
HALF = D // 2
SHARES = (HALF // PIECE, 4, PIECE, CHUNK)


def dot(a, b):
    return jnp.dot(a, b, preferred_element_type=F32)


def dot_nt(a, b):
    return lax.dot_general(a, b, (((1,), (1,)), ((), ())), preferred_element_type=F32)


def dot_tn(a, b):
    return lax.dot_general(a, b, (((0,), (0,)), ((), ())), preferred_element_type=F32)


def sigmoid(v):
    return 0.5 * jnp.tanh(0.5 * v) + 0.5


def in_hbm(array):
    return pltpu.with_memory_space_constraint(array, pltpu.HBM)


def full_spec(memory=pltpu.VMEM):
    return pl.BlockSpec(memory_space=memory)


def pack_kernel(route_hbm, events_hbm, out_ref, route_s, events_s, sems):
    half = ROWS // 2
    loads = [pltpu.make_async_copy(route_hbm, route_s, sems.at[0])]
    for n in range(2):
        rows = pl.ds(n * half, half)
        loads.append(
            pltpu.make_async_copy(events_hbm.at[rows], events_s.at[rows], sems.at[1 + n])
        )
    for load in loads:
        load.start()
    out_ref[...] = jnp.zeros_like(out_ref)
    for load in loads:
        load.wait()
    for j in range(PIECES):
        target = route_s[j]
        device = lax.shift_right_logical(target, 5)
        place = lax.bitwise_and(target, PIECES - 1)
        for k in range(D // 128):
            out_ref[device, k * PIECE : (k + 1) * PIECE, :] = events_s[
                j * PIECE : (j + 1) * PIECE, k * 128 : (k + 1) * 128
            ]
        label = jnp.full((SLOT - 4 * PIECE, 128), (place + 1).astype(F32), F32)
        out_ref[device, 4 * PIECE :, :] = label.astype(BF16)


def pack(route, events):
    return pl.pallas_call(
        pack_kernel,
        out_shape=jax.ShapeDtypeStruct((MEMBERS, SLOT, 128), BF16),
        in_specs=[full_spec(pltpu.HBM)] * 2,
        out_specs=full_spec(),
        scratch_shapes=[
            pltpu.SMEM((PIECES,), jnp.int32),
            pltpu.VMEM((ROWS, D), BF16),
            pltpu.SemaphoreType.DMA((3,)),
        ],
        compiler_params=pltpu.CompilerParams(vmem_limit_bytes=VMEM_SMALL),
        name="pack_pieces",
    )(in_hbm(route), in_hbm(events))


def cell_goals(arrived_ref):
    labels = arrived_ref[:, 4 * PIECE :, :].astype(F32)
    if labels.shape[1] < PIECE:
        labels = jnp.concatenate([labels, labels], axis=1)
    within = lax.broadcasted_iota(jnp.int32, labels.shape, 1).astype(F32)
    return ((labels - 1.0) * PIECE + within).reshape(MEMBERS * PIECE, 128)


def block_order(offset_ref):
    second = jnp.int32(1)
    for b in range(2, BLOCKS):
        second = jnp.where(offset_ref[b] == 1, b, second)
    return (
        second - 1,
        second,
        jnp.where(second == 1, 2, 0),
        jnp.where(second == 3, 1, 3),
    )


def block_rows(order, i):
    return pl.ds(pl.multiple_of(order[i] * BLOCK, BLOCK), BLOCK)


def inner_goals(goals, order):
    block = jnp.floor(goals * (1.0 / BLOCK))
    moved = goals
    for i in range(BLOCKS):
        at = order[i].astype(F32)
        moved = jnp.where(block == at, goals + (float(i) - at) * BLOCK, moved)
    return moved


def live_column(length_ref, order, i):
    first = BLOCK if i == 1 else 0
    return lax.broadcasted_iota(jnp.int32, (BLOCK, 1), 0) + first < length_ref[order[i]]


def normalized(x):
    centered = x - jnp.mean(x, axis=-1, keepdims=True)
    variance = jnp.mean(centered * centered, axis=-1, keepdims=True)
    rstd = lax.rsqrt(variance + EPS)
    return centered * rstd, rstd


def normalized_back(grad, hat, rstd):
    return rstd * (
        grad
        - jnp.mean(grad, axis=-1, keepdims=True)
        - hat * jnp.mean(grad * hat, axis=-1, keepdims=True)
    )


def head_cols(part, head):
    return slice(part * D + head * 128, part * D + head * 128 + 128)


def layer_kernel(
    offset_ref,
    length_ref,
    rab_ref,
    arrived_ref,
    cot_ref,
    w_in_ref,
    w_out_ref,
    other_ref,
    left_ref,
    up_ref,
    gh_ref,
    bal_ref,
    mixed_ref,
    place_s,
    norm_s,
    hid_s,
    slope_s,
    long_att_s,
    long_ds_s,
    long_slope_s,
    short_att_s,
    short_slope_s,
    ctx_s,
    gm_s,
    gctx_s,
    trans_s,
):
    core = lax.axis_index("group")
    order = block_order(offset_ref)
    long_rows, short_rows = slice(0, 2 * BLOCK), slice(2 * BLOCK, 4 * BLOCK)

    tens = jnp.floor(cell_goals(arrived_ref) * (1.0 / PIECE)).astype(BF16)
    pick = (lax.broadcasted_iota(jnp.int32, (8, 128), 1) == 0).astype(BF16)
    ones = lax.bitwise_and(
        lax.broadcasted_iota(jnp.int32, (1, MEMBERS * PIECE), 1), PIECE - 1
    ).astype(F32)
    goal = inner_goals(dot_nt(pick, tens)[0:1, :] * PIECE + ones, order)

    def gather(rows):
        for r in range(rows.start, rows.stop, BLOCK):
            row = lax.broadcasted_iota(jnp.int32, (BLOCK, 1), 0).astype(F32) + float(r)
            place_s[r : r + BLOCK, :] = jnp.where(goal == row, 1.0, 0.0).astype(BF16)
        for k in range(0, D // 128, 2):
            cells = jnp.concatenate(
                [
                    arrived_ref[:, n * PIECE : (n + 1) * PIECE, :].reshape(MEMBERS * PIECE, 128)
                    for n in (k, k + 1)
                ],
                axis=1,
            )
            bal_ref[rows, k * 128 : k * 128 + 256] = dot(place_s[rows, :], cells).astype(BF16)

    def norm(r):
        sl = slice(r, r + 64)
        norm_s[sl, :] = normalized(bal_ref[sl, :].astype(F32))[0].astype(BF16)

    def project(rows, n):
        cols = slice(n, n + 256)
        v = dot(norm_s[rows, :], w_in_ref[:, cols])
        g = sigmoid(v)
        h = v * g
        hid_s[rows, cols] = h.astype(BF16)
        slope_s[rows, cols] = g + h * (1.0 - g)

    row_id = lax.broadcasted_iota(jnp.int32, (BLOCK, BLOCK), 0)
    col_id = lax.broadcasted_iota(jnp.int32, (BLOCK, BLOCK), 1)
    distance = row_id - col_id
    near_pairs = distance >= 0

    def bias(head, apart, buckets):
        total = jnp.full((BLOCK, BLOCK), rab_ref[head, 0], F32)
        for bucket in range(1, buckets):
            total = jnp.where(apart >= 2 ** (bucket - 1), rab_ref[head, bucket], total)
        return total

    def weigh(scores, relative, allowed):
        s = scores * SCALE + relative
        g = sigmoid(s)
        a = s * g
        return (
            jnp.where(allowed, a, 0.0).astype(BF16),
            jnp.where(allowed, g + a * (1.0 - g), 0.0),
        )

    def live_rows(i):
        return row_id + (BLOCK if i == 1 else 0) < length_ref[order[i]]

    allowed = [near_pairs & live_rows(i) for i in range(BLOCKS)] + [live_rows(1)]
    near = [None] * HEADS
    low, high = slice(0, BLOCK), slice(BLOCK, 2 * BLOCK)
    long_tiles = ((low, low, 0), (high, high, 1), (high, low, BLOCKS))

    def long_attend(head):
        near[head] = bias(head, distance, 8)
        far = bias(head, distance + BLOCK, 9)
        scores = dot_nt(hid_s[long_rows, head_cols(2, head)], hid_s[long_rows, head_cols(3, head)])
        long_att_s[head, low, high] = jnp.zeros((BLOCK, BLOCK), BF16)
        long_ds_s[head, low, high] = jnp.zeros((BLOCK, BLOCK), BF16)
        for tile, (i, j, pairs) in enumerate(long_tiles):
            a, slope = weigh(scores[i, j], far if tile == 2 else near[head], allowed[pairs])
            long_att_s[head, i, j] = a
            long_slope_s[head, tile] = slope
        ctx_s[long_rows, head_cols(0, head)] = dot(
            long_att_s[head], hid_s[long_rows, head_cols(1, head)]
        )

    def short_attend(head):
        for i in (2, 3):
            rows = slice(i * BLOCK, (i + 1) * BLOCK)
            scores = dot_nt(hid_s[rows, head_cols(2, head)], hid_s[rows, head_cols(3, head)])
            a, slope = weigh(scores, near[head], allowed[i])
            short_att_s[head, i - 2] = a
            short_slope_s[head, i - 2] = slope
            ctx_s[rows, head_cols(0, head)] = dot(a, hid_s[rows, head_cols(1, head)])

    def upstream(i):
        kept = jnp.where(
            live_column(length_ref, order, i), cot_ref[block_rows(order, i), :].astype(F32), 0.0
        )
        up_ref[i * BLOCK : (i + 1) * BLOCK, :] = kept.astype(BF16)

    def middle(r):
        sl = slice(r, r + 64)
        n, rstd = normalized(ctx_s[sl, :])
        u = hid_s[sl, 0:D].astype(F32)
        mixed_ref[sl, :] = (n * u).astype(BF16)
        gm = gm_s[sl, :]
        gh_ref[sl, 0:D] = (gm * n * slope_s[sl, 0:D]).astype(BF16)
        gctx_s[sl, :] = normalized_back(gm * u, n, rstd).astype(BF16)

    def finish_grads(rows, head, gv, gq, gk):
        for part, grad in ((1, gv), (2, gq * SCALE), (3, gk * SCALE)):
            cols = head_cols(part, head)
            gh_ref[rows, cols] = (grad * slope_s[rows, cols]).astype(BF16)

    def long_back(head):
        gc = gctx_s[long_rows, head_cols(0, head)]
        grads = dot_nt(gc, hid_s[long_rows, head_cols(1, head)])
        for tile, (i, j, _) in enumerate(long_tiles):
            long_ds_s[head, i, j] = (grads[i, j] * long_slope_s[head, tile]).astype(BF16)
        ds = long_ds_s[head]
        finish_grads(
            long_rows,
            head,
            dot_tn(long_att_s[head], gc),
            dot(ds, hid_s[long_rows, head_cols(3, head)]),
            dot_tn(ds, hid_s[long_rows, head_cols(2, head)]),
        )

    def short_back(head):
        for i in (2, 3):
            rows = slice(i * BLOCK, (i + 1) * BLOCK)
            gc = gctx_s[rows, head_cols(0, head)]
            grads = dot_nt(gc, hid_s[rows, head_cols(1, head)])
            ds = (grads * short_slope_s[head, i - 2]).astype(BF16)
            finish_grads(
                rows,
                head,
                dot_tn(short_att_s[head, i - 2], gc),
                dot(ds, hid_s[rows, head_cols(3, head)]),
                dot_tn(ds, hid_s[rows, head_cols(2, head)]),
            )

    parts = (1024, 1536, 1280, 1792, 512, 768, 0, 256)
    gather(long_rows)
    gather(short_rows)
    for r in range(0, 256, 64):
        norm(r)
    for k, n in enumerate(parts):
        project(long_rows, n)
        if k < 4:
            norm(256 + 64 * k)
    for i in range(BLOCKS):
        upstream(i)
    gm_s[...] = dot_nt(up_ref[...], w_out_ref[...])
    for k, n in enumerate(parts):
        if k % 2 == 0:
            long_attend(k // 2)
        project(short_rows, n)
    for head in range(HEADS):
        middle(64 * head)
        short_attend(head)
    trans_s[0] = norm_s[...].T
    for head in range(HEADS):
        long_back(head)
        middle(256 + 64 * head)
    trans_s[1] = mixed_ref[...].T
    for head in range(HEADS):
        short_back(head)

    own_rows = pl.ds(pl.multiple_of(core * HALF, HALF), HALF)
    other_rows = pl.ds(pl.multiple_of((1 - core) * HALF, HALF), HALF)
    left_ref[0] = trans_s[0, own_rows, :]
    left_ref[1] = trans_s[1, own_rows, :]

    def store(at, value):
        other_ref[at] = value.astype(BF16)

    weight_grads(trans_s[0, other_rows, :], trans_s[1, other_rows, :], gh_ref, up_ref, store)


def weight_grads(normed_t, mixed_t, gh_ref, up_ref, store):
    for at in range(0, HID + D, 256):
        if at < HID:
            value = dot(normed_t, gh_ref[:, at : at + 256])
        else:
            value = dot(mixed_t, up_ref[:, at - HID : at - HID + 256])
        for n in (0, 128):
            side, start = (at + n) // CHUNK, (at + n) % CHUNK
            shares = value[:, n : n + 128].reshape(HALF // PIECE, PIECE, 128)
            store((slice(None), side, slice(None), slice(start, start + 128)), shares)


def beside_kernel(
    offset_ref,
    arrived_ref,
    left_ref,
    up_ref,
    gh_ref,
    bal_ref,
    w_in_ref,
    own_ref,
    back_ref,
    gx_s,
    gb_s,
    place_s,
):
    gx_s[...] = dot_nt(gh_ref[...], w_in_ref[...])

    def store(at, value):
        own_ref[at] = value.astype(BF16)

    weight_grads(left_ref[0], left_ref[1], gh_ref, up_ref, store)
    for r in range(0, ROWS, 64):
        sl = slice(r, r + 64)
        hat, rstd = normalized(bal_ref[sl, :].astype(F32))
        grad = normalized_back(gx_s[sl, :], hat, rstd)
        gb_s[sl, :] = (up_ref[sl, :].astype(F32) + grad).astype(BF16)
    goals = inner_goals(cell_goals(arrived_ref), block_order(offset_ref))
    for b in range(BLOCKS):
        row = lax.broadcasted_iota(jnp.int32, (1, BLOCK), 1).astype(F32) + float(b * BLOCK)
        place_s[:, b * BLOCK : (b + 1) * BLOCK] = jnp.where(goals == row, 1.0, 0.0).astype(BF16)
    for n in range(0, D, 256):
        back_ref[:, n : n + 256] = dot(place_s[...], gb_s[:, n : n + 256]).astype(BF16)


def beside(offsets, arrived, left, up, gh, bal, w_in):
    return pl.pallas_call(
        beside_kernel,
        out_shape=(
            jax.ShapeDtypeStruct(SHARES, BF16),
            jax.ShapeDtypeStruct((MEMBERS * PIECE, D), BF16),
        ),
        in_specs=[full_spec(pltpu.SMEM)] + [full_spec()] * 6,
        out_specs=(full_spec(),) * 2,
        scratch_shapes=[
            pltpu.VMEM((ROWS, D), F32),
            pltpu.VMEM((ROWS, D), BF16),
            pltpu.VMEM((MEMBERS * PIECE, ROWS), BF16),
        ],
        compiler_params=pltpu.CompilerParams(vmem_limit_bytes=VMEM_SMALL),
        cost_estimate=pl.CostEstimate(
            flops=3_000_000_000, bytes_accessed=2_000_000, transcendentals=1_000
        ),
        name="beside",
    )(offsets, arrived, left, up, gh, bal, w_in)


def join_kernel(own_ref, got_ref, out_ref):
    out_ref[...] = (own_ref[...].astype(F32) + got_ref[...].astype(F32)).astype(BF16)


def join(own, got):
    return pl.pallas_call(
        join_kernel,
        out_shape=jax.ShapeDtypeStruct(SHARES, BF16),
        in_specs=[full_spec()] * 2,
        out_specs=full_spec(),
        compiler_params=pltpu.CompilerParams(vmem_limit_bytes=VMEM_SMALL),
        cost_estimate=pl.CostEstimate(flops=1_000_000, bytes_accessed=4_000_000, transcendentals=0),
        name="join",
    )(own, got)


def layer(offsets, lengths, rab, arrived, cotangent, w_in, w_out):
    scratch = [
        ((ROWS, MEMBERS * PIECE), BF16),
        ((ROWS, D), BF16),
        ((ROWS, HID), BF16),
        ((ROWS, HID), F32),
        ((HEADS, 2 * BLOCK, 2 * BLOCK), BF16),
        ((HEADS, 2 * BLOCK, 2 * BLOCK), BF16),
        ((HEADS, 3, BLOCK, BLOCK), F32),
        ((HEADS, 2, BLOCK, BLOCK), BF16),
        ((HEADS, 2, BLOCK, BLOCK), F32),
        ((ROWS, D), F32),
        ((ROWS, D), F32),
        ((ROWS, D), BF16),
        ((2, D, ROWS), BF16),
    ]
    rows = jax.ShapeDtypeStruct((ROWS, D), BF16)
    return pl.pallas_call(
        layer_kernel,
        out_shape=(
            jax.ShapeDtypeStruct(SHARES, BF16),
            jax.ShapeDtypeStruct((2, HALF, ROWS), BF16),
            rows,
            jax.ShapeDtypeStruct((ROWS, HID), BF16),
            rows,
            rows,
        ),
        in_specs=[full_spec(pltpu.SMEM)] * 3 + [full_spec()] * 4,
        out_specs=(full_spec(),) * 6,
        scratch_shapes=[pltpu.VMEM(shape, kind) for shape, kind in scratch],
        compiler_params=pltpu.CompilerParams(vmem_limit_bytes=VMEM_LIMIT),
        cost_estimate=pl.CostEstimate(
            flops=4_000_000_000, bytes_accessed=9_000_000, transcendentals=1_500_000
        ),
        name="layer",
    )(offsets, lengths, rab, arrived, cotangent, w_in, w_out)


def total_kernel(received_ref, back_ref, out_ref):
    total = received_ref[0].astype(F32)
    for m in range(1, MEMBERS):
        total += received_ref[m].astype(F32)
    total = (total * (1.0 / 256.0)).astype(BF16)
    out_ref[:, :, :CHUNK] = jnp.broadcast_to(total[None], (MEMBERS, PIECE, CHUNK))
    out_ref[:, :, CHUNK:] = back_ref[...]


def total(received, back):
    return pl.pallas_call(
        total_kernel,
        out_shape=jax.ShapeDtypeStruct((MEMBERS, PIECE, CHUNK + D), BF16),
        in_specs=[full_spec()] * 2,
        out_specs=full_spec(),
        compiler_params=pltpu.CompilerParams(vmem_limit_bytes=VMEM_SMALL),
        cost_estimate=pl.CostEstimate(flops=1_000_000, bytes_accessed=4_000_000, transcendentals=0),
        name="total",
    )(received, back)


def put_shares(source, rows_s, groups):
    for side in range(4):
        at = side * CHUNK
        for g in groups:
            value = source[g, side, :, :CHUNK].astype(F32)
            rows_s[g * PIECE : (g + 1) * PIECE, at : at + CHUNK] = value


def put_rows(rows_s, first, w_in_hbm, w_out_hbm, sems, source):
    copies = []
    height = 64
    parts = rows_s.shape[0] // height
    for part in range(parts):
        put_shares(source, rows_s, range(part * height // PIECE, (part + 1) * height // PIECE))
        here = slice(part * height, (part + 1) * height)
        there = pl.ds(pl.multiple_of(first + part * height, height), height)
        for n, copy in enumerate(
            (
                (rows_s.at[here, :HID], w_in_hbm.at[there]),
                (rows_s.at[here, HID:], w_out_hbm.at[there]),
            )
        ):
            copies.append(pltpu.make_async_copy(*copy, sems.at[2 * part + n]))
            copies[-1].start()
    return copies


def mine_kernel(
    route_hbm,
    offset_ref,
    length_ref,
    received_ref,
    bal_ref,
    mixed_ref,
    w_out_ref,
    events_hbm,
    w_in_grad_hbm,
    w_out_grad_hbm,
    out_hbm,
    route_s,
    rows_s,
    events_s,
    product_s,
    out_s,
    sems,
):
    load = pltpu.make_async_copy(route_hbm, route_s, sems.at[9])
    load.start()
    product_s[...] = dot(mixed_ref[...], w_out_ref[...])
    order = block_order(offset_ref)
    for i in range(BLOCKS):
        rows = slice(i * BLOCK, (i + 1) * BLOCK)
        value = bal_ref[rows, :].astype(F32) + product_s[rows, :]
        value = jnp.where(live_column(length_ref, order, i), value, 0.0)
        out_s[block_rows(order, i), :] = value.astype(BF16)
    copies = [pltpu.make_async_copy(out_s, out_hbm, sems.at[10])]
    copies[0].start()
    copies += put_rows(
        rows_s, lax.axis_index("group") * HALF, w_in_grad_hbm, w_out_grad_hbm, sems, received_ref
    )
    load.wait()
    for j in range(PIECES):
        slot = lax.shift_right_logical(route_s[j], 5)
        piece = received_ref[lax.shift_right_logical(slot, 2), lax.bitwise_and(slot, 3)]
        events_s[j * PIECE : (j + 1) * PIECE, :] = piece[:, CHUNK:]
    copies.append(pltpu.make_async_copy(events_s, events_hbm, sems.at[8]))
    copies[-1].start()
    for copy in copies:
        copy.wait()


def mine_out(route, offsets, lengths, received, bal, mixed, w_out):
    rows = (ROWS, D)
    return pl.pallas_call(
        mine_kernel,
        out_shape=(
            jax.ShapeDtypeStruct(rows, BF16),
            jax.ShapeDtypeStruct((D, HID), F32),
            jax.ShapeDtypeStruct((D, D), F32),
            jax.ShapeDtypeStruct(rows, BF16),
        ),
        in_specs=[full_spec(pltpu.HBM)] + [full_spec(pltpu.SMEM)] * 2 + [full_spec()] * 4,
        out_specs=(full_spec(pltpu.HBM),) * 4,
        scratch_shapes=[
            pltpu.SMEM((PIECES,), jnp.int32),
            pltpu.VMEM((HALF, HID + D), F32),
            pltpu.VMEM(rows, BF16),
            pltpu.VMEM(rows, F32),
            pltpu.VMEM(rows, BF16),
            pltpu.SemaphoreType.DMA((11,)),
        ],
        compiler_params=pltpu.CompilerParams(vmem_limit_bytes=VMEM_SMALL),
        cost_estimate=pl.CostEstimate(
            flops=300_000_000, bytes_accessed=6_000_000, transcendentals=0
        ),
        name="mine_out",
    )(in_hbm(route), offsets, lengths, received, bal, mixed, w_out)


def theirs_kernel(theirs_ref, _, __, w_in_hbm, w_out_hbm, rows_s, sems):
    first = (1 - lax.axis_index("group")) * HALF
    for copy in put_rows(rows_s, first, w_in_hbm, w_out_hbm, sems, theirs_ref):
        copy.wait()


def theirs_out(theirs, w_in_grad, w_out_grad):
    return pl.pallas_call(
        theirs_kernel,
        out_shape=(
            jax.ShapeDtypeStruct((D, HID), F32),
            jax.ShapeDtypeStruct((D, D), F32),
        ),
        in_specs=[full_spec()] + [full_spec(pltpu.HBM)] * 2,
        out_specs=(full_spec(pltpu.HBM),) * 2,
        scratch_shapes=[
            pltpu.VMEM((HALF, HID + D), F32),
            pltpu.SemaphoreType.DMA((8,)),
        ],
        input_output_aliases={1: 0, 2: 1},
        compiler_params=pltpu.CompilerParams(vmem_limit_bytes=VMEM_SMALL),
        cost_estimate=pl.CostEstimate(flops=0, bytes_accessed=2_000_000, transcendentals=0),
        name="theirs_out",
    )(theirs, w_in_grad, w_out_grad)


def body(events, route, block_offset, hist_length, cotangent, w_in, w_out, rab):
    exchange = functools.partial(
        lax.all_to_all, axis_name="member", split_axis=0, concat_axis=0, tiled=True
    )
    swap = functools.partial(lax.ppermute, axis_name="group", perm=[(0, 1), (1, 0)])
    arrived = exchange(pack(route, events))
    other, left, up, gh, bal, mixed = layer(
        block_offset, hist_length, rab, arrived, cotangent, w_in, w_out
    )
    got = swap(other)
    own, back = beside(block_offset, arrived, left, up, gh, bal, w_in)
    received = exchange(join(own, got).reshape(MEMBERS, PIECE, CHUNK))
    received = exchange(total(received, back.reshape(MEMBERS, PIECE, D)))
    theirs = swap(received[:, :, :CHUNK])
    events_grad, w_in_grad, w_out_grad, outputs = mine_out(
        route,
        block_offset,
        hist_length,
        received.reshape(*SHARES[:3], CHUNK + D),
        bal,
        mixed,
        w_out,
    )
    w_in_grad, w_out_grad = theirs_out(theirs.reshape(SHARES), w_in_grad, w_out_grad)
    return outputs, events_grad, w_in_grad, w_out_grad


def solution(mesh):
    placed = (
        P(("group", "member"), None),
        P(("group", "member")),
        P(("group", "member")),
        P(("group", "member")),
        P(("group", "member"), None),
        P(),
        P(),
        P(),
    )
    return jax.shard_map(
        body,
        mesh=mesh,
        in_specs=placed,
        out_specs=(P(("group", "member"), None), P(("group", "member"), None), P(), P()),
        check_vma=False,
    )
```

```python
import functools
import math

import jax
import jax.numpy as jnp
from jax import lax
from jax.experimental import pallas as pl
from jax.experimental.pallas import tpu as pltpu
from jax.sharding import PartitionSpec as P

EPS = 1e-05
BF16 = jnp.bfloat16
F32 = jnp.float32
VMEM_LIMIT = 32 * 1024 * 1024
VMEM_SMALL = 16 * 1024 * 1024

ROWS, D, HID = 512, 512, 2048
BLOCK, BLOCKS, HEADS, BUCKETS = 128, 4, 4, 12
PIECE, PIECES, MEMBERS = 16, 32, 64
SLOT = 72
CHUNK = 640
SCALE = 1.0 / math.sqrt(128)
HALF = D // 2
SHARES = (HALF // PIECE, 4, PIECE, CHUNK)


def dot(a, b):
    return jnp.dot(a, b, preferred_element_type=F32)


def dot_nt(a, b):
    return lax.dot_general(a, b, (((1,), (1,)), ((), ())), preferred_element_type=F32)


def dot_tn(a, b):
    return lax.dot_general(a, b, (((0,), (0,)), ((), ())), preferred_element_type=F32)


def sigmoid(v):
    return 0.5 * jnp.tanh(0.5 * v) + 0.5


def in_hbm(array):
    return pltpu.with_memory_space_constraint(array, pltpu.HBM)


def full_spec(memory=pltpu.VMEM):
    return pl.BlockSpec(memory_space=memory)


def pack_kernel(route_hbm, events_hbm, out_ref, route_s, events_s, sems):
    half = ROWS // 2
    loads = [pltpu.make_async_copy(route_hbm, route_s, sems.at[0])]
    for n in range(2):
        rows = pl.ds(n * half, half)
        loads.append(
            pltpu.make_async_copy(events_hbm.at[rows], events_s.at[rows], sems.at[1 + n])
        )
    for load in loads:
        load.start()
    out_ref[...] = jnp.zeros_like(out_ref)
    for load in loads:
        load.wait()
    for j in range(PIECES):
        target = route_s[j]
        device = lax.shift_right_logical(target, 5)
        place = lax.bitwise_and(target, PIECES - 1)
        for k in range(D // 128):
            out_ref[device, k * PIECE : (k + 1) * PIECE, :] = events_s[
                j * PIECE : (j + 1) * PIECE, k * 128 : (k + 1) * 128
            ]
        label = jnp.full((SLOT - 4 * PIECE, 128), (place + 1).astype(F32), F32)
        out_ref[device, 4 * PIECE :, :] = label.astype(BF16)


def pack(route, events):
    return pl.pallas_call(
        pack_kernel,
        out_shape=jax.ShapeDtypeStruct((MEMBERS, SLOT, 128), BF16),
        in_specs=[full_spec(pltpu.HBM)] * 2,
        out_specs=full_spec(),
        scratch_shapes=[
            pltpu.SMEM((PIECES,), jnp.int32),
            pltpu.VMEM((ROWS, D), BF16),
            pltpu.SemaphoreType.DMA((3,)),
        ],
        compiler_params=pltpu.CompilerParams(vmem_limit_bytes=VMEM_SMALL),
        name="pack_pieces",
    )(in_hbm(route), in_hbm(events))


def cell_goals(arrived_ref):
    labels = arrived_ref[:, 4 * PIECE :, :].astype(F32)
    if labels.shape[1] < PIECE:
        labels = jnp.concatenate([labels, labels], axis=1)
    within = lax.broadcasted_iota(jnp.int32, labels.shape, 1).astype(F32)
    return ((labels - 1.0) * PIECE + within).reshape(MEMBERS * PIECE, 128)


def block_order(offset_ref):
    second = jnp.int32(1)
    for b in range(2, BLOCKS):
        second = jnp.where(offset_ref[b] == 1, b, second)
    return (
        second - 1,
        second,
        jnp.where(second == 1, 2, 0),
        jnp.where(second == 3, 1, 3),
    )


def block_rows(order, i):
    return pl.ds(pl.multiple_of(order[i] * BLOCK, BLOCK), BLOCK)


def inner_goals(goals, order):
    block = jnp.floor(goals * (1.0 / BLOCK))
    moved = goals
    for i in range(BLOCKS):
        at = order[i].astype(F32)
        moved = jnp.where(block == at, goals + (float(i) - at) * BLOCK, moved)
    return moved


def live_column(length_ref, order, i):
    first = BLOCK if i == 1 else 0
    return lax.broadcasted_iota(jnp.int32, (BLOCK, 1), 0) + first < length_ref[order[i]]


def normalized(x):
    centered = x - jnp.mean(x, axis=-1, keepdims=True)
    variance = jnp.mean(centered * centered, axis=-1, keepdims=True)
    rstd = lax.rsqrt(variance + EPS)
    return centered * rstd, rstd


def normalized_back(grad, hat, rstd):
    return rstd * (
        grad
        - jnp.mean(grad, axis=-1, keepdims=True)
        - hat * jnp.mean(grad * hat, axis=-1, keepdims=True)
    )


def head_cols(part, head):
    return slice(part * D + head * 128, part * D + head * 128 + 128)


def layer_kernel(
    offset_ref,
    length_ref,
    rab_ref,
    arrived_ref,
    cot_ref,
    w_in_ref,
    w_out_ref,
    other_ref,
    left_ref,
    up_ref,
    gh_ref,
    bal_ref,
    mixed_ref,
    place_s,
    norm_s,
    hid_s,
    slope_s,
    long_att_s,
    long_ds_s,
    long_slope_s,
    short_att_s,
    short_slope_s,
    ctx_s,
    gm_s,
    gctx_s,
    trans_s,
):
    core = lax.axis_index("group")
    order = block_order(offset_ref)
    long_rows, short_rows = slice(0, 2 * BLOCK), slice(2 * BLOCK, 4 * BLOCK)

    tens = jnp.floor(cell_goals(arrived_ref) * (1.0 / PIECE)).astype(BF16)
    pick = (lax.broadcasted_iota(jnp.int32, (8, 128), 1) == 0).astype(BF16)
    ones = lax.bitwise_and(
        lax.broadcasted_iota(jnp.int32, (1, MEMBERS * PIECE), 1), PIECE - 1
    ).astype(F32)
    goal = inner_goals(dot_nt(pick, tens)[0:1, :] * PIECE + ones, order)

    def gather(rows):
        for r in range(rows.start, rows.stop, BLOCK):
            row = lax.broadcasted_iota(jnp.int32, (BLOCK, 1), 0).astype(F32) + float(r)
            place_s[r : r + BLOCK, :] = jnp.where(goal == row, 1.0, 0.0).astype(BF16)
        for k in range(0, D // 128, 2):
            cells = jnp.concatenate(
                [
                    arrived_ref[:, n * PIECE : (n + 1) * PIECE, :].reshape(MEMBERS * PIECE, 128)
                    for n in (k, k + 1)
                ],
                axis=1,
            )
            bal_ref[rows, k * 128 : k * 128 + 256] = dot(place_s[rows, :], cells).astype(BF16)

    def norm(r):
        sl = slice(r, r + 64)
        norm_s[sl, :] = normalized(bal_ref[sl, :].astype(F32))[0].astype(BF16)

    def project(rows, n):
        cols = slice(n, n + 256)
        v = dot(norm_s[rows, :], w_in_ref[:, cols])
        g = sigmoid(v)
        h = v * g
        hid_s[rows, cols] = h.astype(BF16)
        slope_s[rows, cols] = g + h * (1.0 - g)

    row_id = lax.broadcasted_iota(jnp.int32, (BLOCK, BLOCK), 0)
    col_id = lax.broadcasted_iota(jnp.int32, (BLOCK, BLOCK), 1)
    distance = row_id - col_id
    near_pairs = distance >= 0

    def bias(head, apart, buckets):
        total = jnp.full((BLOCK, BLOCK), rab_ref[head, 0], F32)
        for bucket in range(1, buckets):
            total = jnp.where(apart >= 2 ** (bucket - 1), rab_ref[head, bucket], total)
        return total

    def weigh(scores, relative, allowed):
        s = scores * SCALE + relative
        g = sigmoid(s)
        a = s * g
        return (
            jnp.where(allowed, a, 0.0).astype(BF16),
            jnp.where(allowed, g + a * (1.0 - g), 0.0),
        )

    def live_rows(i):
        return row_id + (BLOCK if i == 1 else 0) < length_ref[order[i]]

    allowed = [near_pairs & live_rows(i) for i in range(BLOCKS)] + [live_rows(1)]
    near = [None] * HEADS
    low, high = slice(0, BLOCK), slice(BLOCK, 2 * BLOCK)
    long_tiles = ((low, low, 0), (high, high, 1), (high, low, BLOCKS))

    def long_attend(head):
        near[head] = bias(head, distance, 8)
        far = bias(head, distance + BLOCK, 9)
        scores = dot_nt(hid_s[long_rows, head_cols(2, head)], hid_s[long_rows, head_cols(3, head)])
        long_att_s[head, low, high] = jnp.zeros((BLOCK, BLOCK), BF16)
        long_ds_s[head, low, high] = jnp.zeros((BLOCK, BLOCK), BF16)
        for tile, (i, j, pairs) in enumerate(long_tiles):
            a, slope = weigh(scores[i, j], far if tile == 2 else near[head], allowed[pairs])
            long_att_s[head, i, j] = a
            long_slope_s[head, tile] = slope
        ctx_s[long_rows, head_cols(0, head)] = dot(
            long_att_s[head], hid_s[long_rows, head_cols(1, head)]
        )

    def short_attend(head):
        for i in (2, 3):
            rows = slice(i * BLOCK, (i + 1) * BLOCK)
            scores = dot_nt(hid_s[rows, head_cols(2, head)], hid_s[rows, head_cols(3, head)])
            a, slope = weigh(scores, near[head], allowed[i])
            short_att_s[head, i - 2] = a
            short_slope_s[head, i - 2] = slope
            ctx_s[rows, head_cols(0, head)] = dot(a, hid_s[rows, head_cols(1, head)])

    def upstream(i):
        kept = jnp.where(
            live_column(length_ref, order, i), cot_ref[block_rows(order, i), :].astype(F32), 0.0
        )
        up_ref[i * BLOCK : (i + 1) * BLOCK, :] = kept.astype(BF16)

    def middle(r):
        sl = slice(r, r + 64)
        n, rstd = normalized(ctx_s[sl, :])
        u = hid_s[sl, 0:D].astype(F32)
        mixed_ref[sl, :] = (n * u).astype(BF16)
        gm = gm_s[sl, :]
        gh_ref[sl, 0:D] = (gm * n * slope_s[sl, 0:D]).astype(BF16)
        gctx_s[sl, :] = normalized_back(gm * u, n, rstd).astype(BF16)

    def finish_grads(rows, head, gv, gq, gk):
        for part, grad in ((1, gv), (2, gq * SCALE), (3, gk * SCALE)):
            cols = head_cols(part, head)
            gh_ref[rows, cols] = (grad * slope_s[rows, cols]).astype(BF16)

    def long_back(head):
        gc = gctx_s[long_rows, head_cols(0, head)]
        grads = dot_nt(gc, hid_s[long_rows, head_cols(1, head)])
        for tile, (i, j, _) in enumerate(long_tiles):
            long_ds_s[head, i, j] = (grads[i, j] * long_slope_s[head, tile]).astype(BF16)
        ds = long_ds_s[head]
        finish_grads(
            long_rows,
            head,
            dot_tn(long_att_s[head], gc),
            dot(ds, hid_s[long_rows, head_cols(3, head)]),
            dot_tn(ds, hid_s[long_rows, head_cols(2, head)]),
        )

    def short_back(head):
        for i in (2, 3):
            rows = slice(i * BLOCK, (i + 1) * BLOCK)
            gc = gctx_s[rows, head_cols(0, head)]
            grads = dot_nt(gc, hid_s[rows, head_cols(1, head)])
            ds = (grads * short_slope_s[head, i - 2]).astype(BF16)
            finish_grads(
                rows,
                head,
                dot_tn(short_att_s[head, i - 2], gc),
                dot(ds, hid_s[rows, head_cols(3, head)]),
                dot_tn(ds, hid_s[rows, head_cols(2, head)]),
            )

    parts = (1024, 1536, 1280, 1792, 512, 768, 0, 256)
    gather(long_rows)
    gather(short_rows)
    for r in range(0, 256, 64):
        norm(r)
    for k, n in enumerate(parts):
        project(long_rows, n)
        if k < 4:
            norm(256 + 64 * k)
    for i in range(BLOCKS):
        upstream(i)
    gm_s[...] = dot_nt(up_ref[...], w_out_ref[...])
    for k, n in enumerate(parts):
        if k % 2 == 0:
            long_attend(k // 2)
        project(short_rows, n)
    for head in range(HEADS):
        middle(64 * head)
        short_attend(head)
    trans_s[0] = norm_s[...].T
    for head in range(HEADS):
        long_back(head)
        middle(256 + 64 * head)
    trans_s[1] = mixed_ref[...].T
    for head in range(HEADS):
        short_back(head)

    own_rows = pl.ds(pl.multiple_of(core * HALF, HALF), HALF)
    other_rows = pl.ds(pl.multiple_of((1 - core) * HALF, HALF), HALF)
    left_ref[0] = trans_s[0, own_rows, :]
    left_ref[1] = trans_s[1, own_rows, :]

    def store(at, value):
        other_ref[at] = value.astype(BF16)

    weight_grads(trans_s[0, other_rows, :], trans_s[1, other_rows, :], gh_ref, up_ref, store)


def weight_grads(normed_t, mixed_t, gh_ref, up_ref, store):
    for at in range(0, HID + D, D):
        if at < HID:
            value = dot(normed_t, gh_ref[:, at : at + D])
        else:
            value = dot(mixed_t, up_ref[...])
        for n in range(0, D, 128):
            side, start = (at + n) // CHUNK, (at + n) % CHUNK
            shares = value[:, n : n + 128].reshape(HALF // PIECE, PIECE, 128)
            store((slice(None), side, slice(None), slice(start, start + 128)), shares)


def beside_kernel(
    offset_ref,
    arrived_ref,
    left_ref,
    up_ref,
    gh_ref,
    bal_ref,
    w_in_ref,
    own_ref,
    back_ref,
    gx_s,
    gb_s,
    place_s,
):
    gx_s[...] = dot_nt(gh_ref[...], w_in_ref[...])

    def store(at, value):
        own_ref[at] = value.astype(BF16)

    weight_grads(left_ref[0], left_ref[1], gh_ref, up_ref, store)
    for r in range(0, ROWS, 64):
        sl = slice(r, r + 64)
        hat, rstd = normalized(bal_ref[sl, :].astype(F32))
        grad = normalized_back(gx_s[sl, :], hat, rstd)
        gb_s[sl, :] = (up_ref[sl, :].astype(F32) + grad).astype(BF16)
    goals = inner_goals(cell_goals(arrived_ref), block_order(offset_ref))
    for b in range(BLOCKS):
        row = lax.broadcasted_iota(jnp.int32, (1, BLOCK), 1).astype(F32) + float(b * BLOCK)
        place_s[:, b * BLOCK : (b + 1) * BLOCK] = jnp.where(goals == row, 1.0, 0.0).astype(BF16)
    for n in range(0, D, 256):
        back_ref[:, n : n + 256] = dot(place_s[...], gb_s[:, n : n + 256]).astype(BF16)


def beside(offsets, arrived, left, up, gh, bal, w_in):
    return pl.pallas_call(
        beside_kernel,
        out_shape=(
            jax.ShapeDtypeStruct(SHARES, BF16),
            jax.ShapeDtypeStruct((MEMBERS * PIECE, D), BF16),
        ),
        in_specs=[full_spec(pltpu.SMEM)] + [full_spec()] * 6,
        out_specs=(full_spec(),) * 2,
        scratch_shapes=[
            pltpu.VMEM((ROWS, D), F32),
            pltpu.VMEM((ROWS, D), BF16),
            pltpu.VMEM((MEMBERS * PIECE, ROWS), BF16),
        ],
        compiler_params=pltpu.CompilerParams(vmem_limit_bytes=VMEM_SMALL),
        cost_estimate=pl.CostEstimate(
            flops=3_000_000_000, bytes_accessed=2_000_000, transcendentals=1_000
        ),
        name="beside",
    )(offsets, arrived, left, up, gh, bal, w_in)


def join_kernel(own_ref, got_ref, out_ref):
    out_ref[...] = (own_ref[...].astype(F32) + got_ref[...].astype(F32)).astype(BF16)


def join(own, got):
    return pl.pallas_call(
        join_kernel,
        out_shape=jax.ShapeDtypeStruct(SHARES, BF16),
        in_specs=[full_spec()] * 2,
        out_specs=full_spec(),
        compiler_params=pltpu.CompilerParams(vmem_limit_bytes=VMEM_SMALL),
        cost_estimate=pl.CostEstimate(flops=1_000_000, bytes_accessed=4_000_000, transcendentals=0),
        name="join",
    )(own, got)


def layer(offsets, lengths, rab, arrived, cotangent, w_in, w_out):
    scratch = [
        ((ROWS, MEMBERS * PIECE), BF16),
        ((ROWS, D), BF16),
        ((ROWS, HID), BF16),
        ((ROWS, HID), F32),
        ((HEADS, 2 * BLOCK, 2 * BLOCK), BF16),
        ((HEADS, 2 * BLOCK, 2 * BLOCK), BF16),
        ((HEADS, 3, BLOCK, BLOCK), F32),
        ((HEADS, 2, BLOCK, BLOCK), BF16),
        ((HEADS, 2, BLOCK, BLOCK), F32),
        ((ROWS, D), F32),
        ((ROWS, D), F32),
        ((ROWS, D), BF16),
        ((2, D, ROWS), BF16),
    ]
    rows = jax.ShapeDtypeStruct((ROWS, D), BF16)
    return pl.pallas_call(
        layer_kernel,
        out_shape=(
            jax.ShapeDtypeStruct(SHARES, BF16),
            jax.ShapeDtypeStruct((2, HALF, ROWS), BF16),
            rows,
            jax.ShapeDtypeStruct((ROWS, HID), BF16),
            rows,
            rows,
        ),
        in_specs=[full_spec(pltpu.SMEM)] * 3 + [full_spec()] * 4,
        out_specs=(full_spec(),) * 6,
        scratch_shapes=[pltpu.VMEM(shape, kind) for shape, kind in scratch],
        compiler_params=pltpu.CompilerParams(vmem_limit_bytes=VMEM_LIMIT),
        cost_estimate=pl.CostEstimate(
            flops=4_000_000_000, bytes_accessed=9_000_000, transcendentals=1_500_000
        ),
        name="layer",
    )(offsets, lengths, rab, arrived, cotangent, w_in, w_out)


def total_kernel(received_ref, back_ref, out_ref):
    total = received_ref[0].astype(F32)
    for m in range(1, MEMBERS):
        total += received_ref[m].astype(F32)
    total = (total * (1.0 / 256.0)).astype(BF16)
    out_ref[:, :, :CHUNK] = jnp.broadcast_to(total[None], (MEMBERS, PIECE, CHUNK))
    out_ref[:, :, CHUNK:] = back_ref[...]


def total(received, back):
    return pl.pallas_call(
        total_kernel,
        out_shape=jax.ShapeDtypeStruct((MEMBERS, PIECE, CHUNK + D), BF16),
        in_specs=[full_spec()] * 2,
        out_specs=full_spec(),
        compiler_params=pltpu.CompilerParams(vmem_limit_bytes=VMEM_SMALL),
        cost_estimate=pl.CostEstimate(flops=1_000_000, bytes_accessed=4_000_000, transcendentals=0),
        name="total",
    )(received, back)


def put_shares(source, rows_s, groups):
    for side in range(4):
        at = side * CHUNK
        for g in groups:
            value = source[g, side, :, :CHUNK].astype(F32)
            rows_s[g * PIECE : (g + 1) * PIECE, at : at + CHUNK] = value


def put_rows(rows_s, first, w_in_hbm, w_out_hbm, sems, source):
    copies = []
    height = 64
    parts = rows_s.shape[0] // height
    for part in range(parts):
        put_shares(source, rows_s, range(part * height // PIECE, (part + 1) * height // PIECE))
        here = slice(part * height, (part + 1) * height)
        there = pl.ds(pl.multiple_of(first + part * height, height), height)
        for n, copy in enumerate(
            (
                (rows_s.at[here, :HID], w_in_hbm.at[there]),
                (rows_s.at[here, HID:], w_out_hbm.at[there]),
            )
        ):
            copies.append(pltpu.make_async_copy(*copy, sems.at[2 * part + n]))
            copies[-1].start()
    return copies


def mine_kernel(
    route_hbm,
    offset_ref,
    length_ref,
    received_ref,
    bal_ref,
    mixed_ref,
    w_out_ref,
    events_hbm,
    w_in_grad_hbm,
    w_out_grad_hbm,
    out_hbm,
    route_s,
    rows_s,
    events_s,
    product_s,
    out_s,
    sems,
):
    load = pltpu.make_async_copy(route_hbm, route_s, sems.at[9])
    load.start()
    product_s[...] = dot(mixed_ref[...], w_out_ref[...])
    order = block_order(offset_ref)
    for i in range(BLOCKS):
        rows = slice(i * BLOCK, (i + 1) * BLOCK)
        value = bal_ref[rows, :].astype(F32) + product_s[rows, :]
        value = jnp.where(live_column(length_ref, order, i), value, 0.0)
        out_s[block_rows(order, i), :] = value.astype(BF16)
    copies = [pltpu.make_async_copy(out_s, out_hbm, sems.at[10])]
    copies[0].start()
    copies += put_rows(
        rows_s, lax.axis_index("group") * HALF, w_in_grad_hbm, w_out_grad_hbm, sems, received_ref
    )
    load.wait()
    for j in range(PIECES):
        slot = lax.shift_right_logical(route_s[j], 5)
        piece = received_ref[lax.shift_right_logical(slot, 2), lax.bitwise_and(slot, 3)]
        events_s[j * PIECE : (j + 1) * PIECE, :] = piece[:, CHUNK:]
    copies.append(pltpu.make_async_copy(events_s, events_hbm, sems.at[8]))
    copies[-1].start()
    for copy in copies:
        copy.wait()


def mine_out(route, offsets, lengths, received, bal, mixed, w_out):
    rows = (ROWS, D)
    return pl.pallas_call(
        mine_kernel,
        out_shape=(
            jax.ShapeDtypeStruct(rows, BF16),
            jax.ShapeDtypeStruct((D, HID), F32),
            jax.ShapeDtypeStruct((D, D), F32),
            jax.ShapeDtypeStruct(rows, BF16),
        ),
        in_specs=[full_spec(pltpu.HBM)] + [full_spec(pltpu.SMEM)] * 2 + [full_spec()] * 4,
        out_specs=(full_spec(pltpu.HBM),) * 4,
        scratch_shapes=[
            pltpu.SMEM((PIECES,), jnp.int32),
            pltpu.VMEM((HALF, HID + D), F32),
            pltpu.VMEM(rows, BF16),
            pltpu.VMEM(rows, F32),
            pltpu.VMEM(rows, BF16),
            pltpu.SemaphoreType.DMA((11,)),
        ],
        compiler_params=pltpu.CompilerParams(vmem_limit_bytes=VMEM_SMALL),
        cost_estimate=pl.CostEstimate(
            flops=300_000_000, bytes_accessed=6_000_000, transcendentals=0
        ),
        name="mine_out",
    )(in_hbm(route), offsets, lengths, received, bal, mixed, w_out)


def theirs_kernel(theirs_ref, _, __, w_in_hbm, w_out_hbm, rows_s, sems):
    first = (1 - lax.axis_index("group")) * HALF
    for copy in put_rows(rows_s, first, w_in_hbm, w_out_hbm, sems, theirs_ref):
        copy.wait()


def theirs_out(theirs, w_in_grad, w_out_grad):
    return pl.pallas_call(
        theirs_kernel,
        out_shape=(
            jax.ShapeDtypeStruct((D, HID), F32),
            jax.ShapeDtypeStruct((D, D), F32),
        ),
        in_specs=[full_spec()] + [full_spec(pltpu.HBM)] * 2,
        out_specs=(full_spec(pltpu.HBM),) * 2,
        scratch_shapes=[
            pltpu.VMEM((HALF, HID + D), F32),
            pltpu.SemaphoreType.DMA((8,)),
        ],
        input_output_aliases={1: 0, 2: 1},
        compiler_params=pltpu.CompilerParams(vmem_limit_bytes=VMEM_SMALL),
        cost_estimate=pl.CostEstimate(flops=0, bytes_accessed=2_000_000, transcendentals=0),
        name="theirs_out",
    )(theirs, w_in_grad, w_out_grad)


def body(events, route, block_offset, hist_length, cotangent, w_in, w_out, rab):
    exchange = functools.partial(
        lax.all_to_all, axis_name="member", split_axis=0, concat_axis=0, tiled=True
    )
    swap = functools.partial(lax.ppermute, axis_name="group", perm=[(0, 1), (1, 0)])
    arrived = exchange(pack(route, events))
    other, left, up, gh, bal, mixed = layer(
        block_offset, hist_length, rab, arrived, cotangent, w_in, w_out
    )
    got = swap(other)
    own, back = beside(block_offset, arrived, left, up, gh, bal, w_in)
    received = exchange(join(own, got).reshape(MEMBERS, PIECE, CHUNK))
    received = exchange(total(received, back.reshape(MEMBERS, PIECE, D)))
    theirs = swap(received[:, :, :CHUNK])
    events_grad, w_in_grad, w_out_grad, outputs = mine_out(
        route,
        block_offset,
        hist_length,
        received.reshape(*SHARES[:3], CHUNK + D),
        bal,
        mixed,
        w_out,
    )
    w_in_grad, w_out_grad = theirs_out(theirs.reshape(SHARES), w_in_grad, w_out_grad)
    return outputs, events_grad, w_in_grad, w_out_grad


def solution(mesh):
    placed = (
        P(("group", "member"), None),
        P(("group", "member")),
        P(("group", "member")),
        P(("group", "member")),
        P(("group", "member"), None),
        P(),
        P(),
        P(),
    )
    return jax.shard_map(
        body,
        mesh=mesh,
        in_specs=placed,
        out_specs=(P(("group", "member"), None), P(("group", "member"), None), P(), P()),
        check_vma=False,
    )
```
